256 devices in a mesh: ctx: 64 (over x, z, core), head: 4 (over y).
Axes of the slice: x: 4, y: 4, z: 8, core: 2. Of those that a mesh axis runs over, the one named last changes fastest.
Arguments:
- queries: bfloat16 [8192, 4096], P('ctx', 'head'), may hold values from -140 to 140
- keys: bfloat16 [8192, 4096], P('ctx', 'head'), may hold values from -5 to 5
- values: bfloat16 [8192, 4096], P('ctx', 'head'), may hold values from -22 to 22
- init_state: float32 [32, 128, 128], P('head'), may hold values from -48 to 48
- lin_gain: float32 [4096], P('head'), may hold values from 0.25 to 1.75
- rate_table: float32 [16], replicated, may hold values from 0 to 0.04
- rate_index: int32 [32], P('head'), may hold values from 0 to 15
- speed: float32 [8192, 32], P('ctx', 'head'), may hold values from 0.45 to 2
- drop: float32 [8192, 32], P('ctx', 'head'), may hold values from 0 to 1.4
- doc_id: int32 [8192], P('ctx'), may hold values from 0 to 3, as said below
Outputs:
- mixed: bfloat16 [8192, 4096], P('ctx', 'head')
The draws below stay inside these ranges and needn't reach their ends.
Inputs may be any that keep to these rules, and one draw needn't show every extreme that they name: `doc_id`: never falling from token to token, every document present; each document has at most 4096 tokens, and one has exactly that many; document 0 continues the document of the carried state.
All inputs are finite; a program needn't handle non-finite values.
Results may differ from the reference program's by a relative error of at most 0.0095.
Values may be sent and summed in bfloat16 or wider, within the bound.
No kernel may reach another device: no remote copies, remote signals or barrier semaphores. Data moves between devices by JAX's collectives and lax.ppermute only.
A program may use at most 192 MiB of HBM per device.

```python
import math
import jax
import jax.numpy as jnp
from jax import lax

HEAD_TOTAL = 32
DH = 128
TOK_DEV = 128
WINDOW = 4096
NRATE = 16
CONTEXT_TOKENS = 8192


def draw_queries(key, part):
    key = jax.random.fold_in(key, 11)
    result = jnp.clip(jax.random.normal(key, (CONTEXT_TOKENS, HEAD_TOTAL * DH), jnp.float32), -5.0, 5.0)
    return result.astype(jnp.bfloat16)


def draw_keys(key, part):
    key = jax.random.fold_in(key, 12)
    result = jnp.clip(jax.random.normal(key, (CONTEXT_TOKENS, HEAD_TOTAL * DH), jnp.float32), -5.0, 5.0)
    return result.astype(jnp.bfloat16)


def draw_values(key, part):
    key = jax.random.fold_in(key, 13)
    first_key, second_key = jax.random.split(key, 2)
    columns = jnp.arange(HEAD_TOTAL * DH).astype(jnp.float32)
    jitter = jax.random.uniform(first_key, (HEAD_TOTAL * DH,), jnp.float32, -0.35, 0.35)
    column_scale = jnp.exp(math.log(0.3) + math.log(10.0) * columns / (HEAD_TOTAL * DH - 1) + jitter)
    normal_part = jnp.clip(jax.random.normal(second_key, (CONTEXT_TOKENS, HEAD_TOTAL * DH), jnp.float32), -5.0, 5.0)
    result = column_scale[None, :] * normal_part
    return result.astype(jnp.bfloat16)


def draw_rate_table(key, part):
    key = jax.random.fold_in(key, 14)
    first_key, second_key, third_key = jax.random.split(key, 3)
    fast_share = 0.5
    is_fast = jax.random.uniform(first_key, (NRATE,), jnp.float32) < fast_share
    fast_rate = jnp.exp(jax.random.uniform(second_key, (NRATE,), jnp.float32, math.log(1.0 / 50.0), math.log(1.0 / 30.0)))
    slow_rate = jax.random.uniform(third_key, (NRATE,), jnp.float32, 0.05, 0.25) / CONTEXT_TOKENS
    return jnp.where(is_fast, fast_rate, slow_rate)


def draw_speed(key, part):
    key = jax.random.fold_in(key, 15)
    device_key, token_key = jax.random.split(key, 2)
    device_factor = jnp.exp(jax.random.uniform(device_key, (CONTEXT_TOKENS // TOK_DEV, HEAD_TOTAL), jnp.float32, math.log(0.7), math.log(1.4)))
    repeated = jnp.repeat(device_factor, TOK_DEV, axis=0)
    token_factor = jnp.exp(jax.random.uniform(token_key, (CONTEXT_TOKENS, HEAD_TOTAL), jnp.float32, math.log(0.7), math.log(1.4)))
    return repeated * token_factor


def draw_drop(key, part):
    key = jax.random.fold_in(key, 16)
    position_random_key, depth_random_key = jax.random.split(key, 2)
    cluster_rows = jax.random.randint(position_random_key, (3, HEAD_TOTAL), 0, CONTEXT_TOKENS)
    cluster_depth = jax.random.uniform(depth_random_key, (3, HEAD_TOTAL), jnp.float32, math.log(1.25), math.log(2.0))
    match_flags = jnp.arange(CONTEXT_TOKENS)[:, None, None] == cluster_rows[None]
    return jnp.sum(jnp.where(match_flags, cluster_depth[None], 0.0), axis=1)


def draw_doc_id(key, part):
    key = jax.random.fold_in(key, 17)
    start_key, split_key = jax.random.split(key, 2)
    half_length = CONTEXT_TOKENS // 2
    first_start = jax.random.randint(start_key, (), CONTEXT_TOKENS // 8, CONTEXT_TOKENS // 4 + 1)
    last_start = jax.random.randint(split_key, (), first_start + half_length + 1, CONTEXT_TOKENS)
    places = jnp.arange(CONTEXT_TOKENS, dtype=jnp.int32)
    result = (places >= first_start).astype(jnp.int32) + (places >= first_start + half_length).astype(jnp.int32)
    result = result + (places >= last_start).astype(jnp.int32)
    return result


def touch_ends(entries, rng, low, high):
    dims = entries.shape
    index_at = [jax.random.randint(jax.random.fold_in(rng, axis), (), 0, dims[axis]) for axis in range(len(dims))]
    entries = entries.at[tuple(index_at)].set(low)
    longest = dims.index(max(dims))
    index_at[longest] = (index_at[longest] + 1) % dims[longest]
    return entries.at[tuple(index_at)].set(high)


def level_of(key, shape, cuts, low, top_value):
    gain, own = 1.0, jax.random.fold_in(key, 6)
    for dim, parts in cuts:
        steps = jnp.exp(jax.random.uniform(jax.random.fold_in(own, dim), (parts,), jnp.float32, low / len(cuts), top_value / len(cuts)))
        gain = gain * jnp.repeat(steps, shape[dim] // parts).reshape([-1 if axis == dim else 1 for axis in range(len(shape))])
    return gain


def normal_values(key, shape, scale, most, cuts=(), kind=jnp.bfloat16):
    drawn = scale * jax.random.normal(key, shape, jnp.float32)
    if cuts:
        drawn = drawn * level_of(key, shape, cuts, -0.22, 0.18)
    return jnp.clip(drawn, -most, most).astype(kind)


def setup_inputs(seed: int = 0) -> dict:
    splits = jax.random.split(jax.random.key(seed), 11)
    queries = draw_queries(jax.random.fold_in(splits[10], 71), 0)
    keys = draw_keys(jax.random.fold_in(splits[10], 71), 0)
    values = draw_values(jax.random.fold_in(splits[10], 71), 0)
    init_state = normal_values(splits[3], (HEAD_TOTAL, DH, DH), 8.0, 48.0, ((0, 4),), jnp.float32)
    lin_gain = jnp.clip(1.0 + 0.15 * jax.random.normal(splits[4], (HEAD_TOTAL * DH,), jnp.float32), 0.25, 1.75)
    rate_table = draw_rate_table(jax.random.fold_in(splits[10], 71), 0)
    rate_index = touch_ends(jax.random.randint(splits[6], (HEAD_TOTAL,), 0, NRATE), jax.random.fold_in(splits[6], 1), 0, NRATE - 1).astype(jnp.int32)
    speed = draw_speed(jax.random.fold_in(splits[10], 71), 0)
    drop = draw_drop(jax.random.fold_in(splits[10], 71), 0)
    doc_id = draw_doc_id(jax.random.fold_in(splits[10], 71), 0)
    return dict(queries=queries, keys=keys, values=values, init_state=init_state, lin_gain=lin_gain, rate_table=rate_table, rate_index=rate_index, speed=speed, drop=drop, doc_id=doc_id)


def linear_block(query_part, key_part, value_part, cumulative, doc_part, score_scale):
    places = jnp.arange(query_part.shape[0])
    inside = (places[:, None] >= places[None, :]) & (doc_part[:, None] == doc_part[None, :])
    spread = cumulative.T[:, :, None] - cumulative.T[:, None, :]
    fading = jnp.exp(jnp.where(inside[None], spread, 0.0))
    affinity = jnp.einsum('thd,shd->hts', query_part.astype(jnp.float32), key_part.astype(jnp.float32))
    weights = jnp.where(inside[None], fading * affinity * score_scale, 0.0).astype(jnp.bfloat16)
    weights = lax.optimization_barrier(weights).astype(jnp.float32)
    within = jnp.einsum('hts,shd->thd', weights, value_part.astype(jnp.float32))
    overall = cumulative[-1]
    keeping = doc_part == doc_part[-1]
    factor = jnp.where(keeping[:, None], jnp.exp(overall[None, :] - cumulative), 0.0)
    scaled = (key_part.astype(jnp.float32) * factor[:, :, None]).astype(jnp.bfloat16)
    scaled = lax.optimization_barrier(scaled).astype(jnp.float32)
    summary = jnp.einsum('shd,she->hde', scaled, value_part.astype(jnp.float32))
    return (within, overall, summary)

def carried_term(query_part, cumulative, doc_part, carry_doc, entering, score_scale):
    projected = jnp.einsum('thd,hde->the', query_part.astype(jnp.float32), entering, precision=lax.Precision.HIGHEST)
    live = (doc_part == carry_doc)[:, None, None]
    return jnp.where(live, jnp.exp(cumulative)[:, :, None] * projected * score_scale, 0.0)

def reference(queries, keys, values, init_state, lin_gain, rate_table, rate_index, speed, drop, doc_id):
    score_scale = 1.0 / math.sqrt(DH)
    blocks = CONTEXT_TOKENS // TOK_DEV
    picked = rate_index[:, None] == jnp.arange(NRATE, dtype=jnp.int32)[None, :]
    head_rate = lax.optimization_barrier(jnp.sum(jnp.where(picked, rate_table[None, :], 0.0), axis=1))
    log_decay = -head_rate[None, :] * speed - drop
    doc_float = doc_id.astype(jnp.float32)

    def advance(carry, pieces):
        entering, carry_doc = carry
        query_part, key_part, value_part, decay_part, doc_part = pieces
        cumulative = jnp.cumsum(decay_part, axis=0)
        within, overall, summary = linear_block(query_part, key_part, value_part, cumulative, doc_part, score_scale)
        outside = carried_term(query_part, cumulative, doc_part, carry_doc, entering, score_scale)
        linked = jnp.where(doc_part[-1] == carry_doc, 1.0, 0.0)
        following = summary + jnp.exp(overall)[:, None, None] * entering * linked
        return ((following, doc_part[-1]), within + outside)
    initial = (init_state, jnp.zeros((), jnp.float32))
    pieces = (queries.reshape(blocks, TOK_DEV, HEAD_TOTAL, DH), keys.reshape(blocks, TOK_DEV, HEAD_TOTAL, DH), values.reshape(blocks, TOK_DEV, HEAD_TOTAL, DH), log_decay.reshape(blocks, TOK_DEV, HEAD_TOTAL), doc_float.reshape(blocks, TOK_DEV))
    final_carry, linear_out = lax.scan(advance, initial, pieces)
    linear_out = linear_out.reshape(CONTEXT_TOKENS, HEAD_TOTAL, DH)
    square_mean = lax.optimization_barrier(jnp.mean(linear_out * linear_out, axis=(1, 2)))
    inverse_rms = 1.0 / jnp.sqrt(square_mean + 1e-06)
    key_pad = jnp.concatenate([jnp.zeros((WINDOW, HEAD_TOTAL * DH), jnp.bfloat16), keys], axis=0)
    value_pad = jnp.concatenate([jnp.zeros((WINDOW, HEAD_TOTAL * DH), jnp.bfloat16), values], axis=0)
    doc_pad = jnp.concatenate([jnp.full((WINDOW,), -1, jnp.int32), doc_id.astype(jnp.int32)], axis=0)

    def window_block(block_index):
        begin = (block_index * TOK_DEV).astype(jnp.int32)
        query_part = lax.dynamic_slice_in_dim(queries, begin, TOK_DEV, 0).reshape(TOK_DEV, HEAD_TOTAL, DH).astype(jnp.float32)
        key_part = lax.dynamic_slice_in_dim(key_pad, begin, WINDOW + TOK_DEV, 0).reshape(WINDOW + TOK_DEV, HEAD_TOTAL, DH).astype(jnp.float32)
        value_part = lax.dynamic_slice_in_dim(value_pad, begin, WINDOW + TOK_DEV, 0).reshape(WINDOW + TOK_DEV, HEAD_TOTAL, DH).astype(jnp.float32)
        doc_keys = lax.dynamic_slice_in_dim(doc_pad, begin, WINDOW + TOK_DEV, 0)
        doc_query = lax.dynamic_slice_in_dim(doc_id.astype(jnp.int32), begin, TOK_DEV, 0)
        query_place = begin + jnp.arange(TOK_DEV, dtype=jnp.int32)
        key_place = begin - WINDOW + jnp.arange(WINDOW + TOK_DEV, dtype=jnp.int32)
        allowed = (key_place[None, :] <= query_place[:, None]) & (key_place[None, :] > query_place[:, None] - WINDOW)
        allowed = allowed & (key_place[None, :] >= 0) & (doc_keys[None, :] == doc_query[:, None])
        scores = jnp.einsum('thd,shd->hts', query_part, key_part) * score_scale
        scores = jnp.where(allowed[None], scores, -1e+30)
        top_score = lax.optimization_barrier(jnp.max(scores, axis=2, keepdims=True))
        weights = jnp.exp(scores - top_score)
        weight_sum = lax.optimization_barrier(jnp.sum(weights, axis=2))
        rounded = lax.optimization_barrier(weights.astype(jnp.bfloat16)).astype(jnp.float32)
        output_sum = jnp.einsum('hts,shd->thd', rounded, value_part)
        return output_sum / weight_sum.T[:, :, None]
    window_out = lax.map(window_block, jnp.arange(blocks, dtype=jnp.int32)).reshape(CONTEXT_TOKENS, HEAD_TOTAL, DH)
    gain_heads = lin_gain.reshape(HEAD_TOTAL, DH)
    mixed = gain_heads[None] * linear_out * inverse_rms[:, None, None] + window_out
    return mixed.astype(jnp.bfloat16).reshape(CONTEXT_TOKENS, HEAD_TOTAL * DH)
```

```python
import math

import jax
import jax.numpy as jnp
from jax import lax
from jax.experimental import pallas as pl
from jax.experimental.pallas import tpu as pltpu
from jax.sharding import Mesh
from jax.sharding import PartitionSpec as P

HEAD_TOTAL = 32
DH = 128
TOK = 128
WINDOW = 4096
HEADS = 8
META = 16
KV_ROWS = 2 * DH + META
ROWS = KV_ROWS + TOK
PLANE = 2 * HEADS * TOK
SCALE = 1.0 / math.sqrt(DH)
EXP2_SCALE = SCALE / math.log(2.0)
LOW = -1e30
F32 = jnp.float32
BF16 = jnp.bfloat16
CHUNK = 2 * TOK


def dot(a, b):
    return jnp.dot(a, b, preferred_element_type=F32)


def split3(x):
    high = x.astype(BF16)
    rest = x - high.astype(F32)
    mid = rest.astype(BF16)
    low = (rest - mid.astype(F32)).astype(BF16)
    return high, mid, low


def joined(rows, at):
    part = rows.astype(F32)
    return part[at : at + 1] + part[at + 1 : at + 2] + part[at + 2 : at + 3]


def column(row):
    return jnp.transpose(jnp.broadcast_to(row, (TOK, TOK)))


def split_dot(a, state):
    high = state.astype(BF16)
    low = (state - high.astype(F32)).astype(BF16)
    return dot(a, high) + dot(a, low)


def prepare_kernel(table_ref, index_ref, q_ref, k_ref, v_ref, speed_ref, drop_ref, doc_ref, out_ref):
    lane = lax.broadcasted_iota(jnp.int32, (1, HEADS), 1)
    rate = jnp.zeros((1, HEADS), F32)
    for h in range(HEADS):
        rate = jnp.where(lane == h, table_ref[index_ref[h]], rate)
    log_decay = -rate * speed_ref[...] - drop_ref[...]
    upto = (
        lax.broadcasted_iota(jnp.int32, (TOK, TOK), 0)
        <= lax.broadcasted_iota(jnp.int32, (TOK, TOK), 1)
    ).astype(F32)
    cum = lax.dot_general(
        log_decay,
        upto,
        (((0,), (0,)), ((), ())),
        precision=lax.Precision.HIGHEST,
        preferred_element_type=F32,
    )
    high, mid, low = split3(cum)
    row = lax.broadcasted_iota(jnp.int32, (META, TOK), 0)
    doc = jnp.broadcast_to(doc_ref[...].astype(F32), (META, TOK))
    for h in range(HEADS):
        cols = pl.ds(h * DH, DH)
        out_ref[h, 0:DH, :] = jnp.transpose(k_ref[:, cols])
        out_ref[h, DH : 2 * DH, :] = v_ref[:, cols]
        meta = jnp.where(row == 3, doc, 0.0)
        for n, part in enumerate((high, mid, low)):
            meta = jnp.where(row == n, jnp.broadcast_to(part[h : h + 1].astype(F32), (META, TOK)), meta)
        out_ref[h, 2 * DH : KV_ROWS, :] = meta.astype(BF16)
        out_ref[h, KV_ROWS:ROWS, :] = q_ref[:, cols]


def linear_kernel(info_ref, own_ref, other_ref, init_ref, partial_ref, weight_ref, state_ref):
    x, core = info_ref[0], info_ref[2]
    first = core == 0
    state = jnp.where(x == 0, init_ref[0], 0.0)
    carry = jnp.where(x == 0, jnp.zeros((1, TOK), F32), jnp.full((1, TOK), -1.0, F32))
    prefix = jnp.zeros((1, TOK), F32)
    places = lax.broadcasted_iota(jnp.int32, (TOK, TOK), 0)
    causal = places >= lax.broadcasted_iota(jnp.int32, (TOK, TOK), 1)

    def read(swap, i):
        mine, theirs = own_ref[i, 0:KV_ROWS, :], other_ref[i]
        got = jnp.where(swap, theirs, mine)
        rows = got[2 * DH :]
        cum = joined(rows, 0)
        doc = rows.astype(F32)[3:4]
        overall = jnp.broadcast_to(cum[:, TOK - 1 :], (1, TOK))
        last = jnp.broadcast_to(doc[:, TOK - 1 :], (1, TOK))
        return got[:DH], got[DH : 2 * DH], cum, doc, overall, last

    def advance(state, carry, prefix, block):
        keys, values, cum, doc, overall, last = block
        factor = jnp.where(doc == last, jnp.exp(overall - cum), 0.0)
        scaled = (keys.astype(F32) * factor).astype(BF16)
        keep = jnp.where(last == carry, jnp.exp(overall), 0.0)
        return dot(scaled, values) + keep * state, last, prefix + overall

    for i in range(HEADS):
        even = read(jnp.logical_not(first), i)
        odd = read(first, i)
        middle = advance(state, carry, prefix, even)
        at_state = jnp.where(first, state, middle[0])
        at_carry = jnp.where(first, carry, middle[1])
        at_prefix = jnp.where(first, prefix, middle[2])
        keys, values, cum, doc, _, _ = [jnp.where(first, a, b) for a, b in zip(even, odd)]
        queries = own_ref[i, KV_ROWS:ROWS, :]
        cum_col, doc_col = column(cum), column(doc)
        inside = causal & (doc_col == doc)
        fading = jnp.exp(jnp.where(inside, cum_col - cum, 0.0))
        weights = jnp.where(inside, fading * dot(queries, keys) * SCALE, 0.0).astype(BF16)
        grown = jnp.exp(cum_col) * SCALE
        outside = jnp.where(doc_col == at_carry, grown * split_dot(queries, at_state), 0.0)
        partial_ref[i] = dot(weights, values) + outside
        weight_ref[i] = jnp.exp(cum_col + at_prefix) * SCALE
        state, carry, prefix = advance(*middle, odd)
    state_ref[0:DH, :] = state
    row = lax.broadcasted_iota(jnp.int32, (8, TOK), 0)
    state_ref[DH : DH + 8, :] = jnp.where(row == 0, prefix, carry)


def enter_kernel(info_ref, own_ref, partial_ref, weight_ref, near_ref, far_ref, linear_ref, square_ref):
    x = info_ref[0]
    near_decay, near_doc = near_ref[DH : DH + 1, :], near_ref[DH + 1 : DH + 2, :]
    far_doc = far_ref[DH + 1 : DH + 2, :]
    keep = jnp.where((far_doc == near_doc) & (x >= 2), jnp.exp(near_decay), 0.0)
    state = near_ref[0:DH, :] + keep * far_ref[0:DH, :]
    ones = jnp.ones((8, DH), F32)
    for i in range(HEADS):
        doc_col = column(own_ref[i, 2 * DH : KV_ROWS, :].astype(F32)[3:4])
        live = (doc_col == near_doc) & (x >= 1)
        product = split_dot(own_ref[i, KV_ROWS:ROWS, :], state)
        linear = partial_ref[i] + jnp.where(live, weight_ref[i] * product, 0.0)
        linear_ref[i] = linear.astype(BF16)
        square = lax.dot_general(
            ones,
            linear * linear,
            (((1,), (1,)), ((), ())),
            precision=lax.Precision.HIGHEST,
            preferred_element_type=F32,
        )
        square_ref[i : i + 1, :] = square[0:1]


def doc_rows(ref, i):
    return ref[i, 2 * DH : 2 * DH + META, :].astype(F32)[3:4]


def below(refs, number):
    total = jnp.zeros((1, TOK), F32)
    for ref in refs:
        for i in range(HEADS):
            total = total + jnp.where(doc_rows(ref, i) < number, 1.0, 0.0)
    return jnp.sum(total)


def first_places(doc_col, counts):
    place = jnp.zeros(doc_col.shape, F32)
    for number, count in counts:
        place = jnp.where(doc_col == number, count, place)
    return place


def soft_part(queries, score_ref, read, begin, end, mask):
    rows = queries.shape[0]

    def fill(n, top):
        keys, _ = read(n)
        scores = mask(dot(queries, keys), n)
        score_ref[n] = scores
        return jnp.maximum(top, jnp.maximum(scores[:, :TOK], scores[:, TOK:]))

    top = lax.fori_loop(begin, end, fill, jnp.full((rows, TOK), LOW, F32))
    top = jnp.max(top, axis=1, keepdims=True)

    def add(n, carry):
        total, output = carry
        _, values = read(n)
        weights = jnp.exp2((score_ref[n] - top) * EXP2_SCALE)
        total = total + weights[:, :TOK] + weights[:, TOK:]
        return total, output + dot(weights.astype(BF16), values)

    zero = jnp.zeros((rows, TOK), F32)
    total, output = lax.fori_loop(begin, end, add, (zero, zero))
    return top, jnp.sum(total, axis=1, keepdims=True), output


def both(a_ref, b_ref, n):
    keys = jnp.concatenate([a_ref[n, 0:DH, :], b_ref[n, 0:DH, :]], axis=1)
    values = jnp.concatenate([a_ref[n, DH : 2 * DH, :], b_ref[n, DH : 2 * DH, :]], axis=0)
    return keys, values


def key_place(core, rows):
    lane = lax.broadcasted_iota(jnp.int32, (rows, CHUNK), 1)
    own = lane + core * TOK
    return jnp.where(lane < TOK, own, lane - core * TOK)


def own_window_kernel(info_ref, own_ref, other_ref, top_ref, total_ref, output_ref, score_ref):
    core = info_ref[2]
    counts = [(float(d), below((own_ref, other_ref), float(d))) for d in range(4)]
    rows = 2 * TOK
    places = key_place(core, rows)
    row = lax.broadcasted_iota(jnp.int32, (rows, 1), 0)
    for tile in range(HEADS // 2):
        i = 2 * tile
        doc_col = jnp.concatenate([column(doc_rows(own_ref, i)), column(doc_rows(own_ref, i + 1))], axis=0)
        low = first_places(doc_col, counts).astype(jnp.int32)[:, :1]
        queries = jnp.concatenate([own_ref[i, KV_ROWS:ROWS, :], own_ref[i + 1, KV_ROWS:ROWS, :]], axis=0)
        at = (i + row // TOK) * CHUNK + core * TOK + row % TOK
        low = jnp.maximum(low, at - (WINDOW - 1))

        def mask(scores, n):
            key = places + n * CHUNK
            return jnp.where((key >= low) & (key <= at), scores, LOW)

        begin = jnp.min(low) // CHUNK
        top, total, output = soft_part(
            queries, score_ref, lambda n: both(own_ref, other_ref, n), begin, i + 2, mask
        )
        top_ref[pl.ds(tile * rows, rows), :] = jnp.broadcast_to(top, (rows, TOK))
        total_ref[pl.ds(tile * rows, rows), :] = jnp.broadcast_to(total, (rows, TOK))
        output_ref[pl.ds(tile * rows, rows), :] = output


def past_window_kernel(
    info_ref, own_ref, near_ref, near_other_ref, far_ref, far_other_ref, top_ref, total_ref,
    output_ref, linear_ref, square_ref, out_ref, near_score_ref, far_score_ref,
):
    x, core = info_ref[0], info_ref[2]
    rows = 2 * TOK
    whole = float(PLANE)
    counts = []
    for d in range(4):
        far = jnp.where(x >= 2, below((far_ref, far_other_ref), float(d)), whole)
        near = jnp.where(x >= 1, below((near_ref, near_other_ref), float(d)), whole)
        counts.append((float(d), far + near))
    places = key_place(core, rows)
    row = lax.broadcasted_iota(jnp.int32, (rows, 1), 0)
    meta_row = lax.broadcasted_iota(jnp.int32, (META, TOK), 0)
    for tile in range(HEADS // 2):
        i = 2 * tile
        doc_col = jnp.concatenate([column(doc_rows(own_ref, i)), column(doc_rows(own_ref, i + 1))], axis=0)
        low = first_places(doc_col, counts).astype(jnp.int32)[:, :1]
        queries = jnp.concatenate([own_ref[i, KV_ROWS:ROWS, :], own_ref[i + 1, KV_ROWS:ROWS, :]], axis=0)
        at = (i + row // TOK) * CHUNK + core * TOK + row % TOK + 2 * PLANE
        low = jnp.maximum(low, at - (WINDOW - 1))
        start = jnp.min(low)

        def mask_far(scores, n):
            return jnp.where(places + n * CHUNK >= low, scores, LOW)

        def mask_near(scores, n):
            return jnp.where(places + (n * CHUNK + PLANE) >= low, scores, LOW)

        far_begin = jnp.clip(start // CHUNK, 0, HEADS)
        near_begin = jnp.clip((start - PLANE) // CHUNK, 0, HEADS)
        span = pl.ds(tile * rows, rows)
        parts = [(top_ref[span, :1], total_ref[span, :1], output_ref[span, :])]
        parts.append(
            soft_part(queries, near_score_ref, lambda n: both(near_ref, near_other_ref, n), near_begin, HEADS, mask_near)
        )
        parts.append(
            soft_part(queries, far_score_ref, lambda n: both(far_ref, far_other_ref, n), far_begin, HEADS, mask_far)
        )
        top = jnp.maximum(parts[0][0], jnp.maximum(parts[1][0], parts[2][0]))
        total = jnp.zeros((rows, 1), F32)
        output = jnp.zeros((rows, DH), F32)
        for part_top, part_total, part_output in parts:
            shrink = jnp.exp2((part_top - top) * EXP2_SCALE)
            total = total + part_total * shrink
            output = output + part_output * shrink
        result = (output / total).astype(BF16)
        out_ref[i, 0:TOK, :] = result[:TOK]
        out_ref[i + 1, 0:TOK, :] = result[TOK:]
    for i in range(HEADS):
        out_ref[i, TOK : 2 * TOK, :] = linear_ref[i]
        meta = jnp.zeros((META, TOK), F32)
        for n, part in enumerate(split3(square_ref[i : i + 1, :])):
            meta = jnp.where(meta_row == n, jnp.broadcast_to(part.astype(F32), (META, TOK)), meta)
        out_ref[i, 2 * TOK :, :] = meta.astype(BF16)


def finish_kernel(got_ref, gain_ref, out_ref):
    total = jnp.zeros((1, TOK), F32)
    for h in range(HEADS):
        total = total + joined(got_ref[h, 2 * TOK :, :], 0)
    inverse = column(lax.rsqrt(total / (HEAD_TOTAL * DH) + 1e-06))
    for h in range(HEADS):
        cols = pl.ds(h * DH, DH)
        linear = got_ref[h, TOK : 2 * TOK, :].astype(F32)
        window = got_ref[h, 0:TOK, :].astype(F32)
        out_ref[:, cols] = (gain_ref[:, cols] * linear * inverse + window).astype(BF16)


VMEM = pl.BlockSpec(memory_space=pltpu.VMEM)
SMEM = pl.BlockSpec(memory_space=pltpu.SMEM)


def call(kernel, name, specs, shapes, scratch=(), flops=0, moved=0):
    many = isinstance(shapes, (list, tuple))
    return pl.pallas_call(
        kernel,
        name=name,
        out_shape=shapes,
        in_specs=specs,
        out_specs=[VMEM] * len(shapes) if many else VMEM,
        scratch_shapes=list(scratch),
        compiler_params=pltpu.CompilerParams(vmem_limit_bytes=40 * 2**20),
        cost_estimate=pl.CostEstimate(flops=flops, bytes_accessed=moved, transcendentals=0),
    )


def body(queries, keys, values, init_state, lin_gain, rate_table, rate_index, speed, drop, doc_id):
    x, z, core = (lax.axis_index(a).astype(jnp.int32) for a in ("x", "z", "core"))
    info = jnp.stack([x, z, core])
    shape = jax.ShapeDtypeStruct
    packed = call(
        prepare_kernel, "prepare", [SMEM, SMEM] + [VMEM] * 6, shape((HEADS, ROWS, TOK), BF16), moved=2 << 20
    )(rate_table, rate_index, queries, keys, values, speed, drop, doc_id[None, :])
    own = lax.all_to_all(packed, "z", 0, 0, tiled=True)
    sent = own[:, :KV_ROWS]
    pair = [(0, 1), (1, 0)]
    other = lax.ppermute(sent, "core", pair)
    near = lax.ppermute(sent, "x", [(0, 1), (1, 2), (2, 3)])
    far = lax.ppermute(sent, "x", [(0, 2), (1, 3)])

    tokens = HEADS * TOK
    init = lax.dynamic_slice_in_dim(init_state, z, 1, 0)
    partial, weight, state = call(
        linear_kernel,
        "linear",
        [SMEM] + [VMEM] * 3,
        [shape((HEADS, TOK, DH), F32), shape((HEADS, TOK, DH), F32), shape((DH + 8, DH), F32)],
        moved=4 << 20,
    )(info, own, other, init)
    near_state = lax.ppermute(state, "x", [(0, 1), (1, 2), (2, 3)])
    far_state = lax.ppermute(state, "x", [(0, 2), (1, 3)])
    own_top, own_total, own_output = call(
        own_window_kernel,
        "own_window",
        [SMEM] + [VMEM] * 2,
        [shape((tokens, TOK), F32), shape((tokens, TOK), F32), shape((tokens, DH), F32)],
        scratch=[pltpu.VMEM((HEADS, 2 * TOK, CHUNK), F32)],
        moved=6 << 20,
    )(info, own, other)
    linear, square = call(
        enter_kernel,
        "enter",
        [SMEM] + [VMEM] * 5,
        [shape((HEADS, TOK, DH), BF16), shape((HEADS, TOK), F32)],
        moved=3 << 20,
    )(info, own, partial, weight, near_state, far_state)
    square = square + lax.ppermute(square, "head", [(i, i ^ 1) for i in range(4)])
    square = square + lax.ppermute(square, "head", [(i, i ^ 2) for i in range(4)])
    near_other = lax.ppermute(near, "core", pair)
    far_other = lax.ppermute(far, "core", pair)
    mixed = call(
        past_window_kernel,
        "past_window",
        [SMEM] + [VMEM] * 10,
        shape((HEADS, 2 * TOK + META, DH), BF16),
        scratch=[pltpu.VMEM((HEADS, 2 * TOK, CHUNK), F32)] * 2,
        moved=12 << 20,
    )(info, own, near, near_other, far, far_other, own_top, own_total, own_output, linear, square)
    back = lax.all_to_all(mixed, "z", 0, 0, tiled=True)
    return call(finish_kernel, "finish", [VMEM] * 2, shape((TOK, HEADS * DH), BF16), moved=1 << 20)(
        back, lin_gain[None, :]
    )


def solution(mesh):
    split = Mesh(mesh.devices.reshape(4, 8, 2, 4), ("x", "z", "core", "head"))
    ctx = ("x", "z", "core")
    placed = (
        P(ctx, "head"),
        P(ctx, "head"),
        P(ctx, "head"),
        P("head", None, None),
        P("head"),
        P(),
        P("head"),
        P(ctx, "head"),
        P(ctx, "head"),
        P(ctx),
    )
    return jax.shard_map(body, mesh=split, in_specs=placed, out_specs=P(ctx, "head"), check_vma=False)
```

```python
import math

import jax
import jax.numpy as jnp
from jax import lax
from jax.experimental import pallas as pl
from jax.experimental.pallas import tpu as pltpu
from jax.sharding import Mesh
from jax.sharding import PartitionSpec as P

HEAD_TOTAL = 32
DH = 128
TOK = 128
WINDOW = 4096
HEADS = 8
META = 16
KV_ROWS = 2 * DH + META
ROWS = KV_ROWS + TOK
PLANE = 2 * HEADS * TOK
SCALE = 1.0 / math.sqrt(DH)
EXP2_SCALE = SCALE / math.log(2.0)
LOW = -1e30
F32 = jnp.float32
BF16 = jnp.bfloat16
CHUNK = 2 * TOK
TILES = HEADS // 2
META_AT = DH
VALUE_AT = DH + META


def dot(a, b):
    return jnp.dot(a, b, preferred_element_type=F32)


def split3(x):
    high = x.astype(BF16)
    rest = x - high.astype(F32)
    mid = rest.astype(BF16)
    low = (rest - mid.astype(F32)).astype(BF16)
    return high, mid, low


def joined(rows, at):
    part = rows.astype(F32)
    return part[at : at + 1] + part[at + 1 : at + 2] + part[at + 2 : at + 3]


def column(row):
    return jnp.transpose(jnp.broadcast_to(row, (TOK, TOK)))


def split_dot(a, state):
    high = state.astype(BF16)
    low = (state - high.astype(F32)).astype(BF16)
    return dot(a, high) + dot(a, low)


def prepare_kernel(
    table_ref, index_ref, q_hbm, k_hbm, v_hbm, speed_ref, drop_ref, doc_ref, out_ref, q_ref, k_ref, v_ref, sems
):
    copies = [
        pltpu.make_async_copy(src, dst, sems.at[n])
        for n, (src, dst) in enumerate(((k_hbm, k_ref), (v_hbm, v_ref), (q_hbm, q_ref)))
    ]
    for copy in copies:
        copy.start()
    head = lax.broadcasted_iota(jnp.int32, (HEADS, TOK), 0)
    rate = jnp.zeros((HEADS, TOK), F32)
    for h in range(HEADS):
        rate = jnp.where(head == h, table_ref[index_ref[h]], rate)
    log_decay = -rate * speed_ref[...] - drop_ref[...]
    upto = (
        lax.broadcasted_iota(jnp.int32, (TOK, TOK), 0)
        <= lax.broadcasted_iota(jnp.int32, (TOK, TOK), 1)
    ).astype(F32)
    cum = jnp.dot(log_decay, upto, precision=lax.Precision.HIGHEST, preferred_element_type=F32)
    parts = [part.astype(F32) for part in split3(cum)]
    row = lax.broadcasted_iota(jnp.int32, (META, TOK), 0)
    doc = jnp.broadcast_to(doc_ref[...].astype(F32), (META, TOK))
    bias = jnp.where(doc == (row - 4).astype(F32), 0.0, LOW)
    shared = jnp.where(row == 3, doc, jnp.where((row >= 4) & (row < 8), bias, 0.0))
    for h in range(HEADS):
        meta = shared
        for n, part in enumerate(parts):
            meta = jnp.where(row == n, jnp.broadcast_to(part[h : h + 1], (META, TOK)), meta)
        out_ref[h, META_AT:VALUE_AT, :] = meta.astype(BF16)
    copies[0].wait()
    for h in range(HEADS):
        out_ref[h, 0:DH, :] = jnp.transpose(k_ref[:, pl.ds(h * DH, DH)])
    copies[1].wait()
    copies[2].wait()
    for h in range(HEADS):
        cols = pl.ds(h * DH, DH)
        out_ref[h, VALUE_AT:KV_ROWS, :] = v_ref[:, cols]
        out_ref[h, KV_ROWS:ROWS, :] = q_ref[:, cols]


def meta_rows(ref, i):
    return ref[i, META_AT:VALUE_AT, :].astype(F32)


def linear_kernel(info_ref, own_ref, other_ref, init_ref, partial_ref, weight_ref, state_ref, mark_ref):
    x, core = info_ref[0], info_ref[2]
    first = core == 0
    state = jnp.where(x == 0, init_ref[0], 0.0)
    carry = jnp.where(x == 0, jnp.zeros((1, TOK), F32), jnp.full((1, TOK), -1.0, F32))
    prefix = jnp.zeros((1, TOK), F32)
    places = lax.broadcasted_iota(jnp.int32, (TOK, TOK), 0)
    lanes = lax.broadcasted_iota(jnp.int32, (TOK, TOK), 1)
    causal = places >= lanes
    marked = (lanes >= 4) & (lanes < 8)
    number = (lanes - 4).astype(F32)
    start_doc = None

    def read(swap, i):
        mine, theirs = own_ref[i, 0:KV_ROWS, :], other_ref[i]
        got = jnp.where(swap, theirs, mine)
        rows = got[META_AT:VALUE_AT].astype(F32)
        cum, doc = rows[0:1] + rows[1:2] + rows[2:3], rows[3:4]
        overall = jnp.broadcast_to(cum[:, TOK - 1 :], (1, TOK))
        last = jnp.broadcast_to(doc[:, TOK - 1 :], (1, TOK))
        return got[:DH], got[VALUE_AT:], cum, doc, overall, last

    def advance(state, carry, prefix, block):
        keys, values, cum, doc, overall, last = block
        factor = jnp.where(doc == last, jnp.exp(overall - cum), 0.0)
        scaled = (keys.astype(F32) * factor).astype(BF16)
        keep = jnp.where(last == carry, jnp.exp(overall), 0.0)
        return dot(scaled, values) + keep * state, last, prefix + overall

    for i in range(HEADS):
        even = read(jnp.logical_not(first), i)
        odd = read(first, i)
        if start_doc is None:
            start_doc = jnp.broadcast_to(even[3][:, :1], (1, TOK))
        middle = advance(state, carry, prefix, even)
        at_state = jnp.where(first, state, middle[0])
        at_carry = jnp.where(first, carry, middle[1])
        at_prefix = jnp.where(first, prefix, middle[2])
        keys, values, cum, doc, _, _ = [jnp.where(first, a, b) for a, b in zip(even, odd)]
        queries = own_ref[i, KV_ROWS:ROWS, :]
        cum_col, doc_col = column(cum), column(doc)
        inside = causal & (doc_col == doc)
        fading = jnp.exp(jnp.where(inside, cum_col - cum, 0.0))
        weights = jnp.where(inside, fading * dot(queries, keys) * SCALE, 0.0).astype(BF16)
        grown = jnp.exp(cum_col) * SCALE
        outside = jnp.where(doc_col == at_carry, grown * split_dot(queries, at_state), 0.0)
        partial_ref[i] = dot(weights, values) + outside
        weight_ref[i] = jnp.where(doc_col == start_doc, jnp.exp(cum_col + at_prefix) * SCALE, 0.0)
        mark_ref[i] = jnp.where(marked & (doc_col == number), 1.0, 0.0).astype(BF16)
        state, carry, prefix = advance(*middle, odd)
    state_ref[0:DH, :] = state
    row = lax.broadcasted_iota(jnp.int32, (8, TOK), 0)
    state_ref[DH : DH + 8, :] = jnp.where(row == 0, prefix, jnp.where(row == 1, carry, start_doc))


def enter_kernel(
    info_ref, own_ref, partial_ref, weight_ref, state_ref, near_ref, far_ref, linear_ref, square_ref, need_ref
):
    x = info_ref[0]
    near_decay, near_doc = near_ref[DH : DH + 1, :], near_ref[DH + 1 : DH + 2, :]
    far_doc, start_doc = far_ref[DH + 1 : DH + 2, :], state_ref[DH + 2 : DH + 3, :]
    keep = jnp.where((far_doc == near_doc) & (x >= 2), jnp.exp(near_decay), 0.0)
    state = near_ref[0:DH, :] + keep * far_ref[0:DH, :]
    state = jnp.where((start_doc == near_doc) & (x >= 1), state, 0.0)
    ones = jnp.ones((8, DH), F32)
    for i in range(HEADS):
        linear = partial_ref[i] + weight_ref[i] * split_dot(own_ref[i, KV_ROWS:ROWS, :], state)
        linear_ref[i] = linear.astype(BF16)
        square = lax.dot_general(
            ones,
            linear * linear,
            (((1,), (1,)), ((), ())),
            precision=lax.Precision.HIGHEST,
            preferred_element_type=F32,
        )
        square_ref[i : i + 1, :] = square[0:1]
    for tile in range(TILES):
        tile_doc = jnp.broadcast_to(meta_rows(own_ref, 2 * tile)[3:4, :1], (1, TOK))
        need_ref[2 * tile] = jnp.where(x >= 1, jnp.max(jnp.where(tile_doc == near_doc, 1, 0)), 0)
        need_ref[2 * tile + 1] = jnp.where(x >= 2, jnp.max(jnp.where(tile_doc == far_doc, 1, 0)), 0)


def marked_queries(own_ref, mark_ref, tile):
    i = 2 * tile
    queries = jnp.concatenate([own_ref[i, KV_ROWS:ROWS, :], own_ref[i + 1, KV_ROWS:ROWS, :]], axis=0)
    marks = jnp.concatenate([mark_ref[i], mark_ref[i + 1]], axis=0)[:, :META]
    return jnp.concatenate([queries, marks], axis=1)


def absorb(queries, ref, pieces, diagonal, old):
    scores = []
    top = None
    for m in pieces:
        keys = jnp.concatenate([ref[2 * m, 0:VALUE_AT, :], ref[2 * m + 1, 0:VALUE_AT, :]], axis=1)
        score = dot(queries, keys)
        if m == diagonal[0]:
            score = jnp.where(diagonal[1], score, LOW)
        scores.append(score)
        most = jnp.maximum(score[:, :TOK], score[:, TOK:])
        top = most if top is None else jnp.maximum(top, most)
    top = jnp.max(top, axis=1, keepdims=True)
    if old is not None:
        top = jnp.maximum(top, old[0])
    base = top * EXP2_SCALE
    sums, output = None, None
    for m, score in zip(pieces, scores):
        weights = jnp.exp2(score * EXP2_SCALE - base)
        part = weights[:, :TOK] + weights[:, TOK:]
        sums = part if sums is None else sums + part
        values = jnp.concatenate([ref[2 * m, VALUE_AT:KV_ROWS, :], ref[2 * m + 1, VALUE_AT:KV_ROWS, :]], axis=0)
        product = dot(weights.astype(BF16), values)
        output = product if output is None else output + product
    total = jnp.sum(sums, axis=1, keepdims=True)
    if old is not None:
        shrink = jnp.exp2(old[0] * EXP2_SCALE - base)
        total = total + old[1] * shrink
        output = output + old[2] * shrink
    return top, total, output


def tile_places(core, own):
    rows = lax.broadcasted_iota(jnp.int32, (CHUNK, CHUNK), 0)
    lanes = lax.broadcasted_iota(jnp.int32, (CHUNK, CHUNK), 1)
    key_core = core if own else 1 - core
    at = jnp.where(rows < TOK, rows, rows + TOK) + core * TOK
    key = jnp.where(lanes < TOK, lanes, lanes + TOK) + key_core * TOK
    return at, key


def span_of(tile):
    return pl.ds(tile * CHUNK, CHUNK)


def load_part(refs, tile):
    top_ref, total_ref, output_ref = refs
    span = span_of(tile)
    return top_ref[span, :1], total_ref[span, :1], output_ref[span, :]


def store_part(refs, tile, part):
    span = span_of(tile)
    for ref, value in zip(refs, part):
        ref[span, :] = jnp.broadcast_to(value, (CHUNK, TOK))


def own_window_kernel(info_ref, own_ref, other_ref, mark_ref, *refs):
    core = info_ref[2]
    masks = []
    for own in (True, False):
        at, key = tile_places(core, own)
        masks.append(key <= at)
    for tile in range(TILES):
        queries = marked_queries(own_ref, mark_ref, tile)
        part = absorb(queries, own_ref, range(tile + 1), (tile, masks[0]), None)
        part = absorb(queries, other_ref, range(tile + 1), (tile, masks[1]), part)
        store_part(refs, tile, part)


def past_blocks(core, own, own_ref, mark_ref, need_ref, near_ref, far_ref, refs):
    at, key = tile_places(core, own)
    mask = key > at
    for tile in range(TILES):

        @pl.when(need_ref[2 * tile] == 1)
        def _(tile=tile):
            queries = marked_queries(own_ref, mark_ref, tile)
            store_part(refs, tile, absorb(queries, near_ref, range(TILES), (None, None), load_part(refs, tile)))

        @pl.when(need_ref[2 * tile + 1] == 1)
        def _(tile=tile):
            queries = marked_queries(own_ref, mark_ref, tile)
            store_part(refs, tile, absorb(queries, far_ref, range(tile, TILES), (tile, mask), load_part(refs, tile)))


def past_own_kernel(info_ref, need_ref, own_ref, mark_ref, near_ref, far_ref, a_ref, b_ref, c_ref, *refs):
    for before, after in zip((a_ref, b_ref, c_ref), refs):
        after[...] = before[...]
    past_blocks(info_ref[2], True, own_ref, mark_ref, need_ref, near_ref, far_ref, refs)


def past_other_kernel(
    info_ref, need_ref, own_ref, mark_ref, near_ref, far_ref, a_ref, b_ref, c_ref, linear_ref, square_ref, out_ref, *refs
):
    for before, after in zip((a_ref, b_ref, c_ref), refs):
        after[...] = before[...]
    row = lax.broadcasted_iota(jnp.int32, (META, TOK), 0)
    for i in range(HEADS):
        out_ref[i, TOK : 2 * TOK, :] = linear_ref[i]
        meta = jnp.zeros((META, TOK), F32)
        for n, part in enumerate(split3(square_ref[i : i + 1, :])):
            meta = jnp.where(row == n, jnp.broadcast_to(part.astype(F32), (META, TOK)), meta)
        out_ref[i, 2 * TOK :, :] = meta.astype(BF16)
    past_blocks(info_ref[2], False, own_ref, mark_ref, need_ref, near_ref, far_ref, refs)
    _, total_ref, output_ref = refs
    for i in range(HEADS):
        span = pl.ds(i * TOK, TOK)
        out_ref[i, 0:TOK, :] = (output_ref[span, :] / total_ref[span, :]).astype(BF16)


def finish_kernel(got_ref, gain_ref, out_ref):
    total = jnp.zeros((1, TOK), F32)
    for h in range(HEADS):
        total = total + joined(got_ref[h, 2 * TOK :, :], 0)
    inverse = column(lax.rsqrt(total / (HEAD_TOTAL * DH) + 1e-06))
    for h in range(HEADS):
        cols = pl.ds(h * DH, DH)
        linear = got_ref[h, TOK : 2 * TOK, :].astype(F32)
        window = got_ref[h, 0:TOK, :].astype(F32)
        out_ref[:, cols] = (gain_ref[:, cols] * linear * inverse + window).astype(BF16)


VMEM = pl.BlockSpec(memory_space=pltpu.VMEM)
SMEM = pl.BlockSpec(memory_space=pltpu.SMEM)
HBM = pl.BlockSpec(memory_space=pltpu.HBM)


def call(kernel, name, specs, shapes, scratch=(), flops=0, moved=0, outs=None):
    many = isinstance(shapes, (list, tuple))
    return pl.pallas_call(
        kernel,
        name=name,
        out_shape=shapes,
        in_specs=specs,
        out_specs=outs or ([VMEM] * len(shapes) if many else VMEM),
        scratch_shapes=list(scratch),
        compiler_params=pltpu.CompilerParams(vmem_limit_bytes=32 * 2**20),
        cost_estimate=pl.CostEstimate(flops=flops, bytes_accessed=moved, transcendentals=0),
    )


def body(queries, keys, values, init_state, lin_gain, rate_table, rate_index, speed, drop, doc_id):
    x, z, core = (lax.axis_index(a).astype(jnp.int32) for a in ("x", "z", "core"))
    info = jnp.stack([x, z, core])
    shape = jax.ShapeDtypeStruct
    packed = call(
        prepare_kernel,
        "prepare",
        [SMEM, SMEM, HBM, HBM, HBM, VMEM, VMEM, VMEM],
        shape((HEADS, ROWS, TOK), BF16),
        scratch=[pltpu.VMEM((TOK, HEADS * DH), BF16)] * 3 + [pltpu.SemaphoreType.DMA((3,))],
        moved=2 << 20,
    )(rate_table, rate_index, queries, keys, values, speed.T, drop.T, doc_id[None, :])
    own = lax.all_to_all(packed, "z", 0, 0, tiled=True)
    sent = own[:, :KV_ROWS]
    pair = [(0, 1), (1, 0)]
    near = lax.ppermute(sent, "x", [(0, 1), (1, 2), (2, 3)])
    far = lax.ppermute(sent, "x", [(0, 2), (1, 3)])
    other = lax.ppermute(sent, "core", pair)

    tokens = HEADS * TOK
    part_shapes = [shape((tokens, TOK), F32), shape((tokens, TOK), F32), shape((tokens, DH), F32)]
    init = lax.dynamic_slice_in_dim(init_state, z, 1, 0)
    partial, weight, state, mark = call(
        linear_kernel,
        "linear",
        [SMEM] + [VMEM] * 3,
        [
            shape((HEADS, TOK, DH), F32),
            shape((HEADS, TOK, DH), F32),
            shape((DH + 8, DH), F32),
            shape((HEADS, TOK, TOK), BF16),
        ],
        flops=2_000_000_000,
        moved=4 << 20,
    )(info, own, other, init)
    near_state = lax.ppermute(state, "x", [(0, 1), (1, 2), (2, 3)])
    far_state = lax.ppermute(state, "x", [(0, 2), (1, 3)])
    own_part = call(
        own_window_kernel, "own_window", [SMEM] + [VMEM] * 3, part_shapes, flops=5_000_000_000, moved=6 << 20
    )(info, own, other, mark)
    linear, square, need = call(
        enter_kernel,
        "enter",
        [SMEM] + [VMEM] * 6,
        [shape((HEADS, TOK, DH), BF16), shape((HEADS, TOK), F32), shape((2 * TILES,), jnp.int32)],
        outs=[VMEM, VMEM, SMEM],
        flops=1_000_000_000,
        moved=3 << 20,
    )(info, own, partial, weight, state, near_state, far_state)
    square = square + lax.ppermute(square, "head", [(i, i ^ 1) for i in range(4)])
    square = square + lax.ppermute(square, "head", [(i, i ^ 2) for i in range(4)])
    near, far, square, own_part = lax.optimization_barrier((near, far, square, own_part))
    near_other = lax.ppermute(near, "core", pair)
    far_other = lax.ppermute(far, "core", pair)
    own_part = call(
        past_own_kernel,
        "past_own",
        [SMEM] * 2 + [VMEM] * 7,
        part_shapes,
        flops=4_000_000_000,
        moved=8 << 20,
    )(info, need, own, mark, near, far, *own_part)
    mixed = call(
        past_other_kernel,
        "past_other",
        [SMEM] * 2 + [VMEM] * 9,
        shape((HEADS, 2 * TOK + META, DH), BF16),
        scratch=[pltpu.VMEM((tokens, TOK), F32)] * 3,
        flops=4_000_000_000,
        moved=8 << 20,
    )(info, need, own, mark, near_other, far_other, *own_part, linear, square)
    back = lax.all_to_all(mixed, "z", 0, 0, tiled=True)
    return call(finish_kernel, "finish", [VMEM] * 2, shape((TOK, HEADS * DH), BF16), moved=1 << 20)(
        back, lin_gain[None, :]
    )


def solution(mesh):
    split = Mesh(mesh.devices.reshape(4, 8, 2, 4), ("x", "z", "core", "head"))
    ctx = ("x", "z", "core")
    placed = (
        P(ctx, "head"),
        P(ctx, "head"),
        P(ctx, "head"),
        P("head", None, None),
        P("head"),
        P(),
        P("head"),
        P(ctx, "head"),
        P(ctx, "head"),
        P(ctx),
    )
    return jax.shard_map(body, mesh=split, in_specs=placed, out_specs=P(ctx, "head"), check_vma=False)
```

```python
import math

import jax
import jax.numpy as jnp
from jax import lax
from jax.experimental import pallas as pl
from jax.experimental.pallas import tpu as pltpu
from jax.sharding import Mesh
from jax.sharding import PartitionSpec as P

HEAD_TOTAL = 32
DH = 128
TOK = 128
WINDOW = 4096
HEADS = 8
META = 16
KV_ROWS = 2 * DH + META
ROWS = KV_ROWS + TOK
PLANE = 2 * HEADS * TOK
SCALE = 1.0 / math.sqrt(DH)
EXP2_SCALE = SCALE / math.log(2.0)
LOW = -1e30
F32 = jnp.float32
BF16 = jnp.bfloat16
CHUNK = 2 * TOK
TILES = HEADS // 2
META_AT = DH
VALUE_AT = DH + META


def dot(a, b):
    return jnp.dot(a, b, preferred_element_type=F32)


def split3(x):
    high = x.astype(BF16)
    rest = x - high.astype(F32)
    mid = rest.astype(BF16)
    low = (rest - mid.astype(F32)).astype(BF16)
    return high, mid, low


def joined(rows, at):
    part = rows.astype(F32)
    return part[at : at + 1] + part[at + 1 : at + 2] + part[at + 2 : at + 3]


def column(row):
    return jnp.transpose(jnp.broadcast_to(row, (TOK, TOK)))


def split_dot(a, state):
    high = state.astype(BF16)
    low = (state - high.astype(F32)).astype(BF16)
    return dot(a, high) + dot(a, low)


def prepare_kernel(
    table_ref, index_ref, q_hbm, k_hbm, v_hbm, speed_ref, drop_ref, doc_ref, out_ref, q_ref, k_ref, v_ref, sems
):
    copies = [
        pltpu.make_async_copy(src, dst, sems.at[n])
        for n, (src, dst) in enumerate(((k_hbm, k_ref), (v_hbm, v_ref), (q_hbm, q_ref)))
    ]
    for copy in copies:
        copy.start()
    head = lax.broadcasted_iota(jnp.int32, (HEADS, TOK), 0)
    rate = jnp.zeros((HEADS, TOK), F32)
    for h in range(HEADS):
        rate = jnp.where(head == h, table_ref[index_ref[h]], rate)
    log_decay = -rate * speed_ref[...] - drop_ref[...]
    upto = (
        lax.broadcasted_iota(jnp.int32, (TOK, TOK), 0)
        <= lax.broadcasted_iota(jnp.int32, (TOK, TOK), 1)
    ).astype(F32)
    cum = jnp.dot(log_decay, upto, precision=lax.Precision.HIGHEST, preferred_element_type=F32)
    parts = [part.astype(F32) for part in split3(cum)]
    row = lax.broadcasted_iota(jnp.int32, (META, TOK), 0)
    doc = jnp.broadcast_to(doc_ref[...].astype(F32), (META, TOK))
    bias = jnp.where(doc == (row - 4).astype(F32), 0.0, LOW)
    shared = jnp.where(row == 3, doc, jnp.where((row >= 4) & (row < 8), bias, 0.0))
    for h in range(HEADS):
        meta = shared
        for n, part in enumerate(parts):
            meta = jnp.where(row == n, jnp.broadcast_to(part[h : h + 1], (META, TOK)), meta)
        out_ref[h, META_AT:VALUE_AT, :] = meta.astype(BF16)
    copies[0].wait()
    for h in range(HEADS):
        out_ref[h, 0:DH, :] = jnp.transpose(k_ref[:, pl.ds(h * DH, DH)])
    copies[1].wait()
    copies[2].wait()
    for h in range(HEADS):
        cols = pl.ds(h * DH, DH)
        out_ref[h, VALUE_AT:KV_ROWS, :] = v_ref[:, cols]
        out_ref[h, KV_ROWS:ROWS, :] = q_ref[:, cols]


def meta_rows(ref, i):
    return ref[i, META_AT:VALUE_AT, :].astype(F32)


def linear_kernel(info_ref, own_ref, other_ref, init_ref, partial_ref, weight_ref, state_ref, mark_ref):
    x, core = info_ref[0], info_ref[2]
    first = core == 0
    state = jnp.where(x == 0, init_ref[0], 0.0)
    carry = jnp.where(x == 0, jnp.zeros((1, TOK), F32), jnp.full((1, TOK), -1.0, F32))
    prefix = jnp.zeros((1, TOK), F32)
    places = lax.broadcasted_iota(jnp.int32, (TOK, TOK), 0)
    lanes = lax.broadcasted_iota(jnp.int32, (TOK, TOK), 1)
    causal = places >= lanes
    marked = (lanes >= 4) & (lanes < 8)
    number = (lanes - 4).astype(F32)
    start_doc = None

    def read(swap, i):
        mine, theirs = own_ref[i, 0:KV_ROWS, :], other_ref[i]
        got = jnp.where(swap, theirs, mine)
        rows = got[META_AT:VALUE_AT].astype(F32)
        cum, doc = rows[0:1] + rows[1:2] + rows[2:3], rows[3:4]
        overall = jnp.broadcast_to(cum[:, TOK - 1 :], (1, TOK))
        last = jnp.broadcast_to(doc[:, TOK - 1 :], (1, TOK))
        return got[:DH], got[VALUE_AT:], cum, doc, overall, last

    def advance(state, carry, prefix, block):
        keys, values, cum, doc, overall, last = block
        factor = jnp.where(doc == last, jnp.exp(overall - cum), 0.0)
        scaled = (keys.astype(F32) * factor).astype(BF16)
        keep = jnp.where(last == carry, jnp.exp(overall), 0.0)
        return dot(scaled, values) + keep * state, last, prefix + overall

    for i in range(HEADS):
        even = read(jnp.logical_not(first), i)
        odd = read(first, i)
        if start_doc is None:
            start_doc = jnp.broadcast_to(even[3][:, :1], (1, TOK))
        middle = advance(state, carry, prefix, even)
        at_state = jnp.where(first, state, middle[0])
        at_carry = jnp.where(first, carry, middle[1])
        at_prefix = jnp.where(first, prefix, middle[2])
        keys, values, cum, doc, _, _ = [jnp.where(first, a, b) for a, b in zip(even, odd)]
        queries = own_ref[i, KV_ROWS:ROWS, :]
        cum_col, doc_col = column(cum), column(doc)
        inside = causal & (doc_col == doc)
        fading = jnp.exp(jnp.where(inside, cum_col - cum, 0.0))
        weights = jnp.where(inside, fading * dot(queries, keys) * SCALE, 0.0).astype(BF16)
        grown = jnp.exp(cum_col) * SCALE
        outside = jnp.where(doc_col == at_carry, grown * split_dot(queries, at_state), 0.0)
        partial_ref[i] = dot(weights, values) + outside
        weight_ref[i] = jnp.where(doc_col == start_doc, jnp.exp(cum_col + at_prefix) * SCALE, 0.0)
        mark_ref[i] = jnp.where(marked & (doc_col == number), 1.0, 0.0).astype(BF16)
        state, carry, prefix = advance(*middle, odd)
    state_ref[0:DH, :] = state
    row = lax.broadcasted_iota(jnp.int32, (8, TOK), 0)
    state_ref[DH : DH + 8, :] = jnp.where(row == 0, prefix, jnp.where(row == 1, carry, start_doc))


def enter_kernel(
    info_ref, own_ref, partial_ref, weight_ref, state_ref, near_ref, far_ref, linear_ref, square_ref, need_ref
):
    x = info_ref[0]
    near_decay, near_doc = near_ref[DH : DH + 1, :], near_ref[DH + 1 : DH + 2, :]
    far_doc, start_doc = far_ref[DH + 1 : DH + 2, :], state_ref[DH + 2 : DH + 3, :]
    keep = jnp.where((far_doc == near_doc) & (x >= 2), jnp.exp(near_decay), 0.0)
    state = near_ref[0:DH, :] + keep * far_ref[0:DH, :]
    state = jnp.where((start_doc == near_doc) & (x >= 1), state, 0.0)
    high = state.astype(BF16)
    low = (state - high.astype(F32)).astype(BF16)
    queries = jnp.concatenate([own_ref[i, KV_ROWS:ROWS, :] for i in range(HEADS)], axis=0)
    product = dot(queries, jnp.concatenate([high, low], axis=1))
    product = product[:, :DH] + product[:, DH:]
    eye = lax.broadcasted_iota(jnp.int32, (TOK, DH), 0) == lax.broadcasted_iota(jnp.int32, (TOK, DH), 1)
    for i in range(HEADS):
        linear = partial_ref[i] + weight_ref[i] * product[i * TOK : (i + 1) * TOK]
        linear_ref[i] = linear.astype(BF16)
        square = jnp.sum(linear * linear, axis=1, keepdims=True)
        square_ref[i : i + 1, :] = jnp.sum(jnp.where(eye, square, 0.0), axis=0, keepdims=True)
    for tile in range(TILES):
        tile_doc = jnp.broadcast_to(meta_rows(own_ref, 2 * tile)[3:4, :1], (1, TOK))
        need_ref[2 * tile] = jnp.where(x >= 1, jnp.max(jnp.where(tile_doc == near_doc, 1, 0)), 0)
        need_ref[2 * tile + 1] = jnp.where(x >= 2, jnp.max(jnp.where(tile_doc == far_doc, 1, 0)), 0)


def marked_queries(own_ref, mark_ref, tile):
    i = 2 * tile
    queries = jnp.concatenate([own_ref[i, KV_ROWS:ROWS, :], own_ref[i + 1, KV_ROWS:ROWS, :]], axis=0)
    marks = jnp.concatenate([mark_ref[i], mark_ref[i + 1]], axis=0)[:, :META]
    return jnp.concatenate([queries, marks], axis=1)


def absorb(queries, ref, pieces, diagonal, old):
    scores = []
    top = None
    for m in pieces:
        keys = jnp.concatenate([ref[2 * m, 0:VALUE_AT, :], ref[2 * m + 1, 0:VALUE_AT, :]], axis=1)
        score = dot(queries, keys)
        if m == diagonal[0]:
            score = jnp.where(diagonal[1], score, LOW)
        scores.append(score)
        most = jnp.maximum(score[:, :TOK], score[:, TOK:])
        top = most if top is None else jnp.maximum(top, most)
    top = jnp.max(top, axis=1, keepdims=True)
    if old is not None:
        top = jnp.maximum(top, old[0])
    base = top * EXP2_SCALE
    sums, output = None, None
    for m, score in zip(pieces, scores):
        weights = jnp.exp2(score * EXP2_SCALE - base)
        part = weights[:, :TOK] + weights[:, TOK:]
        sums = part if sums is None else sums + part
        values = jnp.concatenate([ref[2 * m, VALUE_AT:KV_ROWS, :], ref[2 * m + 1, VALUE_AT:KV_ROWS, :]], axis=0)
        product = dot(weights.astype(BF16), values)
        output = product if output is None else output + product
    total = jnp.sum(sums, axis=1, keepdims=True)
    if old is not None:
        shrink = jnp.exp2(old[0] * EXP2_SCALE - base)
        total = total + old[1] * shrink
        output = output + old[2] * shrink
    return top, total, output


def tile_places(core, own):
    rows = lax.broadcasted_iota(jnp.int32, (CHUNK, CHUNK), 0)
    lanes = lax.broadcasted_iota(jnp.int32, (CHUNK, CHUNK), 1)
    key_core = core if own else 1 - core
    at = jnp.where(rows < TOK, rows, rows + TOK) + core * TOK
    key = jnp.where(lanes < TOK, lanes, lanes + TOK) + key_core * TOK
    return at, key


def span_of(tile):
    return pl.ds(tile * CHUNK, CHUNK)


def load_part(refs, tile):
    top_ref, total_ref, output_ref = refs
    span = span_of(tile)
    return top_ref[span, :1], total_ref[span, :1], output_ref[span, :]


def store_part(refs, tile, part):
    span = span_of(tile)
    for ref, value in zip(refs, part):
        ref[span, :] = jnp.broadcast_to(value, (CHUNK, TOK))


def own_window_kernel(info_ref, own_ref, other_ref, mark_ref, *refs):
    core = info_ref[2]
    masks = []
    for own in (True, False):
        at, key = tile_places(core, own)
        masks.append(key <= at)
    for tile in range(TILES):
        queries = marked_queries(own_ref, mark_ref, tile)
        part = absorb(queries, own_ref, range(tile + 1), (tile, masks[0]), None)
        part = absorb(queries, other_ref, range(tile + 1), (tile, masks[1]), part)
        store_part(refs, tile, part)


def near_kernel(need_ref, own_ref, mark_ref, near_ref, other_ref, a_ref, b_ref, c_ref, *refs):
    olds = (a_ref, b_ref, c_ref)
    for tile in range(TILES):
        needed = need_ref[2 * tile] == 1

        @pl.when(needed)
        def _(tile=tile):
            queries = marked_queries(own_ref, mark_ref, tile)
            part = absorb(queries, near_ref, range(TILES), (None, None), load_part(olds, tile))
            store_part(refs, tile, absorb(queries, other_ref, range(TILES), (None, None), part))

        @pl.when(jnp.logical_not(needed))
        def _(tile=tile):
            store_part(refs, tile, load_part(olds, tile))


def far_blocks(core, own, own_ref, mark_ref, need_ref, far_ref, olds, refs):
    at, key = tile_places(core, own)
    mask = key > at
    for tile in range(TILES):
        needed = need_ref[2 * tile + 1] == 1

        @pl.when(needed)
        def _(tile=tile):
            queries = marked_queries(own_ref, mark_ref, tile)
            store_part(refs, tile, absorb(queries, far_ref, range(tile, TILES), (tile, mask), load_part(olds, tile)))

        @pl.when(jnp.logical_not(needed))
        def _(tile=tile):
            store_part(refs, tile, load_part(olds, tile))


def far_own_kernel(info_ref, need_ref, own_ref, mark_ref, far_ref, a_ref, b_ref, c_ref, *refs):
    far_blocks(info_ref[2], True, own_ref, mark_ref, need_ref, far_ref, (a_ref, b_ref, c_ref), refs)


def far_other_kernel(
    info_ref, need_ref, own_ref, mark_ref, far_ref, a_ref, b_ref, c_ref, linear_ref, square_ref, out_ref, *refs
):
    row = lax.broadcasted_iota(jnp.int32, (META, TOK), 0)
    for i in range(HEADS):
        out_ref[i, TOK : 2 * TOK, :] = linear_ref[i]
        meta = jnp.zeros((META, TOK), F32)
        for n, part in enumerate(split3(square_ref[i : i + 1, :])):
            meta = jnp.where(row == n, jnp.broadcast_to(part.astype(F32), (META, TOK)), meta)
        out_ref[i, 2 * TOK :, :] = meta.astype(BF16)
    far_blocks(info_ref[2], False, own_ref, mark_ref, need_ref, far_ref, (a_ref, b_ref, c_ref), refs)
    _, total_ref, output_ref = refs
    for i in range(HEADS):
        span = pl.ds(i * TOK, TOK)
        out_ref[i, 0:TOK, :] = (output_ref[span, :] / total_ref[span, :]).astype(BF16)


def finish_kernel(got_ref, gain_ref, out_ref):
    total = jnp.zeros((1, TOK), F32)
    for h in range(HEADS):
        total = total + joined(got_ref[h, 2 * TOK :, :], 0)
    inverse = column(lax.rsqrt(total / (HEAD_TOTAL * DH) + 1e-06))
    for h in range(HEADS):
        cols = pl.ds(h * DH, DH)
        linear = got_ref[h, TOK : 2 * TOK, :].astype(F32)
        window = got_ref[h, 0:TOK, :].astype(F32)
        out_ref[:, cols] = (gain_ref[:, cols] * linear * inverse + window).astype(BF16)


VMEM = pl.BlockSpec(memory_space=pltpu.VMEM)
SMEM = pl.BlockSpec(memory_space=pltpu.SMEM)
HBM = pl.BlockSpec(memory_space=pltpu.HBM)


LIMIT = {"prepare": 58}


def call(kernel, name, specs, shapes, scratch=(), outs=None):
    many = isinstance(shapes, (list, tuple))
    return pl.pallas_call(
        kernel,
        name=name,
        out_shape=shapes,
        in_specs=specs,
        out_specs=outs or ([VMEM] * len(shapes) if many else VMEM),
        scratch_shapes=list(scratch),
        compiler_params=pltpu.CompilerParams(vmem_limit_bytes=LIMIT.get(name, 16) * 2**20),
        cost_estimate=pl.CostEstimate(flops=0, bytes_accessed=0, transcendentals=0),
    )


def body(queries, keys, values, init_state, lin_gain, rate_table, rate_index, speed, drop, doc_id):
    x, z, core = (lax.axis_index(a).astype(jnp.int32) for a in ("x", "z", "core"))
    info = jnp.stack([x, z, core])
    shape = jax.ShapeDtypeStruct
    packed = call(
        prepare_kernel,
        "prepare",
        [SMEM, SMEM, HBM, HBM, HBM, VMEM, VMEM, VMEM],
        shape((HEADS, ROWS, TOK), BF16),
        scratch=[pltpu.VMEM((TOK, HEADS * DH), BF16)] * 3 + [pltpu.SemaphoreType.DMA((3,))],
    )(rate_table, rate_index, queries, keys, values, speed.T, drop.T, doc_id[None, :])
    own = lax.all_to_all(packed, "z", 0, 0, tiled=True)
    sent = own[:, :KV_ROWS]
    pair = [(0, 1), (1, 0)]
    near = lax.ppermute(sent, "x", [(0, 1), (1, 2), (2, 3)])
    far = lax.ppermute(sent, "x", [(0, 2), (1, 3)])
    other = lax.ppermute(sent, "core", pair)

    tokens = HEADS * TOK
    part_shapes = [shape((tokens, TOK), F32), shape((tokens, TOK), F32), shape((tokens, DH), F32)]
    init = lax.dynamic_slice_in_dim(init_state, z, 1, 0)
    partial, weight, state, mark = call(
        linear_kernel,
        "linear",
        [SMEM] + [VMEM] * 3,
        [
            shape((HEADS, TOK, DH), F32),
            shape((HEADS, TOK, DH), F32),
            shape((DH + 8, DH), F32),
            shape((HEADS, TOK, TOK), BF16),
        ],
    )(info, own, other, init)
    near_state = lax.ppermute(state, "x", [(0, 1), (1, 2), (2, 3)])
    far_state = lax.ppermute(state, "x", [(0, 2), (1, 3)])
    own_part = call(
        own_window_kernel, "own_window", [SMEM] + [VMEM] * 3, part_shapes
    )(info, own, other, mark)
    near_state, far_state, own_part = lax.optimization_barrier((near_state, far_state, own_part))
    linear, square, need = call(
        enter_kernel,
        "enter",
        [SMEM] + [VMEM] * 6,
        [shape((HEADS, TOK, DH), BF16), shape((HEADS, TOK), F32), shape((2 * TILES,), jnp.int32)],
        outs=[VMEM, VMEM, SMEM],
    )(info, own, partial, weight, state, near_state, far_state)
    square = square + lax.ppermute(square, "head", [(i, i ^ 1) for i in range(4)])
    near, need, own_part, square = lax.optimization_barrier((near, need, own_part, square))
    square = square + lax.ppermute(square, "head", [(i, i ^ 2) for i in range(4)])
    near_other = lax.ppermute(near, "core", pair)
    part = call(near_kernel, "near_window", [SMEM] + [VMEM] * 7, part_shapes)(
        need, own, mark, near, near_other, *own_part
    )
    far, part, square = lax.optimization_barrier((far, part, square))
    far_other = lax.ppermute(far, "core", pair)
    part = call(far_own_kernel, "far_own", [SMEM] * 2 + [VMEM] * 6, part_shapes)(info, need, own, mark, far, *part)
    mixed = call(
        far_other_kernel,
        "far_other",
        [SMEM] * 2 + [VMEM] * 8,
        shape((HEADS, 2 * TOK + META, DH), BF16),
        scratch=[pltpu.VMEM((tokens, TOK), F32)] * 3,
    )(info, need, own, mark, far_other, *part, linear, square)
    back = lax.all_to_all(mixed, "z", 0, 0, tiled=True)
    return call(finish_kernel, "finish", [VMEM] * 2, shape((TOK, HEADS * DH), BF16))(
        back, lin_gain[None, :]
    )


def solution(mesh):
    split = Mesh(mesh.devices.reshape(4, 8, 2, 4), ("x", "z", "core", "head"))
    ctx = ("x", "z", "core")
    placed = (
        P(ctx, "head"),
        P(ctx, "head"),
        P(ctx, "head"),
        P("head", None, None),
        P("head"),
        P(),
        P("head"),
        P(ctx, "head"),
        P(ctx, "head"),
        P(ctx),
    )
    return jax.shard_map(body, mesh=split, in_specs=placed, out_specs=P(ctx, "head"), check_vma=False)
```

```python
import math

import jax
import jax.numpy as jnp
from jax import lax
from jax.experimental import pallas as pl
from jax.experimental.pallas import tpu as pltpu
from jax.sharding import Mesh
from jax.sharding import PartitionSpec as P

HEAD_TOTAL = 32
DH = 128
TOK = 128
WINDOW = 4096
HEADS = 8
META = 16
KV_ROWS = 2 * DH + META
ROWS = KV_ROWS + TOK
PLANE = 2 * HEADS * TOK
SCALE = 1.0 / math.sqrt(DH)
EXP2_SCALE = SCALE / math.log(2.0)
LOW = -1e30
F32 = jnp.float32
BF16 = jnp.bfloat16
CHUNK = 2 * TOK
TILES = HEADS // 2
META_AT = DH
VALUE_AT = DH + META


def dot(a, b):
    return jnp.dot(a, b, preferred_element_type=F32)


def split3(x):
    high = x.astype(BF16)
    rest = x - high.astype(F32)
    mid = rest.astype(BF16)
    low = (rest - mid.astype(F32)).astype(BF16)
    return high, mid, low


def joined(rows, at):
    part = rows.astype(F32)
    return part[at : at + 1] + part[at + 1 : at + 2] + part[at + 2 : at + 3]


def column(row):
    return jnp.transpose(jnp.broadcast_to(row, (TOK, TOK)))


def split_dot(a, state):
    high = state.astype(BF16)
    low = (state - high.astype(F32)).astype(BF16)
    return dot(a, high) + dot(a, low)


def prepare_kernel(
    table_ref, index_ref, q_hbm, k_hbm, v_hbm, speed_ref, drop_ref, doc_ref, out_ref, q_ref, k_ref, v_ref, sems
):
    copies = [
        pltpu.make_async_copy(src, dst, sems.at[n])
        for n, (src, dst) in enumerate(((k_hbm, k_ref), (v_hbm, v_ref), (q_hbm, q_ref)))
    ]
    for copy in copies:
        copy.start()
    head = lax.broadcasted_iota(jnp.int32, (HEADS, TOK), 0)
    rate = jnp.zeros((HEADS, TOK), F32)
    for h in range(HEADS):
        rate = jnp.where(head == h, table_ref[index_ref[h]], rate)
    log_decay = -rate * speed_ref[...] - drop_ref[...]
    upto = (
        lax.broadcasted_iota(jnp.int32, (TOK, TOK), 0)
        <= lax.broadcasted_iota(jnp.int32, (TOK, TOK), 1)
    ).astype(F32)
    cum = jnp.dot(log_decay, upto, precision=lax.Precision.HIGHEST, preferred_element_type=F32)
    parts = [part.astype(F32) for part in split3(cum)]
    row = lax.broadcasted_iota(jnp.int32, (META, TOK), 0)
    doc = jnp.broadcast_to(doc_ref[...].astype(F32), (META, TOK))
    bias = jnp.where(doc == (row - 4).astype(F32), 0.0, LOW)
    shared = jnp.where(row == 3, doc, jnp.where((row >= 4) & (row < 8), bias, 0.0))
    for h in range(HEADS):
        meta = shared
        for n, part in enumerate(parts):
            meta = jnp.where(row == n, jnp.broadcast_to(part[h : h + 1], (META, TOK)), meta)
        out_ref[h, META_AT:VALUE_AT, :] = meta.astype(BF16)
    copies[0].wait()
    for h in range(HEADS):
        out_ref[h, 0:DH, :] = jnp.transpose(k_ref[:, pl.ds(h * DH, DH)])
    copies[1].wait()
    copies[2].wait()
    for h in range(HEADS):
        cols = pl.ds(h * DH, DH)
        out_ref[h, VALUE_AT:KV_ROWS, :] = v_ref[:, cols]
        out_ref[h, KV_ROWS:ROWS, :] = q_ref[:, cols]


def meta_rows(ref, i):
    return ref[i, META_AT:VALUE_AT, :].astype(F32)


def linear_kernel(info_ref, own_ref, other_ref, init_ref, partial_ref, weight_ref, state_ref, mark_ref):
    x, core = info_ref[0], info_ref[2]
    first = core == 0
    state = jnp.where(x == 0, init_ref[0], 0.0)
    carry = jnp.where(x == 0, jnp.zeros((1, TOK), F32), jnp.full((1, TOK), -1.0, F32))
    prefix = jnp.zeros((1, TOK), F32)
    places = lax.broadcasted_iota(jnp.int32, (TOK, TOK), 0)
    lanes = lax.broadcasted_iota(jnp.int32, (TOK, TOK), 1)
    causal = places >= lanes
    marked = (lanes >= 4) & (lanes < 8)
    number = (lanes - 4).astype(F32)
    start_doc = None

    def read(swap, i):
        mine, theirs = own_ref[i, 0:KV_ROWS, :], other_ref[i]
        got = jnp.where(swap, theirs, mine)
        rows = got[META_AT:VALUE_AT].astype(F32)
        cum, doc = rows[0:1] + rows[1:2] + rows[2:3], rows[3:4]
        overall = jnp.broadcast_to(cum[:, TOK - 1 :], (1, TOK))
        last = jnp.broadcast_to(doc[:, TOK - 1 :], (1, TOK))
        return got[:DH], got[VALUE_AT:], cum, doc, overall, last

    def advance(state, carry, prefix, block):
        keys, values, cum, doc, overall, last = block
        factor = jnp.where(doc == last, jnp.exp(overall - cum), 0.0)
        scaled = (keys.astype(F32) * factor).astype(BF16)
        keep = jnp.where(last == carry, jnp.exp(overall), 0.0)
        return dot(scaled, values) + keep * state, last, prefix + overall

    for i in range(HEADS):
        even = read(jnp.logical_not(first), i)
        odd = read(first, i)
        if start_doc is None:
            start_doc = jnp.broadcast_to(even[3][:, :1], (1, TOK))
        middle = advance(state, carry, prefix, even)
        at_state = jnp.where(first, state, middle[0])
        at_carry = jnp.where(first, carry, middle[1])
        at_prefix = jnp.where(first, prefix, middle[2])
        keys, values, cum, doc, _, _ = [jnp.where(first, a, b) for a, b in zip(even, odd)]
        queries = own_ref[i, KV_ROWS:ROWS, :]
        cum_col, doc_col = column(cum), column(doc)
        inside = causal & (doc_col == doc)
        fading = jnp.exp(jnp.where(inside, cum_col - cum, 0.0))
        weights = jnp.where(inside, fading * dot(queries, keys) * SCALE, 0.0).astype(BF16)
        grown = jnp.exp(cum_col) * SCALE
        outside = jnp.where(doc_col == at_carry, grown * split_dot(queries, at_state), 0.0)
        partial_ref[i] = dot(weights, values) + outside
        weight_ref[i] = jnp.where(doc_col == start_doc, jnp.exp(cum_col + at_prefix) * SCALE, 0.0)
        mark_ref[i] = jnp.where(marked & (doc_col == number), 1.0, 0.0).astype(BF16)
        state, carry, prefix = advance(*middle, odd)
    state_ref[0:DH, :] = state
    row = lax.broadcasted_iota(jnp.int32, (8, TOK), 0)
    state_ref[DH : DH + 8, :] = jnp.where(row == 0, prefix, jnp.where(row == 1, carry, start_doc))


def enter_kernel(
    info_ref, own_ref, partial_ref, weight_ref, state_ref, near_ref, far_ref, linear_ref, square_ref, need_ref
):
    x = info_ref[0]
    near_decay, near_doc = near_ref[DH : DH + 1, :], near_ref[DH + 1 : DH + 2, :]
    far_doc, start_doc = far_ref[DH + 1 : DH + 2, :], state_ref[DH + 2 : DH + 3, :]
    keep = jnp.where((far_doc == near_doc) & (x >= 2), jnp.exp(near_decay), 0.0)
    state = near_ref[0:DH, :] + keep * far_ref[0:DH, :]
    state = jnp.where((start_doc == near_doc) & (x >= 1), state, 0.0)
    high = state.astype(BF16)
    low = (state - high.astype(F32)).astype(BF16)
    queries = jnp.concatenate([own_ref[i, KV_ROWS:ROWS, :] for i in range(HEADS)], axis=0)
    product = dot(queries, jnp.concatenate([high, low], axis=1))
    product = product[:, :DH] + product[:, DH:]
    eye = lax.broadcasted_iota(jnp.int32, (TOK, DH), 0) == lax.broadcasted_iota(jnp.int32, (TOK, DH), 1)
    for i in range(HEADS):
        linear = partial_ref[i] + weight_ref[i] * product[i * TOK : (i + 1) * TOK]
        linear_ref[i] = linear.astype(BF16)
        square = jnp.sum(linear * linear, axis=1, keepdims=True)
        square_ref[i : i + 1, :] = jnp.sum(jnp.where(eye, square, 0.0), axis=0, keepdims=True)
    for tile in range(TILES):
        tile_doc = jnp.broadcast_to(meta_rows(own_ref, 2 * tile)[3:4, :1], (1, TOK))
        need_ref[2 * tile] = jnp.where(x >= 1, jnp.max(jnp.where(tile_doc == near_doc, 1, 0)), 0)
        need_ref[2 * tile + 1] = jnp.where(x >= 2, jnp.max(jnp.where(tile_doc == far_doc, 1, 0)), 0)


def marked_queries(own_ref, mark_ref, tile):
    i = 2 * tile
    queries = jnp.concatenate([own_ref[i, KV_ROWS:ROWS, :], own_ref[i + 1, KV_ROWS:ROWS, :]], axis=0)
    marks = jnp.concatenate([mark_ref[i], mark_ref[i + 1]], axis=0)[:, :META]
    return jnp.concatenate([queries, marks], axis=1)


def absorb(queries, ref, pieces, diagonal, old):
    scores = []
    top = None
    for m in pieces:
        keys = jnp.concatenate([ref[2 * m, 0:VALUE_AT, :], ref[2 * m + 1, 0:VALUE_AT, :]], axis=1)
        score = dot(queries, keys)
        if m == diagonal[0]:
            score = jnp.where(diagonal[1], score, LOW)
        scores.append(score)
        most = jnp.maximum(score[:, :TOK], score[:, TOK:])
        top = most if top is None else jnp.maximum(top, most)
    top = jnp.max(top, axis=1, keepdims=True)
    if old is not None:
        top = jnp.maximum(top, old[0])
    base = top * EXP2_SCALE
    sums, output = None, None
    for m, score in zip(pieces, scores):
        weights = jnp.exp2(score * EXP2_SCALE - base)
        part = weights[:, :TOK] + weights[:, TOK:]
        sums = part if sums is None else sums + part
        values = jnp.concatenate([ref[2 * m, VALUE_AT:KV_ROWS, :], ref[2 * m + 1, VALUE_AT:KV_ROWS, :]], axis=0)
        product = dot(weights.astype(BF16), values)
        output = product if output is None else output + product
    total = jnp.sum(sums, axis=1, keepdims=True)
    if old is not None:
        shrink = jnp.exp2(old[0] * EXP2_SCALE - base)
        total = total + old[1] * shrink
        output = output + old[2] * shrink
    return top, total, output


def tile_places(core, own):
    rows = lax.broadcasted_iota(jnp.int32, (CHUNK, CHUNK), 0)
    lanes = lax.broadcasted_iota(jnp.int32, (CHUNK, CHUNK), 1)
    key_core = core if own else 1 - core
    at = jnp.where(rows < TOK, rows, rows + TOK) + core * TOK
    key = jnp.where(lanes < TOK, lanes, lanes + TOK) + key_core * TOK
    return at, key


def span_of(tile):
    return pl.ds(tile * CHUNK, CHUNK)


def load_part(refs, tile):
    top_ref, total_ref, output_ref = refs
    span = span_of(tile)
    return top_ref[span, :1], total_ref[span, :1], output_ref[span, :]


def store_part(refs, tile, part):
    span = span_of(tile)
    for ref, value in zip(refs, part):
        ref[span, :] = jnp.broadcast_to(value, (CHUNK, TOK))


def own_window_kernel(info_ref, own_ref, other_ref, mark_ref, *refs):
    core = info_ref[2]
    masks = []
    for own in (True, False):
        at, key = tile_places(core, own)
        masks.append(key <= at)
    for tile in range(TILES):
        queries = marked_queries(own_ref, mark_ref, tile)
        part = absorb(queries, own_ref, range(tile + 1), (tile, masks[0]), None)
        part = absorb(queries, other_ref, range(tile + 1), (tile, masks[1]), part)
        store_part(refs, tile, part)


def near_kernel(need_ref, own_ref, mark_ref, near_ref, other_ref, more_ref, a_ref, b_ref, c_ref, *refs):
    olds = (a_ref, b_ref, c_ref)
    for tile in range(TILES):
        needed = need_ref[2 * tile] == 1

        @pl.when(needed)
        def _(tile=tile):
            queries = marked_queries(own_ref, mark_ref, tile)
            part = absorb(queries, near_ref, range(TILES), (None, None), load_part(olds, tile))
            part = absorb(queries, other_ref, range(TILES // 2), (None, None), part)
            store_part(refs, tile, absorb(queries, more_ref, range(TILES // 2), (None, None), part))

        @pl.when(jnp.logical_not(needed))
        def _(tile=tile):
            store_part(refs, tile, load_part(olds, tile))


def far_blocks(core, own, own_ref, mark_ref, need_ref, far_ref, olds, refs):
    at, key = tile_places(core, own)
    mask = key > at
    for tile in range(TILES):
        needed = need_ref[2 * tile + 1] == 1

        @pl.when(needed)
        def _(tile=tile):
            queries = marked_queries(own_ref, mark_ref, tile)
            store_part(refs, tile, absorb(queries, far_ref, range(tile, TILES), (tile, mask), load_part(olds, tile)))

        @pl.when(jnp.logical_not(needed))
        def _(tile=tile):
            store_part(refs, tile, load_part(olds, tile))


def far_own_kernel(info_ref, need_ref, own_ref, mark_ref, far_ref, a_ref, b_ref, c_ref, *refs):
    far_blocks(info_ref[2], True, own_ref, mark_ref, need_ref, far_ref, (a_ref, b_ref, c_ref), refs)


def far_other_kernel(
    info_ref, need_ref, own_ref, mark_ref, far_ref, a_ref, b_ref, c_ref, linear_ref, square_ref, out_ref, *refs
):
    row = lax.broadcasted_iota(jnp.int32, (META, TOK), 0)
    for i in range(HEADS):
        out_ref[i, TOK : 2 * TOK, :] = linear_ref[i]
        meta = jnp.zeros((META, TOK), F32)
        for n, part in enumerate(split3(square_ref[i : i + 1, :])):
            meta = jnp.where(row == n, jnp.broadcast_to(part.astype(F32), (META, TOK)), meta)
        out_ref[i, 2 * TOK :, :] = meta.astype(BF16)
    far_blocks(info_ref[2], False, own_ref, mark_ref, need_ref, far_ref, (a_ref, b_ref, c_ref), refs)
    _, total_ref, output_ref = refs
    for i in range(HEADS):
        span = pl.ds(i * TOK, TOK)
        out_ref[i, 0:TOK, :] = (output_ref[span, :] / total_ref[span, :]).astype(BF16)


def finish_kernel(got_ref, gain_ref, out_ref):
    total = jnp.zeros((1, TOK), F32)
    for h in range(HEADS):
        total = total + joined(got_ref[h, 2 * TOK :, :], 0)
    inverse = column(lax.rsqrt(total / (HEAD_TOTAL * DH) + 1e-06))
    for h in range(HEADS):
        cols = pl.ds(h * DH, DH)
        linear = got_ref[h, TOK : 2 * TOK, :].astype(F32)
        window = got_ref[h, 0:TOK, :].astype(F32)
        out_ref[:, cols] = (gain_ref[:, cols] * linear * inverse + window).astype(BF16)


VMEM = pl.BlockSpec(memory_space=pltpu.VMEM)
SMEM = pl.BlockSpec(memory_space=pltpu.SMEM)
HBM = pl.BlockSpec(memory_space=pltpu.HBM)


LIMIT = {"prepare": 58}


def call(kernel, name, specs, shapes, scratch=(), outs=None):
    many = isinstance(shapes, (list, tuple))
    return pl.pallas_call(
        kernel,
        name=name,
        out_shape=shapes,
        in_specs=specs,
        out_specs=outs or ([VMEM] * len(shapes) if many else VMEM),
        scratch_shapes=list(scratch),
        compiler_params=pltpu.CompilerParams(vmem_limit_bytes=LIMIT.get(name, 16) * 2**20),
        cost_estimate=pl.CostEstimate(flops=0, bytes_accessed=0, transcendentals=0),
    )


def body(queries, keys, values, init_state, lin_gain, rate_table, rate_index, speed, drop, doc_id):
    x, z, core = (lax.axis_index(a).astype(jnp.int32) for a in ("x", "z", "core"))
    info = jnp.stack([x, z, core])
    shape = jax.ShapeDtypeStruct
    packed = call(
        prepare_kernel,
        "prepare",
        [SMEM, SMEM, HBM, HBM, HBM, VMEM, VMEM, VMEM],
        shape((HEADS, ROWS, TOK), BF16),
        scratch=[pltpu.VMEM((TOK, HEADS * DH), BF16)] * 3 + [pltpu.SemaphoreType.DMA((3,))],
    )(rate_table, rate_index, queries, keys, values, speed.T, drop.T, doc_id[None, :])
    own = lax.all_to_all(packed, "z", 0, 0, tiled=True)
    sent = own[:, :KV_ROWS]
    pair = [(0, 1), (1, 0)]
    near = lax.ppermute(sent, "x", [(0, 1), (1, 2), (2, 3)])
    other = lax.ppermute(sent, "core", pair)

    tokens = HEADS * TOK
    part_shapes = [shape((tokens, TOK), F32), shape((tokens, TOK), F32), shape((tokens, DH), F32)]
    init = lax.dynamic_slice_in_dim(init_state, z, 1, 0)
    partial, weight, state, mark = call(
        linear_kernel,
        "linear",
        [SMEM] + [VMEM] * 3,
        [
            shape((HEADS, TOK, DH), F32),
            shape((HEADS, TOK, DH), F32),
            shape((DH + 8, DH), F32),
            shape((HEADS, TOK, TOK), BF16),
        ],
    )(info, own, other, init)
    near_state = lax.ppermute(state, "x", [(0, 1), (1, 2), (2, 3)])
    far_state = lax.ppermute(state, "x", [(0, 2), (1, 3)])
    own_part = call(
        own_window_kernel, "own_window", [SMEM] + [VMEM] * 3, part_shapes
    )(info, own, other, mark)
    sent, own_part = lax.optimization_barrier((sent, own_part))
    far = lax.ppermute(sent, "x", [(0, 2), (1, 3)])
    near_state, far_state, own_part = lax.optimization_barrier((near_state, far_state, own_part))
    linear, square, need = call(
        enter_kernel,
        "enter",
        [SMEM] + [VMEM] * 6,
        [shape((HEADS, TOK, DH), BF16), shape((HEADS, TOK), F32), shape((2 * TILES,), jnp.int32)],
        outs=[VMEM, VMEM, SMEM],
    )(info, own, partial, weight, state, near_state, far_state)
    square = square + lax.ppermute(square, "head", [(i, i ^ 1) for i in range(4)])
    near, need, own_part, square = lax.optimization_barrier((near, need, own_part, square))
    square = square + lax.ppermute(square, "head", [(i, i ^ 2) for i in range(4)])
    near_other = [lax.ppermute(near[at : at + TILES], "core", pair) for at in (0, TILES)]
    part = call(near_kernel, "near_window", [SMEM] + [VMEM] * 8, part_shapes)(
        need, own, mark, near, *near_other, *own_part
    )
    far, part, square = lax.optimization_barrier((far, part, square))
    far_other = lax.ppermute(far, "core", pair)
    part = call(far_own_kernel, "far_own", [SMEM] * 2 + [VMEM] * 6, part_shapes)(info, need, own, mark, far, *part)
    mixed = call(
        far_other_kernel,
        "far_other",
        [SMEM] * 2 + [VMEM] * 8,
        shape((HEADS, 2 * TOK + META, DH), BF16),
        scratch=[pltpu.VMEM((tokens, TOK), F32)] * 3,
    )(info, need, own, mark, far_other, *part, linear, square)
    back = lax.all_to_all(mixed, "z", 0, 0, tiled=True)
    return call(finish_kernel, "finish", [VMEM] * 2, shape((TOK, HEADS * DH), BF16))(
        back, lin_gain[None, :]
    )


def solution(mesh):
    split = Mesh(mesh.devices.reshape(4, 8, 2, 4), ("x", "z", "core", "head"))
    ctx = ("x", "z", "core")
    placed = (
        P(ctx, "head"),
        P(ctx, "head"),
        P(ctx, "head"),
        P("head", None, None),
        P("head"),
        P(),
        P("head"),
        P(ctx, "head"),
        P(ctx, "head"),
        P(ctx),
    )
    return jax.shard_map(body, mesh=split, in_specs=placed, out_specs=P(ctx, "head"), check_vma=False)
```

```python
import math

import jax
import jax.numpy as jnp
from jax import lax
from jax.experimental import pallas as pl
from jax.experimental.pallas import tpu as pltpu
from jax.sharding import Mesh
from jax.sharding import PartitionSpec as P

HEAD_TOTAL = 32
DH = 128
TOK = 128
WINDOW = 4096
HEADS = 8
META = 16
KV_ROWS = 2 * DH + META
ROWS = KV_ROWS + TOK
PLANE = 2 * HEADS * TOK
SCALE = 1.0 / math.sqrt(DH)
EXP2_SCALE = SCALE / math.log(2.0)
LOW = -1e30
F32 = jnp.float32
BF16 = jnp.bfloat16
CHUNK = 2 * TOK
TILES = HEADS // 2
META_AT = DH
VALUE_AT = DH + META


def dot(a, b):
    return jnp.dot(a, b, preferred_element_type=F32)


def split3(x):
    high = x.astype(BF16)
    rest = x - high.astype(F32)
    mid = rest.astype(BF16)
    low = (rest - mid.astype(F32)).astype(BF16)
    return high, mid, low


def joined(rows, at):
    part = rows.astype(F32)
    return part[at : at + 1] + part[at + 1 : at + 2] + part[at + 2 : at + 3]


def column(row):
    return jnp.transpose(jnp.broadcast_to(row, (TOK, TOK)))


def split_dot(a, state):
    high = state.astype(BF16)
    low = (state - high.astype(F32)).astype(BF16)
    return dot(a, high) + dot(a, low)


def prepare_kernel(
    table_ref, index_ref, q_hbm, k_hbm, v_hbm, speed_ref, drop_ref, doc_ref, out_ref, q_ref, k_ref, v_ref, sems
):
    copies = [
        pltpu.make_async_copy(src, dst, sems.at[n])
        for n, (src, dst) in enumerate(((k_hbm, k_ref), (v_hbm, v_ref), (q_hbm, q_ref)))
    ]
    for copy in copies:
        copy.start()
    head = lax.broadcasted_iota(jnp.int32, (HEADS, TOK), 0)
    rate = jnp.zeros((HEADS, TOK), F32)
    for h in range(HEADS):
        rate = jnp.where(head == h, table_ref[index_ref[h]], rate)
    log_decay = -rate * speed_ref[...] - drop_ref[...]
    upto = (
        lax.broadcasted_iota(jnp.int32, (TOK, TOK), 0)
        <= lax.broadcasted_iota(jnp.int32, (TOK, TOK), 1)
    ).astype(F32)
    cum = jnp.dot(log_decay, upto, precision=lax.Precision.HIGHEST, preferred_element_type=F32)
    parts = [part.astype(F32) for part in split3(cum)]
    row = lax.broadcasted_iota(jnp.int32, (META, TOK), 0)
    doc = jnp.broadcast_to(doc_ref[...].astype(F32), (META, TOK))
    bias = jnp.where(doc == (row - 4).astype(F32), 0.0, LOW)
    shared = jnp.where(row == 3, doc, jnp.where((row >= 4) & (row < 8), bias, 0.0))
    for h in range(HEADS):
        meta = shared
        for n, part in enumerate(parts):
            meta = jnp.where(row == n, jnp.broadcast_to(part[h : h + 1], (META, TOK)), meta)
        out_ref[h, META_AT:VALUE_AT, :] = meta.astype(BF16)
    copies[0].wait()
    for h in range(HEADS):
        out_ref[h, 0:DH, :] = jnp.transpose(k_ref[:, pl.ds(h * DH, DH)])
    copies[1].wait()
    copies[2].wait()
    for h in range(HEADS):
        cols = pl.ds(h * DH, DH)
        out_ref[h, VALUE_AT:KV_ROWS, :] = v_ref[:, cols]
        out_ref[h, KV_ROWS:ROWS, :] = q_ref[:, cols]


def meta_rows(ref, i):
    return ref[i, META_AT:VALUE_AT, :].astype(F32)


def linear_kernel(info_ref, own_ref, other_ref, init_ref, partial_ref, weight_ref, state_ref, mark_ref):
    x, core = info_ref[0], info_ref[2]
    first = core == 0
    state = jnp.where(x == 0, init_ref[0], 0.0)
    carry = jnp.where(x == 0, jnp.zeros((1, TOK), F32), jnp.full((1, TOK), -1.0, F32))
    prefix = jnp.zeros((1, TOK), F32)
    places = lax.broadcasted_iota(jnp.int32, (TOK, TOK), 0)
    lanes = lax.broadcasted_iota(jnp.int32, (TOK, TOK), 1)
    causal = places >= lanes
    marked = (lanes >= 4) & (lanes < 8)
    number = (lanes - 4).astype(F32)
    start_doc = None

    def read(swap, i):
        mine, theirs = own_ref[i, 0:KV_ROWS, :], other_ref[i]
        got = jnp.where(swap, theirs, mine)
        rows = got[META_AT:VALUE_AT].astype(F32)
        cum, doc = rows[0:1] + rows[1:2] + rows[2:3], rows[3:4]
        overall = jnp.broadcast_to(cum[:, TOK - 1 :], (1, TOK))
        last = jnp.broadcast_to(doc[:, TOK - 1 :], (1, TOK))
        return got[:DH], got[VALUE_AT:], cum, doc, overall, last

    def advance(state, carry, prefix, block):
        keys, values, cum, doc, overall, last = block
        factor = jnp.where(doc == last, jnp.exp(overall - cum), 0.0)
        scaled = (keys.astype(F32) * factor).astype(BF16)
        keep = jnp.where(last == carry, jnp.exp(overall), 0.0)
        return dot(scaled, values) + keep * state, last, prefix + overall

    for i in range(HEADS):
        even = read(jnp.logical_not(first), i)
        odd = read(first, i)
        if start_doc is None:
            start_doc = jnp.broadcast_to(even[3][:, :1], (1, TOK))
        middle = advance(state, carry, prefix, even)
        at_state = jnp.where(first, state, middle[0])
        at_carry = jnp.where(first, carry, middle[1])
        at_prefix = jnp.where(first, prefix, middle[2])
        keys, values, cum, doc, _, _ = [jnp.where(first, a, b) for a, b in zip(even, odd)]
        queries = own_ref[i, KV_ROWS:ROWS, :]
        cum_col, doc_col = column(cum), column(doc)
        inside = causal & (doc_col == doc)
        fading = jnp.exp(jnp.where(inside, cum_col - cum, 0.0))
        weights = jnp.where(inside, fading * dot(queries, keys) * SCALE, 0.0).astype(BF16)
        grown = jnp.exp(cum_col) * SCALE
        outside = jnp.where(doc_col == at_carry, grown * split_dot(queries, at_state), 0.0)
        partial_ref[i] = dot(weights, values) + outside
        weight_ref[i] = jnp.where(doc_col == start_doc, jnp.exp(cum_col + at_prefix) * SCALE, 0.0)
        mark_ref[i] = jnp.where(marked & (doc_col == number), 1.0, 0.0).astype(BF16)
        state, carry, prefix = advance(*middle, odd)
    state_ref[0:DH, :] = state
    row = lax.broadcasted_iota(jnp.int32, (8, TOK), 0)
    state_ref[DH : DH + 8, :] = jnp.where(row == 0, prefix, jnp.where(row == 1, carry, start_doc))


def enter_kernel(
    info_ref, own_ref, partial_ref, weight_ref, state_ref, near_ref, far_ref, linear_ref, square_ref, need_ref
):
    x = info_ref[0]
    near_decay, near_doc = near_ref[DH : DH + 1, :], near_ref[DH + 1 : DH + 2, :]
    far_doc, start_doc = far_ref[DH + 1 : DH + 2, :], state_ref[DH + 2 : DH + 3, :]
    keep = jnp.where((far_doc == near_doc) & (x >= 2), jnp.exp(near_decay), 0.0)
    state = near_ref[0:DH, :] + keep * far_ref[0:DH, :]
    state = jnp.where((start_doc == near_doc) & (x >= 1), state, 0.0)
    high = state.astype(BF16)
    low = (state - high.astype(F32)).astype(BF16)
    queries = jnp.concatenate([own_ref[i, KV_ROWS:ROWS, :] for i in range(HEADS)], axis=0)
    product = dot(queries, jnp.concatenate([high, low], axis=1))
    product = product[:, :DH] + product[:, DH:]
    eye = lax.broadcasted_iota(jnp.int32, (TOK, DH), 0) == lax.broadcasted_iota(jnp.int32, (TOK, DH), 1)
    for i in range(HEADS):
        linear = partial_ref[i] + weight_ref[i] * product[i * TOK : (i + 1) * TOK]
        linear_ref[i] = linear.astype(BF16)
        square = jnp.sum(linear * linear, axis=1, keepdims=True)
        square_ref[i : i + 1, :] = jnp.sum(jnp.where(eye, square, 0.0), axis=0, keepdims=True)
    for tile in range(TILES):
        tile_doc = jnp.broadcast_to(meta_rows(own_ref, 2 * tile)[3:4, :1], (1, TOK))
        need_ref[2 * tile] = jnp.where(x >= 1, jnp.max(jnp.where(tile_doc == near_doc, 1, 0)), 0)
        need_ref[2 * tile + 1] = jnp.where(x >= 2, jnp.max(jnp.where(tile_doc == far_doc, 1, 0)), 0)


def marked_queries(own_ref, mark_ref, tile):
    i = 2 * tile
    queries = jnp.concatenate([own_ref[i, KV_ROWS:ROWS, :], own_ref[i + 1, KV_ROWS:ROWS, :]], axis=0)
    marks = jnp.concatenate([mark_ref[i], mark_ref[i + 1]], axis=0)[:, :META]
    return jnp.concatenate([queries, marks], axis=1)


def absorb(queries, ref, pieces, diagonal, old):
    scores = []
    top = None
    for m in pieces:
        keys = jnp.concatenate([ref[2 * m, 0:VALUE_AT, :], ref[2 * m + 1, 0:VALUE_AT, :]], axis=1)
        score = dot(queries, keys)
        if m == diagonal[0]:
            score = jnp.where(diagonal[1], score, LOW)
        scores.append(score)
        most = jnp.maximum(score[:, :TOK], score[:, TOK:])
        top = most if top is None else jnp.maximum(top, most)
    top = jnp.max(top, axis=1, keepdims=True)
    if old is not None:
        top = jnp.maximum(top, old[0])
    base = top * EXP2_SCALE
    sums, output = None, None
    for m, score in zip(pieces, scores):
        weights = jnp.exp2(score * EXP2_SCALE - base)
        part = weights[:, :TOK] + weights[:, TOK:]
        sums = part if sums is None else sums + part
        values = jnp.concatenate([ref[2 * m, VALUE_AT:KV_ROWS, :], ref[2 * m + 1, VALUE_AT:KV_ROWS, :]], axis=0)
        product = dot(weights.astype(BF16), values)
        output = product if output is None else output + product
    total = jnp.sum(sums, axis=1, keepdims=True)
    if old is not None:
        shrink = jnp.exp2(old[0] * EXP2_SCALE - base)
        total = total + old[1] * shrink
        output = output + old[2] * shrink
    return top, total, output


def tile_places(core, own):
    rows = lax.broadcasted_iota(jnp.int32, (CHUNK, CHUNK), 0)
    lanes = lax.broadcasted_iota(jnp.int32, (CHUNK, CHUNK), 1)
    key_core = core if own else 1 - core
    at = jnp.where(rows < TOK, rows, rows + TOK) + core * TOK
    key = jnp.where(lanes < TOK, lanes, lanes + TOK) + key_core * TOK
    return at, key


def span_of(tile):
    return pl.ds(tile * CHUNK, CHUNK)


def load_part(refs, tile):
    top_ref, total_ref, output_ref = refs
    span = span_of(tile)
    return top_ref[span, :1], total_ref[span, :1], output_ref[span, :]


def store_part(refs, tile, part):
    span = span_of(tile)
    for ref, value in zip(refs, part):
        ref[span, :] = jnp.broadcast_to(value, (CHUNK, TOK))


def own_window_kernel(info_ref, own_ref, other_ref, mark_ref, *refs):
    core = info_ref[2]
    masks = []
    for own in (True, False):
        at, key = tile_places(core, own)
        masks.append(key <= at)
    for tile in range(TILES):
        queries = marked_queries(own_ref, mark_ref, tile)
        part = absorb(queries, own_ref, range(tile + 1), (tile, masks[0]), None)
        part = absorb(queries, other_ref, range(tile + 1), (tile, masks[1]), part)
        store_part(refs, tile, part)


def near_kernel(need_ref, own_ref, mark_ref, near_ref, other_ref, more_ref, a_ref, b_ref, c_ref, *refs):
    olds = (a_ref, b_ref, c_ref)
    for tile in range(TILES):
        needed = need_ref[2 * tile] == 1

        @pl.when(needed)
        def _(tile=tile):
            queries = marked_queries(own_ref, mark_ref, tile)
            part = absorb(queries, near_ref, range(TILES), (None, None), load_part(olds, tile))
            part = absorb(queries, other_ref, range(TILES // 2), (None, None), part)
            store_part(refs, tile, absorb(queries, more_ref, range(TILES // 2), (None, None), part))

        @pl.when(jnp.logical_not(needed))
        def _(tile=tile):
            store_part(refs, tile, load_part(olds, tile))


def far_blocks(core, own, own_ref, mark_ref, need_ref, far_ref, olds, refs):
    at, key = tile_places(core, own)
    mask = key > at
    for tile in range(TILES):
        needed = need_ref[2 * tile + 1] == 1

        @pl.when(needed)
        def _(tile=tile):
            queries = marked_queries(own_ref, mark_ref, tile)
            store_part(refs, tile, absorb(queries, far_ref, range(tile, TILES), (tile, mask), load_part(olds, tile)))

        @pl.when(jnp.logical_not(needed))
        def _(tile=tile):
            store_part(refs, tile, load_part(olds, tile))


def far_own_kernel(info_ref, need_ref, own_ref, mark_ref, far_ref, a_ref, b_ref, c_ref, *refs):
    far_blocks(info_ref[2], True, own_ref, mark_ref, need_ref, far_ref, (a_ref, b_ref, c_ref), refs)


def far_other_kernel(
    info_ref, need_ref, own_ref, mark_ref, far_ref, a_ref, b_ref, c_ref, linear_ref, square_ref, out_ref, *refs
):
    row = lax.broadcasted_iota(jnp.int32, (META, TOK), 0)
    for i in range(HEADS):
        out_ref[i, TOK : 2 * TOK, :] = linear_ref[i]
        meta = jnp.zeros((META, TOK), F32)
        for n, part in enumerate(split3(square_ref[i : i + 1, :])):
            meta = jnp.where(row == n, jnp.broadcast_to(part.astype(F32), (META, TOK)), meta)
        out_ref[i, 2 * TOK :, :] = meta.astype(BF16)
    far_blocks(info_ref[2], False, own_ref, mark_ref, need_ref, far_ref, (a_ref, b_ref, c_ref), refs)
    _, total_ref, output_ref = refs
    for i in range(HEADS):
        span = pl.ds(i * TOK, TOK)
        out_ref[i, 0:TOK, :] = (output_ref[span, :] / total_ref[span, :]).astype(BF16)


def finish_kernel(got_ref, gain_ref, out_ref):
    total = jnp.zeros((1, TOK), F32)
    for h in range(HEADS):
        total = total + joined(got_ref[h, 2 * TOK :, :], 0)
    inverse = column(lax.rsqrt(total / (HEAD_TOTAL * DH) + 1e-06))
    for h in range(HEADS):
        cols = pl.ds(h * DH, DH)
        linear = got_ref[h, TOK : 2 * TOK, :].astype(F32)
        window = got_ref[h, 0:TOK, :].astype(F32)
        out_ref[:, cols] = (gain_ref[:, cols] * linear * inverse + window).astype(BF16)


VMEM = pl.BlockSpec(memory_space=pltpu.VMEM)
SMEM = pl.BlockSpec(memory_space=pltpu.SMEM)
HBM = pl.BlockSpec(memory_space=pltpu.HBM)


LIMIT = {"prepare": 58}


def call(kernel, name, specs, shapes, scratch=(), outs=None):
    many = isinstance(shapes, (list, tuple))
    return pl.pallas_call(
        kernel,
        name=name,
        out_shape=shapes,
        in_specs=specs,
        out_specs=outs or ([VMEM] * len(shapes) if many else VMEM),
        scratch_shapes=list(scratch),
        compiler_params=pltpu.CompilerParams(vmem_limit_bytes=LIMIT.get(name, 16) * 2**20),
        cost_estimate=pl.CostEstimate(flops=0, bytes_accessed=0, transcendentals=0),
    )


def body(queries, keys, values, init_state, lin_gain, rate_table, rate_index, speed, drop, doc_id):
    x, z, core = (lax.axis_index(a).astype(jnp.int32) for a in ("x", "z", "core"))
    info = jnp.stack([x, z, core])
    shape = jax.ShapeDtypeStruct
    packed = call(
        prepare_kernel,
        "prepare",
        [SMEM, SMEM, HBM, HBM, HBM, VMEM, VMEM, VMEM],
        shape((HEADS, ROWS, TOK), BF16),
        scratch=[pltpu.VMEM((TOK, HEADS * DH), BF16)] * 3 + [pltpu.SemaphoreType.DMA((3,))],
    )(rate_table, rate_index, queries, keys, values, speed.T, drop.T, doc_id[None, :])
    own = lax.all_to_all(packed, "z", 0, 0, tiled=True)
    sent = own[:, :KV_ROWS]
    pair = [(0, 1), (1, 0)]
    near = lax.ppermute(sent, "x", [(0, 1), (1, 2), (2, 3)])
    other = lax.ppermute(sent, "core", pair)

    tokens = HEADS * TOK
    part_shapes = [shape((tokens, TOK), F32), shape((tokens, TOK), F32), shape((tokens, DH), F32)]
    init = lax.dynamic_slice_in_dim(init_state, z, 1, 0)
    partial, weight, state, mark = call(
        linear_kernel,
        "linear",
        [SMEM] + [VMEM] * 3,
        [
            shape((HEADS, TOK, DH), F32),
            shape((HEADS, TOK, DH), F32),
            shape((DH + 8, DH), F32),
            shape((HEADS, TOK, TOK), BF16),
        ],
    )(info, own, other, init)
    near_state = lax.ppermute(state, "x", [(0, 1), (1, 2), (2, 3)])
    far_state = lax.ppermute(state, "x", [(0, 2), (1, 3)])
    own_part = call(
        own_window_kernel, "own_window", [SMEM] + [VMEM] * 3, part_shapes
    )(info, own, other, mark)
    sent, own_part = lax.optimization_barrier((sent, own_part))
    far = lax.ppermute(sent, "x", [(0, 2), (1, 3)])
    near_state, far_state, own_part = lax.optimization_barrier((near_state, far_state, own_part))
    linear, square, need = call(
        enter_kernel,
        "enter",
        [SMEM] + [VMEM] * 6,
        [shape((HEADS, TOK, DH), BF16), shape((HEADS, TOK), F32), shape((2 * TILES,), jnp.int32)],
        outs=[VMEM, VMEM, SMEM],
    )(info, own, partial, weight, state, near_state, far_state)
    square = square + lax.ppermute(square, "head", [(i, i ^ 1) for i in range(4)])
    near, own_part = lax.optimization_barrier((near, own_part))
    near_other = [lax.ppermute(near[at : at + TILES], "core", pair) for at in (0, TILES)]
    part = call(near_kernel, "near_window", [SMEM] + [VMEM] * 8, part_shapes)(
        need, own, mark, near, *near_other, *own_part
    )
    far, part, square = lax.optimization_barrier((far, part, square))
    square = square + lax.ppermute(square, "head", [(i, i ^ 2) for i in range(4)])
    far_other = lax.ppermute(far, "core", pair)
    part = call(far_own_kernel, "far_own", [SMEM] * 2 + [VMEM] * 6, part_shapes)(info, need, own, mark, far, *part)
    mixed = call(
        far_other_kernel,
        "far_other",
        [SMEM] * 2 + [VMEM] * 8,
        shape((HEADS, 2 * TOK + META, DH), BF16),
        scratch=[pltpu.VMEM((tokens, TOK), F32)] * 3,
    )(info, need, own, mark, far_other, *part, linear, square)
    back = lax.all_to_all(mixed, "z", 0, 0, tiled=True)
    return call(finish_kernel, "finish", [VMEM] * 2, shape((TOK, HEADS * DH), BF16))(
        back, lin_gain[None, :]
    )


def solution(mesh):
    split = Mesh(mesh.devices.reshape(4, 8, 2, 4), ("x", "z", "core", "head"))
    ctx = ("x", "z", "core")
    placed = (
        P(ctx, "head"),
        P(ctx, "head"),
        P(ctx, "head"),
        P("head", None, None),
        P("head"),
        P(),
        P("head"),
        P(ctx, "head"),
        P(ctx, "head"),
        P(ctx),
    )
    return jax.shard_map(body, mesh=split, in_specs=placed, out_specs=P(ctx, "head"), check_vma=False)
```

```python
import math

import jax
import jax.numpy as jnp
from jax import lax
from jax.experimental import pallas as pl
from jax.experimental.pallas import tpu as pltpu
from jax.sharding import Mesh
from jax.sharding import PartitionSpec as P

HEAD_TOTAL = 32
DH = 128
TOK = 128
WINDOW = 4096
HEADS = 8
META = 16
KV_ROWS = 2 * DH + META
ROWS = KV_ROWS + TOK
PLANE = 2 * HEADS * TOK
SCALE = 1.0 / math.sqrt(DH)
EXP2_SCALE = SCALE / math.log(2.0)
LOW = -1e30
F32 = jnp.float32
BF16 = jnp.bfloat16
CHUNK = 2 * TOK
TILES = HEADS // 2
META_AT = DH
VALUE_AT = DH + META


def dot(a, b):
    return jnp.dot(a, b, preferred_element_type=F32)


def split3(x):
    high = x.astype(BF16)
    rest = x - high.astype(F32)
    mid = rest.astype(BF16)
    low = (rest - mid.astype(F32)).astype(BF16)
    return high, mid, low


def joined(rows, at):
    part = rows.astype(F32)
    return part[at : at + 1] + part[at + 1 : at + 2] + part[at + 2 : at + 3]


def column(row):
    return jnp.transpose(jnp.broadcast_to(row, (TOK, TOK)))


def split_dot(a, state):
    high = state.astype(BF16)
    low = (state - high.astype(F32)).astype(BF16)
    return dot(a, high) + dot(a, low)


def prepare_kernel(
    table_ref, index_ref, q_hbm, k_hbm, v_hbm, speed_ref, drop_ref, doc_ref, out_ref, q_ref, k_ref, v_ref, sems
):
    copies = [
        pltpu.make_async_copy(src, dst, sems.at[n])
        for n, (src, dst) in enumerate(((k_hbm, k_ref), (v_hbm, v_ref), (q_hbm, q_ref)))
    ]
    for copy in copies:
        copy.start()
    head = lax.broadcasted_iota(jnp.int32, (HEADS, TOK), 0)
    rate = jnp.zeros((HEADS, TOK), F32)
    for h in range(HEADS):
        rate = jnp.where(head == h, table_ref[index_ref[h]], rate)
    log_decay = -rate * speed_ref[...] - drop_ref[...]
    upto = (
        lax.broadcasted_iota(jnp.int32, (TOK, TOK), 0)
        <= lax.broadcasted_iota(jnp.int32, (TOK, TOK), 1)
    ).astype(F32)
    cum = jnp.dot(log_decay, upto, precision=lax.Precision.HIGHEST, preferred_element_type=F32)
    parts = [part.astype(F32) for part in split3(cum)]
    row = lax.broadcasted_iota(jnp.int32, (META, TOK), 0)
    doc = jnp.broadcast_to(doc_ref[...].astype(F32), (META, TOK))
    bias = jnp.where(doc == (row - 4).astype(F32), 0.0, LOW)
    shared = jnp.where(row == 3, doc, jnp.where((row >= 4) & (row < 8), bias, 0.0))
    for h in range(HEADS):
        meta = shared
        for n, part in enumerate(parts):
            meta = jnp.where(row == n, jnp.broadcast_to(part[h : h + 1], (META, TOK)), meta)
        out_ref[h, META_AT:VALUE_AT, :] = meta.astype(BF16)
    copies[0].wait()
    for h in range(HEADS):
        out_ref[h, 0:DH, :] = jnp.transpose(k_ref[:, pl.ds(h * DH, DH)])
    copies[1].wait()
    copies[2].wait()
    for h in range(HEADS):
        cols = pl.ds(h * DH, DH)
        out_ref[h, VALUE_AT:KV_ROWS, :] = v_ref[:, cols]
        out_ref[h, KV_ROWS:ROWS, :] = q_ref[:, cols]


def meta_rows(ref, i):
    return ref[i, META_AT:VALUE_AT, :].astype(F32)


def linear_kernel(info_ref, own_ref, other_ref, init_ref, partial_ref, weight_ref, state_ref, mark_ref):
    x, core = info_ref[0], info_ref[2]
    first = core == 0
    state = jnp.where(x == 0, init_ref[0], 0.0)
    carry = jnp.where(x == 0, jnp.zeros((1, TOK), F32), jnp.full((1, TOK), -1.0, F32))
    prefix = jnp.zeros((1, TOK), F32)
    places = lax.broadcasted_iota(jnp.int32, (TOK, TOK), 0)
    lanes = lax.broadcasted_iota(jnp.int32, (TOK, TOK), 1)
    causal = places >= lanes
    marked = (lanes >= 4) & (lanes < 8)
    number = (lanes - 4).astype(F32)
    start_doc = None

    def read(swap, i):
        mine, theirs = own_ref[i, 0:KV_ROWS, :], other_ref[i]
        got = jnp.where(swap, theirs, mine)
        rows = got[META_AT:VALUE_AT].astype(F32)
        cum, doc = rows[0:1] + rows[1:2] + rows[2:3], rows[3:4]
        overall = jnp.broadcast_to(cum[:, TOK - 1 :], (1, TOK))
        last = jnp.broadcast_to(doc[:, TOK - 1 :], (1, TOK))
        return got[:DH], got[VALUE_AT:], cum, doc, overall, last

    def advance(state, carry, prefix, block):
        keys, values, cum, doc, overall, last = block
        factor = jnp.where(doc == last, jnp.exp(overall - cum), 0.0)
        scaled = (keys.astype(F32) * factor).astype(BF16)
        keep = jnp.where(last == carry, jnp.exp(overall), 0.0)
        return dot(scaled, values) + keep * state, last, prefix + overall

    for i in range(HEADS):
        even = read(jnp.logical_not(first), i)
        odd = read(first, i)
        if start_doc is None:
            start_doc = jnp.broadcast_to(even[3][:, :1], (1, TOK))
        middle = advance(state, carry, prefix, even)
        at_state = jnp.where(first, state, middle[0])
        at_carry = jnp.where(first, carry, middle[1])
        at_prefix = jnp.where(first, prefix, middle[2])
        keys, values, cum, doc, _, _ = [jnp.where(first, a, b) for a, b in zip(even, odd)]
        queries = own_ref[i, KV_ROWS:ROWS, :]
        cum_col, doc_col = column(cum), column(doc)
        inside = causal & (doc_col == doc)
        fading = jnp.exp(jnp.where(inside, cum_col - cum, 0.0))
        weights = jnp.where(inside, fading * dot(queries, keys) * SCALE, 0.0).astype(BF16)
        grown = jnp.exp(cum_col) * SCALE
        outside = jnp.where(doc_col == at_carry, grown * split_dot(queries, at_state), 0.0)
        partial_ref[i] = dot(weights, values) + outside
        weight_ref[i] = jnp.where(doc_col == start_doc, jnp.exp(cum_col + at_prefix) * SCALE, 0.0)
        mark_ref[i] = jnp.where(marked & (doc_col == number), 1.0, 0.0).astype(BF16)
        state, carry, prefix = advance(*middle, odd)
    state_ref[0:DH, :] = state
    row = lax.broadcasted_iota(jnp.int32, (8, TOK), 0)
    state_ref[DH : DH + 8, :] = jnp.where(row == 0, prefix, jnp.where(row == 1, carry, start_doc))


def enter_kernel(
    info_ref, own_ref, partial_ref, weight_ref, state_ref, near_ref, far_ref, linear_ref, square_ref, need_ref
):
    x = info_ref[0]
    near_decay, near_doc = near_ref[DH : DH + 1, :], near_ref[DH + 1 : DH + 2, :]
    far_doc, start_doc = far_ref[DH + 1 : DH + 2, :], state_ref[DH + 2 : DH + 3, :]
    keep = jnp.where((far_doc == near_doc) & (x >= 2), jnp.exp(near_decay), 0.0)
    state = near_ref[0:DH, :] + keep * far_ref[0:DH, :]
    state = jnp.where((start_doc == near_doc) & (x >= 1), state, 0.0)
    high = state.astype(BF16)
    low = (state - high.astype(F32)).astype(BF16)
    queries = jnp.concatenate([own_ref[i, KV_ROWS:ROWS, :] for i in range(HEADS)], axis=0)
    product = dot(queries, jnp.concatenate([high, low], axis=1))
    product = product[:, :DH] + product[:, DH:]
    eye = lax.broadcasted_iota(jnp.int32, (TOK, DH), 0) == lax.broadcasted_iota(jnp.int32, (TOK, DH), 1)
    for i in range(HEADS):
        linear = partial_ref[i] + weight_ref[i] * product[i * TOK : (i + 1) * TOK]
        linear_ref[i] = linear.astype(BF16)
        square = jnp.sum(linear * linear, axis=1, keepdims=True)
        square_ref[i : i + 1, :] = jnp.sum(jnp.where(eye, square, 0.0), axis=0, keepdims=True)
    for tile in range(TILES):
        tile_doc = jnp.broadcast_to(meta_rows(own_ref, 2 * tile)[3:4, :1], (1, TOK))
        need_ref[2 * tile] = jnp.where(x >= 1, jnp.max(jnp.where(tile_doc == near_doc, 1, 0)), 0)
        need_ref[2 * tile + 1] = jnp.where(x >= 2, jnp.max(jnp.where(tile_doc == far_doc, 1, 0)), 0)


def marked_queries(own_ref, mark_ref, tile):
    i = 2 * tile
    queries = jnp.concatenate([own_ref[i, KV_ROWS:ROWS, :], own_ref[i + 1, KV_ROWS:ROWS, :]], axis=0)
    marks = jnp.concatenate([mark_ref[i], mark_ref[i + 1]], axis=0)[:, :META]
    return jnp.concatenate([queries, marks], axis=1)


def absorb(queries, pieces, old):
    scores = []
    top = None
    for ref, m, mask in pieces:
        keys = jnp.concatenate([ref[2 * m, 0:VALUE_AT, :], ref[2 * m + 1, 0:VALUE_AT, :]], axis=1)
        score = dot(queries, keys)
        if mask is not None:
            score = jnp.where(mask, score, LOW)
        scores.append(score)
        most = jnp.maximum(score[:, :TOK], score[:, TOK:])
        top = most if top is None else jnp.maximum(top, most)
    top = jnp.max(top, axis=1, keepdims=True)
    if old is not None:
        top = jnp.maximum(top, old[0])
    base = top * EXP2_SCALE
    sums, output = None, None
    for (ref, m, _), score in zip(pieces, scores):
        weights = jnp.exp2(score * EXP2_SCALE - base)
        part = weights[:, :TOK] + weights[:, TOK:]
        sums = part if sums is None else sums + part
        values = jnp.concatenate([ref[2 * m, VALUE_AT:KV_ROWS, :], ref[2 * m + 1, VALUE_AT:KV_ROWS, :]], axis=0)
        product = dot(weights.astype(BF16), values)
        output = product if output is None else output + product
    total = jnp.sum(sums, axis=1, keepdims=True)
    if old is not None:
        shrink = jnp.exp2(old[0] * EXP2_SCALE - base)
        total = total + old[1] * shrink
        output = output + old[2] * shrink
    return top, total, output


def tile_places(core, own):
    rows = lax.broadcasted_iota(jnp.int32, (CHUNK, CHUNK), 0)
    lanes = lax.broadcasted_iota(jnp.int32, (CHUNK, CHUNK), 1)
    key_core = core if own else 1 - core
    at = jnp.where(rows < TOK, rows, rows + TOK) + core * TOK
    key = jnp.where(lanes < TOK, lanes, lanes + TOK) + key_core * TOK
    return at, key


def span_of(tile):
    return pl.ds(tile * CHUNK, CHUNK)


def load_part(refs, tile):
    top_ref, total_ref, output_ref = refs
    span = span_of(tile)
    return top_ref[span, :1], total_ref[span, :1], output_ref[span, :]


def store_part(refs, tile, part):
    span = span_of(tile)
    for ref, value in zip(refs, part):
        ref[span, :] = jnp.broadcast_to(value, (CHUNK, TOK))


def own_window_kernel(info_ref, own_ref, other_ref, mark_ref, *refs):
    core = info_ref[2]
    masks = []
    for own in (True, False):
        at, key = tile_places(core, own)
        masks.append(key <= at)
    for tile in range(TILES):
        queries = marked_queries(own_ref, mark_ref, tile)
        pieces = [
            (ref, m, mask if m == tile else None)
            for ref, mask in zip((own_ref, other_ref), masks)
            for m in range(tile + 1)
        ]
        store_part(refs, tile, absorb(queries, pieces, None))


def near_kernel(need_ref, own_ref, mark_ref, near_ref, other_ref, more_ref, a_ref, b_ref, c_ref, *refs):
    olds = (a_ref, b_ref, c_ref)
    for tile in range(TILES):
        needed = need_ref[2 * tile] == 1

        @pl.when(needed)
        def _(tile=tile):
            queries = marked_queries(own_ref, mark_ref, tile)
            pieces = [(near_ref, m, None) for m in range(TILES)]
            pieces += [(ref, m, None) for ref in (other_ref, more_ref) for m in range(TILES // 2)]
            store_part(refs, tile, absorb(queries, pieces, load_part(olds, tile)))

        @pl.when(jnp.logical_not(needed))
        def _(tile=tile):
            store_part(refs, tile, load_part(olds, tile))


def far_blocks(core, own, own_ref, mark_ref, need_ref, far_ref, olds, refs):
    at, key = tile_places(core, own)
    mask = key > at
    for tile in range(TILES):
        needed = need_ref[2 * tile + 1] == 1

        @pl.when(needed)
        def _(tile=tile):
            queries = marked_queries(own_ref, mark_ref, tile)
            pieces = [(far_ref, m, mask if m == tile else None) for m in range(tile, TILES)]
            store_part(refs, tile, absorb(queries, pieces, load_part(olds, tile)))

        @pl.when(jnp.logical_not(needed))
        def _(tile=tile):
            store_part(refs, tile, load_part(olds, tile))


def far_own_kernel(info_ref, need_ref, own_ref, mark_ref, far_ref, a_ref, b_ref, c_ref, *refs):
    far_blocks(info_ref[2], True, own_ref, mark_ref, need_ref, far_ref, (a_ref, b_ref, c_ref), refs)


def far_other_kernel(
    info_ref, need_ref, own_ref, mark_ref, far_ref, a_ref, b_ref, c_ref, linear_ref, square_ref, out_ref, *refs
):
    row = lax.broadcasted_iota(jnp.int32, (META, TOK), 0)
    for i in range(HEADS):
        out_ref[i, TOK : 2 * TOK, :] = linear_ref[i]
        meta = jnp.zeros((META, TOK), F32)
        for n, part in enumerate(split3(square_ref[i : i + 1, :])):
            meta = jnp.where(row == n, jnp.broadcast_to(part.astype(F32), (META, TOK)), meta)
        out_ref[i, 2 * TOK :, :] = meta.astype(BF16)
    far_blocks(info_ref[2], False, own_ref, mark_ref, need_ref, far_ref, (a_ref, b_ref, c_ref), refs)
    _, total_ref, output_ref = refs
    for i in range(HEADS):
        span = pl.ds(i * TOK, TOK)
        out_ref[i, 0:TOK, :] = (output_ref[span, :] / total_ref[span, :]).astype(BF16)


def finish_kernel(got_ref, gain_ref, out_ref):
    total = jnp.zeros((1, TOK), F32)
    for h in range(HEADS):
        total = total + joined(got_ref[h, 2 * TOK :, :], 0)
    inverse = column(lax.rsqrt(total / (HEAD_TOTAL * DH) + 1e-06))
    for h in range(HEADS):
        cols = pl.ds(h * DH, DH)
        linear = got_ref[h, TOK : 2 * TOK, :].astype(F32)
        window = got_ref[h, 0:TOK, :].astype(F32)
        out_ref[:, cols] = (gain_ref[:, cols] * linear * inverse + window).astype(BF16)


VMEM = pl.BlockSpec(memory_space=pltpu.VMEM)
SMEM = pl.BlockSpec(memory_space=pltpu.SMEM)
HBM = pl.BlockSpec(memory_space=pltpu.HBM)


LIMIT = {"prepare": 58}


def call(kernel, name, specs, shapes, scratch=(), outs=None):
    many = isinstance(shapes, (list, tuple))
    return pl.pallas_call(
        kernel,
        name=name,
        out_shape=shapes,
        in_specs=specs,
        out_specs=outs or ([VMEM] * len(shapes) if many else VMEM),
        scratch_shapes=list(scratch),
        compiler_params=pltpu.CompilerParams(vmem_limit_bytes=LIMIT.get(name, 16) * 2**20),
        cost_estimate=pl.CostEstimate(flops=0, bytes_accessed=0, transcendentals=0),
    )


def body(queries, keys, values, init_state, lin_gain, rate_table, rate_index, speed, drop, doc_id):
    x, z, core = (lax.axis_index(a).astype(jnp.int32) for a in ("x", "z", "core"))
    info = jnp.stack([x, z, core])
    shape = jax.ShapeDtypeStruct
    packed = call(
        prepare_kernel,
        "prepare",
        [SMEM, SMEM, HBM, HBM, HBM, VMEM, VMEM, VMEM],
        shape((HEADS, ROWS, TOK), BF16),
        scratch=[pltpu.VMEM((TOK, HEADS * DH), BF16)] * 3 + [pltpu.SemaphoreType.DMA((3,))],
    )(rate_table, rate_index, queries, keys, values, speed.T, drop.T, doc_id[None, :])
    own = lax.all_to_all(packed, "z", 0, 0, tiled=True)
    sent = own[:, :KV_ROWS]
    pair = [(0, 1), (1, 0)]
    near = lax.ppermute(sent, "x", [(0, 1), (1, 2), (2, 3)])
    other = lax.ppermute(sent, "core", pair)

    tokens = HEADS * TOK
    part_shapes = [shape((tokens, TOK), F32), shape((tokens, TOK), F32), shape((tokens, DH), F32)]
    init = lax.dynamic_slice_in_dim(init_state, z, 1, 0)
    partial, weight, state, mark = call(
        linear_kernel,
        "linear",
        [SMEM] + [VMEM] * 3,
        [
            shape((HEADS, TOK, DH), F32),
            shape((HEADS, TOK, DH), F32),
            shape((DH + 8, DH), F32),
            shape((HEADS, TOK, TOK), BF16),
        ],
    )(info, own, other, init)
    near_state = lax.ppermute(state, "x", [(0, 1), (1, 2), (2, 3)])
    far_state = lax.ppermute(state, "x", [(0, 2), (1, 3)])
    own_part = call(
        own_window_kernel, "own_window", [SMEM] + [VMEM] * 3, part_shapes
    )(info, own, other, mark)
    sent, own_part = lax.optimization_barrier((sent, own_part))
    far = lax.ppermute(sent, "x", [(0, 2), (1, 3)])
    near_state, far_state, own_part = lax.optimization_barrier((near_state, far_state, own_part))
    linear, square, need = call(
        enter_kernel,
        "enter",
        [SMEM] + [VMEM] * 6,
        [shape((HEADS, TOK, DH), BF16), shape((HEADS, TOK), F32), shape((2 * TILES,), jnp.int32)],
        outs=[VMEM, VMEM, SMEM],
    )(info, own, partial, weight, state, near_state, far_state)
    square = square + lax.ppermute(square, "head", [(i, i ^ 1) for i in range(4)])
    near, own_part = lax.optimization_barrier((near, own_part))
    near_other = [lax.ppermute(near[at : at + TILES], "core", pair) for at in (0, TILES)]
    part = call(near_kernel, "near_window", [SMEM] + [VMEM] * 8, part_shapes)(
        need, own, mark, near, *near_other, *own_part
    )
    far, part, square = lax.optimization_barrier((far, part, square))
    square = square + lax.ppermute(square, "head", [(i, 3 - i) for i in range(4)])
    far_other = lax.ppermute(far, "core", pair)
    part = call(far_own_kernel, "far_own", [SMEM] * 2 + [VMEM] * 6, part_shapes)(info, need, own, mark, far, *part)
    mixed = call(
        far_other_kernel,
        "far_other",
        [SMEM] * 2 + [VMEM] * 8,
        shape((HEADS, 2 * TOK + META, DH), BF16),
        scratch=[pltpu.VMEM((tokens, TOK), F32)] * 3,
    )(info, need, own, mark, far_other, *part, linear, square)
    back = lax.all_to_all(mixed, "z", 0, 0, tiled=True)
    return call(finish_kernel, "finish", [VMEM] * 2, shape((TOK, HEADS * DH), BF16))(
        back, lin_gain[None, :]
    )


def solution(mesh):
    split = Mesh(mesh.devices.reshape(4, 8, 2, 4), ("x", "z", "core", "head"))
    ctx = ("x", "z", "core")
    placed = (
        P(ctx, "head"),
        P(ctx, "head"),
        P(ctx, "head"),
        P("head", None, None),
        P("head"),
        P(),
        P("head"),
        P(ctx, "head"),
        P(ctx, "head"),
        P(ctx),
    )
    return jax.shard_map(body, mesh=split, in_specs=placed, out_specs=P(ctx, "head"), check_vma=False)
```

```python
import math

import jax
import jax.numpy as jnp
from jax import lax
from jax.experimental import pallas as pl
from jax.experimental.pallas import tpu as pltpu
from jax.sharding import Mesh
from jax.sharding import PartitionSpec as P

HEAD_TOTAL = 32
DH = 128
TOK = 128
WINDOW = 4096
HEADS = 8
META = 16
KV_ROWS = 2 * DH + META
ROWS = KV_ROWS + TOK
PLANE = 2 * HEADS * TOK
SCALE = 1.0 / math.sqrt(DH)
EXP2_SCALE = SCALE / math.log(2.0)
LOW = -1e30
F32 = jnp.float32
BF16 = jnp.bfloat16
CHUNK = 2 * TOK
TILES = HEADS // 2
META_AT = DH
VALUE_AT = DH + META


def dot(a, b):
    return jnp.dot(a, b, preferred_element_type=F32)


def split3(x):
    high = x.astype(BF16)
    rest = x - high.astype(F32)
    mid = rest.astype(BF16)
    low = (rest - mid.astype(F32)).astype(BF16)
    return high, mid, low


def joined(rows, at):
    part = rows.astype(F32)
    return part[at : at + 1] + part[at + 1 : at + 2] + part[at + 2 : at + 3]


def column(row):
    return jnp.transpose(jnp.broadcast_to(row, (TOK, TOK)))


def split_dot(a, state):
    high = state.astype(BF16)
    low = (state - high.astype(F32)).astype(BF16)
    return dot(a, high) + dot(a, low)


def prepare_kernel(
    table_ref, index_ref, q_hbm, k_hbm, v_hbm, speed_ref, drop_ref, doc_ref, out_ref, q_ref, k_ref, v_ref, sems
):
    copies = [
        pltpu.make_async_copy(src, dst, sems.at[n])
        for n, (src, dst) in enumerate(((k_hbm, k_ref), (v_hbm, v_ref), (q_hbm, q_ref)))
    ]
    for copy in copies:
        copy.start()
    head = lax.broadcasted_iota(jnp.int32, (HEADS, TOK), 0)
    rate = jnp.zeros((HEADS, TOK), F32)
    for h in range(HEADS):
        rate = jnp.where(head == h, table_ref[index_ref[h]], rate)
    log_decay = -rate * speed_ref[...] - drop_ref[...]
    upto = (
        lax.broadcasted_iota(jnp.int32, (TOK, TOK), 0)
        <= lax.broadcasted_iota(jnp.int32, (TOK, TOK), 1)
    ).astype(F32)
    cum = jnp.dot(log_decay, upto, precision=lax.Precision.HIGHEST, preferred_element_type=F32)
    parts = [part.astype(F32) for part in split3(cum)]
    row = lax.broadcasted_iota(jnp.int32, (META, TOK), 0)
    doc = jnp.broadcast_to(doc_ref[...].astype(F32), (META, TOK))
    bias = jnp.where(doc == (row - 4).astype(F32), 0.0, LOW)
    shared = jnp.where(row == 3, doc, jnp.where((row >= 4) & (row < 8), bias, 0.0))
    for h in range(HEADS):
        meta = shared
        for n, part in enumerate(parts):
            meta = jnp.where(row == n, jnp.broadcast_to(part[h : h + 1], (META, TOK)), meta)
        out_ref[h, META_AT:VALUE_AT, :] = meta.astype(BF16)
    copies[0].wait()
    for h in range(HEADS):
        out_ref[h, 0:DH, :] = jnp.transpose(k_ref[:, pl.ds(h * DH, DH)])
    copies[1].wait()
    copies[2].wait()
    for h in range(HEADS):
        cols = pl.ds(h * DH, DH)
        out_ref[h, VALUE_AT:KV_ROWS, :] = v_ref[:, cols]
        out_ref[h, KV_ROWS:ROWS, :] = q_ref[:, cols]


def meta_rows(ref, i):
    return ref[i, META_AT:VALUE_AT, :].astype(F32)


def linear_kernel(info_ref, own_ref, other_ref, init_ref, partial_ref, weight_ref, state_ref, mark_ref):
    x, core = info_ref[0], info_ref[2]
    first = core == 0
    state = jnp.where(x == 0, init_ref[0], 0.0)
    carry = jnp.where(x == 0, jnp.zeros((1, TOK), F32), jnp.full((1, TOK), -1.0, F32))
    prefix = jnp.zeros((1, TOK), F32)
    places = lax.broadcasted_iota(jnp.int32, (TOK, TOK), 0)
    lanes = lax.broadcasted_iota(jnp.int32, (TOK, TOK), 1)
    causal = places >= lanes
    marked = (lanes >= 4) & (lanes < 8)
    number = (lanes - 4).astype(F32)
    start_doc = None

    def read(swap, i):
        mine, theirs = own_ref[i, 0:KV_ROWS, :], other_ref[i]
        got = jnp.where(swap, theirs, mine)
        rows = got[META_AT:VALUE_AT].astype(F32)
        cum, doc = rows[0:1] + rows[1:2] + rows[2:3], rows[3:4]
        overall = jnp.broadcast_to(cum[:, TOK - 1 :], (1, TOK))
        last = jnp.broadcast_to(doc[:, TOK - 1 :], (1, TOK))
        return got[:DH], got[VALUE_AT:], cum, doc, overall, last

    def advance(state, carry, prefix, block):
        keys, values, cum, doc, overall, last = block
        factor = jnp.where(doc == last, jnp.exp(overall - cum), 0.0)
        scaled = (keys.astype(F32) * factor).astype(BF16)
        keep = jnp.where(last == carry, jnp.exp(overall), 0.0)
        return dot(scaled, values) + keep * state, last, prefix + overall

    for i in range(HEADS):
        even = read(jnp.logical_not(first), i)
        odd = read(first, i)
        if start_doc is None:
            start_doc = jnp.broadcast_to(even[3][:, :1], (1, TOK))
        middle = advance(state, carry, prefix, even)
        at_state = jnp.where(first, state, middle[0])
        at_carry = jnp.where(first, carry, middle[1])
        at_prefix = jnp.where(first, prefix, middle[2])
        keys, values, cum, doc, _, _ = [jnp.where(first, a, b) for a, b in zip(even, odd)]
        queries = own_ref[i, KV_ROWS:ROWS, :]
        cum_col, doc_col = column(cum), column(doc)
        inside = causal & (doc_col == doc)
        fading = jnp.exp(jnp.where(inside, cum_col - cum, 0.0))
        weights = jnp.where(inside, fading * dot(queries, keys) * SCALE, 0.0).astype(BF16)
        grown = jnp.exp(cum_col) * SCALE
        outside = jnp.where(doc_col == at_carry, grown * split_dot(queries, at_state), 0.0)
        partial_ref[i] = dot(weights, values) + outside
        weight_ref[i] = jnp.where(doc_col == start_doc, jnp.exp(cum_col + at_prefix) * SCALE, 0.0)
        mark_ref[i] = jnp.where(marked & (doc_col == number), 1.0, 0.0).astype(BF16)
        state, carry, prefix = advance(*middle, odd)
    state_ref[0:DH, :] = state
    row = lax.broadcasted_iota(jnp.int32, (8, TOK), 0)
    state_ref[DH : DH + 8, :] = jnp.where(row == 0, prefix, jnp.where(row == 1, carry, start_doc))


def enter_kernel(
    info_ref, own_ref, partial_ref, weight_ref, state_ref, near_ref, far_ref, linear_ref, square_ref, need_ref
):
    x = info_ref[0]
    near_decay, near_doc = near_ref[DH : DH + 1, :], near_ref[DH + 1 : DH + 2, :]
    far_doc, start_doc = far_ref[DH + 1 : DH + 2, :], state_ref[DH + 2 : DH + 3, :]
    keep = jnp.where((far_doc == near_doc) & (x >= 2), jnp.exp(near_decay), 0.0)
    state = near_ref[0:DH, :] + keep * far_ref[0:DH, :]
    state = jnp.where((start_doc == near_doc) & (x >= 1), state, 0.0)
    high = state.astype(BF16)
    low = (state - high.astype(F32)).astype(BF16)
    queries = jnp.concatenate([own_ref[i, KV_ROWS:ROWS, :] for i in range(HEADS)], axis=0)
    product = dot(queries, jnp.concatenate([high, low], axis=1))
    product = product[:, :DH] + product[:, DH:]
    eye = lax.broadcasted_iota(jnp.int32, (TOK, DH), 0) == lax.broadcasted_iota(jnp.int32, (TOK, DH), 1)
    for i in range(HEADS):
        linear = partial_ref[i] + weight_ref[i] * product[i * TOK : (i + 1) * TOK]
        linear_ref[i] = linear.astype(BF16)
        square = jnp.sum(linear * linear, axis=1, keepdims=True)
        square_ref[i : i + 1, :] = jnp.sum(jnp.where(eye, square, 0.0), axis=0, keepdims=True)
    for tile in range(TILES):
        tile_doc = jnp.broadcast_to(meta_rows(own_ref, 2 * tile)[3:4, :1], (1, TOK))
        need_ref[2 * tile] = jnp.where(x >= 1, jnp.max(jnp.where(tile_doc == near_doc, 1, 0)), 0)
        need_ref[2 * tile + 1] = jnp.where(x >= 2, jnp.max(jnp.where(tile_doc == far_doc, 1, 0)), 0)


def marked_queries(own_ref, mark_ref, tile):
    i = 2 * tile
    queries = jnp.concatenate([own_ref[i, KV_ROWS:ROWS, :], own_ref[i + 1, KV_ROWS:ROWS, :]], axis=0)
    marks = jnp.concatenate([mark_ref[i], mark_ref[i + 1]], axis=0)[:, :META]
    return jnp.concatenate([queries, marks], axis=1)


def absorb(queries, pieces, old):
    scores = []
    top = None
    for ref, m, mask in pieces:
        keys = jnp.concatenate([ref[2 * m, 0:VALUE_AT, :], ref[2 * m + 1, 0:VALUE_AT, :]], axis=1)
        score = dot(queries, keys)
        if mask is not None:
            score = jnp.where(mask, score, LOW)
        scores.append(score)
        most = jnp.maximum(score[:, :TOK], score[:, TOK:])
        top = most if top is None else jnp.maximum(top, most)
    top = jnp.max(top, axis=1, keepdims=True)
    if old is not None:
        top = jnp.maximum(top, old[0])
    base = top * EXP2_SCALE
    sums, output = None, None
    for (ref, m, _), score in zip(pieces, scores):
        weights = jnp.exp2(score * EXP2_SCALE - base)
        part = weights[:, :TOK] + weights[:, TOK:]
        sums = part if sums is None else sums + part
        values = jnp.concatenate([ref[2 * m, VALUE_AT:KV_ROWS, :], ref[2 * m + 1, VALUE_AT:KV_ROWS, :]], axis=0)
        product = dot(weights.astype(BF16), values)
        output = product if output is None else output + product
    total = jnp.sum(sums, axis=1, keepdims=True)
    if old is not None:
        shrink = jnp.exp2(old[0] * EXP2_SCALE - base)
        total = total + old[1] * shrink
        output = output + old[2] * shrink
    return top, total, output


def tile_places(core, own):
    rows = lax.broadcasted_iota(jnp.int32, (CHUNK, CHUNK), 0)
    lanes = lax.broadcasted_iota(jnp.int32, (CHUNK, CHUNK), 1)
    key_core = core if own else 1 - core
    at = jnp.where(rows < TOK, rows, rows + TOK) + core * TOK
    key = jnp.where(lanes < TOK, lanes, lanes + TOK) + key_core * TOK
    return at, key


def span_of(tile):
    return pl.ds(tile * CHUNK, CHUNK)


def load_part(refs, tile):
    top_ref, total_ref, output_ref = refs
    span = span_of(tile)
    return top_ref[span, :1], total_ref[span, :1], output_ref[span, :]


def store_part(refs, tile, part):
    span = span_of(tile)
    for ref, value in zip(refs, part):
        ref[span, :] = jnp.broadcast_to(value, (CHUNK, TOK))


def own_window_kernel(info_ref, own_ref, other_ref, mark_ref, *refs):
    core = info_ref[2]
    masks = []
    for own in (True, False):
        at, key = tile_places(core, own)
        masks.append(key <= at)
    for tile in range(TILES):
        queries = marked_queries(own_ref, mark_ref, tile)
        pieces = [
            (ref, m, mask if m == tile else None)
            for ref, mask in zip((own_ref, other_ref), masks)
            for m in range(tile + 1)
        ]
        store_part(refs, tile, absorb(queries, pieces, None))


def near_kernel(need_ref, own_ref, mark_ref, near_ref, other_ref, more_ref, a_ref, b_ref, c_ref, *refs):
    olds = (a_ref, b_ref, c_ref)
    for tile in range(TILES):
        needed = need_ref[2 * tile] == 1

        @pl.when(needed)
        def _(tile=tile):
            queries = marked_queries(own_ref, mark_ref, tile)
            pieces = [(near_ref, m, None) for m in range(TILES)]
            pieces += [(ref, m, None) for ref in (other_ref, more_ref) for m in range(TILES // 2)]
            store_part(refs, tile, absorb(queries, pieces, load_part(olds, tile)))

        @pl.when(jnp.logical_not(needed))
        def _(tile=tile):
            store_part(refs, tile, load_part(olds, tile))


def far_blocks(core, own, own_ref, mark_ref, need_ref, far_ref, olds, refs):
    at, key = tile_places(core, own)
    mask = key > at
    for tile in range(TILES):
        needed = need_ref[2 * tile + 1] == 1

        @pl.when(needed)
        def _(tile=tile):
            queries = marked_queries(own_ref, mark_ref, tile)
            pieces = [(far_ref, m, mask if m == tile else None) for m in range(tile, TILES)]
            store_part(refs, tile, absorb(queries, pieces, load_part(olds, tile)))

        @pl.when(jnp.logical_not(needed))
        def _(tile=tile):
            store_part(refs, tile, load_part(olds, tile))


def far_own_kernel(info_ref, need_ref, own_ref, mark_ref, far_ref, a_ref, b_ref, c_ref, *refs):
    far_blocks(info_ref[2], True, own_ref, mark_ref, need_ref, far_ref, (a_ref, b_ref, c_ref), refs)


def far_other_kernel(
    info_ref, need_ref, own_ref, mark_ref, far_ref, a_ref, b_ref, c_ref, linear_ref, square_ref, out_ref, *refs
):
    row = lax.broadcasted_iota(jnp.int32, (META, TOK), 0)
    for i in range(HEADS):
        out_ref[i, TOK : 2 * TOK, :] = linear_ref[i]
        meta = jnp.zeros((META, TOK), F32)
        for n, part in enumerate(split3(square_ref[i : i + 1, :])):
            meta = jnp.where(row == n, jnp.broadcast_to(part.astype(F32), (META, TOK)), meta)
        out_ref[i, 2 * TOK :, :] = meta.astype(BF16)
    far_blocks(info_ref[2], False, own_ref, mark_ref, need_ref, far_ref, (a_ref, b_ref, c_ref), refs)
    _, total_ref, output_ref = refs
    for i in range(HEADS):
        span = pl.ds(i * TOK, TOK)
        out_ref[i, 0:TOK, :] = (output_ref[span, :] / total_ref[span, :]).astype(BF16)


def finish_kernel(got_ref, gain_ref, out_ref):
    total = jnp.zeros((1, TOK), F32)
    for h in range(HEADS):
        total = total + joined(got_ref[h, 2 * TOK :, :], 0)
    inverse = column(lax.rsqrt(total / (HEAD_TOTAL * DH) + 1e-06))
    for h in range(HEADS):
        cols = pl.ds(h * DH, DH)
        linear = got_ref[h, TOK : 2 * TOK, :].astype(F32)
        window = got_ref[h, 0:TOK, :].astype(F32)
        out_ref[:, cols] = (gain_ref[:, cols] * linear * inverse + window).astype(BF16)


VMEM = pl.BlockSpec(memory_space=pltpu.VMEM)
SMEM = pl.BlockSpec(memory_space=pltpu.SMEM)
HBM = pl.BlockSpec(memory_space=pltpu.HBM)


LIMIT = {"prepare": 58}


def call(kernel, name, specs, shapes, scratch=(), outs=None):
    many = isinstance(shapes, (list, tuple))
    return pl.pallas_call(
        kernel,
        name=name,
        out_shape=shapes,
        in_specs=specs,
        out_specs=outs or ([VMEM] * len(shapes) if many else VMEM),
        scratch_shapes=list(scratch),
        compiler_params=pltpu.CompilerParams(vmem_limit_bytes=LIMIT.get(name, 16) * 2**20),
        cost_estimate=pl.CostEstimate(flops=0, bytes_accessed=0, transcendentals=0),
    )


def body(queries, keys, values, init_state, lin_gain, rate_table, rate_index, speed, drop, doc_id):
    x, z, core = (lax.axis_index(a).astype(jnp.int32) for a in ("x", "z", "core"))
    info = jnp.stack([x, z, core])
    shape = jax.ShapeDtypeStruct
    packed = call(
        prepare_kernel,
        "prepare",
        [SMEM, SMEM, HBM, HBM, HBM, VMEM, VMEM, VMEM],
        shape((HEADS, ROWS, TOK), BF16),
        scratch=[pltpu.VMEM((TOK, HEADS * DH), BF16)] * 3 + [pltpu.SemaphoreType.DMA((3,))],
    )(rate_table, rate_index, queries, keys, values, speed.T, drop.T, doc_id[None, :])
    own = lax.all_to_all(packed, "z", 0, 0, tiled=True)
    sent = own[:, :KV_ROWS]
    pair = [(0, 1), (1, 0)]
    near = lax.ppermute(sent, "x", [(0, 1), (1, 2), (2, 3)])
    other = lax.ppermute(sent, "core", pair)

    tokens = HEADS * TOK
    part_shapes = [shape((tokens, TOK), F32), shape((tokens, TOK), F32), shape((tokens, DH), F32)]
    init = lax.dynamic_slice_in_dim(init_state, z, 1, 0)
    partial, weight, state, mark = call(
        linear_kernel,
        "linear",
        [SMEM] + [VMEM] * 3,
        [
            shape((HEADS, TOK, DH), F32),
            shape((HEADS, TOK, DH), F32),
            shape((DH + 8, DH), F32),
            shape((HEADS, TOK, TOK), BF16),
        ],
    )(info, own, other, init)
    near_state = lax.ppermute(state, "x", [(0, 1), (1, 2), (2, 3)])
    far_state = lax.ppermute(state, "x", [(0, 2), (1, 3)])
    own_part = call(
        own_window_kernel, "own_window", [SMEM] + [VMEM] * 3, part_shapes
    )(info, own, other, mark)
    sent, own_part = lax.optimization_barrier((sent, own_part))
    far = lax.ppermute(sent, "x", [(0, 2), (1, 3)])
    near_state, far_state, own_part = lax.optimization_barrier((near_state, far_state, own_part))
    linear, square, need = call(
        enter_kernel,
        "enter",
        [SMEM] + [VMEM] * 6,
        [shape((HEADS, TOK, DH), BF16), shape((HEADS, TOK), F32), shape((2 * TILES,), jnp.int32)],
        outs=[VMEM, VMEM, SMEM],
    )(info, own, partial, weight, state, near_state, far_state)
    near, own_part = lax.optimization_barrier((near, own_part))
    near_other = [lax.ppermute(near[at : at + TILES], "core", pair) for at in (0, TILES)]
    squares = [lax.ppermute(square, "head", [(i, i ^ step) for i in range(4)]) for step in (1, 2, 3)]
    part = call(near_kernel, "near_window", [SMEM] + [VMEM] * 8, part_shapes)(
        need, own, mark, near, *near_other, *own_part
    )
    far, part, squares = lax.optimization_barrier((far, part, squares))
    square = square + squares[0] + (squares[1] + squares[2])
    far_other = lax.ppermute(far, "core", pair)
    part = call(far_own_kernel, "far_own", [SMEM] * 2 + [VMEM] * 6, part_shapes)(info, need, own, mark, far, *part)
    mixed = call(
        far_other_kernel,
        "far_other",
        [SMEM] * 2 + [VMEM] * 8,
        shape((HEADS, 2 * TOK + META, DH), BF16),
        scratch=[pltpu.VMEM((tokens, TOK), F32)] * 3,
    )(info, need, own, mark, far_other, *part, linear, square)
    back = lax.all_to_all(mixed, "z", 0, 0, tiled=True)
    return call(finish_kernel, "finish", [VMEM] * 2, shape((TOK, HEADS * DH), BF16))(
        back, lin_gain[None, :]
    )


def solution(mesh):
    split = Mesh(mesh.devices.reshape(4, 8, 2, 4), ("x", "z", "core", "head"))
    ctx = ("x", "z", "core")
    placed = (
        P(ctx, "head"),
        P(ctx, "head"),
        P(ctx, "head"),
        P("head", None, None),
        P("head"),
        P(),
        P("head"),
        P(ctx, "head"),
        P(ctx, "head"),
        P(ctx),
    )
    return jax.shard_map(body, mesh=split, in_specs=placed, out_specs=P(ctx, "head"), check_vma=False)
```

```python
import math

import jax
import jax.numpy as jnp
from jax import lax
from jax.experimental import pallas as pl
from jax.experimental.pallas import tpu as pltpu
from jax.sharding import Mesh
from jax.sharding import PartitionSpec as P

HEAD_TOTAL = 32
DH = 128
TOK = 128
WINDOW = 4096
HEADS = 8
META = 16
KV_ROWS = 2 * DH + META
ROWS = KV_ROWS + TOK
PLANE = 2 * HEADS * TOK
SCALE = 1.0 / math.sqrt(DH)
EXP2_SCALE = SCALE / math.log(2.0)
LOW = -1e30
F32 = jnp.float32
BF16 = jnp.bfloat16
CHUNK = 2 * TOK
TILES = HEADS // 2
META_AT = DH
VALUE_AT = DH + META


def dot(a, b):
    return jnp.dot(a, b, preferred_element_type=F32)


def split3(x):
    high = x.astype(BF16)
    rest = x - high.astype(F32)
    mid = rest.astype(BF16)
    low = (rest - mid.astype(F32)).astype(BF16)
    return high, mid, low


def joined(rows, at):
    part = rows.astype(F32)
    return part[at : at + 1] + part[at + 1 : at + 2] + part[at + 2 : at + 3]


def column(row):
    return jnp.transpose(jnp.broadcast_to(row, (TOK, TOK)))


def split_dot(a, state):
    high = state.astype(BF16)
    low = (state - high.astype(F32)).astype(BF16)
    return dot(a, high) + dot(a, low)


def prepare_kernel(
    table_ref, index_ref, q_hbm, k_hbm, v_hbm, speed_ref, drop_ref, doc_ref, out_ref, q_ref, k_ref, v_ref, sems
):
    copies = [
        pltpu.make_async_copy(src, dst, sems.at[n])
        for n, (src, dst) in enumerate(((k_hbm, k_ref), (v_hbm, v_ref), (q_hbm, q_ref)))
    ]
    for copy in copies:
        copy.start()
    head = lax.broadcasted_iota(jnp.int32, (HEADS, TOK), 0)
    rate = jnp.zeros((HEADS, TOK), F32)
    for h in range(HEADS):
        rate = jnp.where(head == h, table_ref[index_ref[h]], rate)
    log_decay = -rate * speed_ref[...] - drop_ref[...]
    upto = (
        lax.broadcasted_iota(jnp.int32, (TOK, TOK), 0)
        <= lax.broadcasted_iota(jnp.int32, (TOK, TOK), 1)
    ).astype(F32)
    cum = jnp.dot(log_decay, upto, precision=lax.Precision.HIGHEST, preferred_element_type=F32)
    parts = [part.astype(F32) for part in split3(cum)]
    row = lax.broadcasted_iota(jnp.int32, (META, TOK), 0)
    doc = jnp.broadcast_to(doc_ref[...].astype(F32), (META, TOK))
    bias = jnp.where(doc == (row - 4).astype(F32), 0.0, LOW)
    shared = jnp.where(row == 3, doc, jnp.where((row >= 4) & (row < 8), bias, 0.0))
    for h in range(HEADS):
        meta = shared
        for n, part in enumerate(parts):
            meta = jnp.where(row == n, jnp.broadcast_to(part[h : h + 1], (META, TOK)), meta)
        out_ref[h, META_AT:VALUE_AT, :] = meta.astype(BF16)
    copies[0].wait()
    for h in range(HEADS):
        out_ref[h, 0:DH, :] = jnp.transpose(k_ref[:, pl.ds(h * DH, DH)])
    copies[1].wait()
    copies[2].wait()
    for h in range(HEADS):
        cols = pl.ds(h * DH, DH)
        out_ref[h, VALUE_AT:KV_ROWS, :] = v_ref[:, cols]
        out_ref[h, KV_ROWS:ROWS, :] = q_ref[:, cols]


def meta_rows(ref, i):
    return ref[i, META_AT:VALUE_AT, :].astype(F32)


def linear_kernel(info_ref, own_ref, low_ref, high_ref, init_ref, partial_ref, weight_ref, state_ref, mark_ref):
    x, core = info_ref[0], info_ref[2]
    first = core == 0
    state = jnp.where(x == 0, init_ref[0], 0.0)
    carry = jnp.where(x == 0, jnp.zeros((1, TOK), F32), jnp.full((1, TOK), -1.0, F32))
    prefix = jnp.zeros((1, TOK), F32)
    places = lax.broadcasted_iota(jnp.int32, (TOK, TOK), 0)
    lanes = lax.broadcasted_iota(jnp.int32, (TOK, TOK), 1)
    causal = places >= lanes
    marked = (lanes >= 4) & (lanes < 8)
    number = (lanes - 4).astype(F32)
    start_doc = None

    def read(swap, i):
        mine, theirs = own_ref[i, 0:KV_ROWS, :], (low_ref, high_ref)[i // TILES][i % TILES]
        got = jnp.where(swap, theirs, mine)
        rows = got[META_AT:VALUE_AT].astype(F32)
        cum, doc = rows[0:1] + rows[1:2] + rows[2:3], rows[3:4]
        overall = jnp.broadcast_to(cum[:, TOK - 1 :], (1, TOK))
        last = jnp.broadcast_to(doc[:, TOK - 1 :], (1, TOK))
        return got[:DH], got[VALUE_AT:], cum, doc, overall, last

    def advance(state, carry, prefix, block):
        keys, values, cum, doc, overall, last = block
        factor = jnp.where(doc == last, jnp.exp(overall - cum), 0.0)
        scaled = (keys.astype(F32) * factor).astype(BF16)
        keep = jnp.where(last == carry, jnp.exp(overall), 0.0)
        return dot(scaled, values) + keep * state, last, prefix + overall

    for i in range(HEADS):
        even = read(jnp.logical_not(first), i)
        odd = read(first, i)
        if start_doc is None:
            start_doc = jnp.broadcast_to(even[3][:, :1], (1, TOK))
        middle = advance(state, carry, prefix, even)
        at_state = jnp.where(first, state, middle[0])
        at_carry = jnp.where(first, carry, middle[1])
        at_prefix = jnp.where(first, prefix, middle[2])
        keys, values, cum, doc, _, _ = [jnp.where(first, a, b) for a, b in zip(even, odd)]
        queries = own_ref[i, KV_ROWS:ROWS, :]
        cum_col, doc_col = column(cum), column(doc)
        inside = causal & (doc_col == doc)
        fading = jnp.exp(jnp.where(inside, cum_col - cum, 0.0))
        weights = jnp.where(inside, fading * dot(queries, keys) * SCALE, 0.0).astype(BF16)
        grown = jnp.exp(cum_col) * SCALE
        outside = jnp.where(doc_col == at_carry, grown * split_dot(queries, at_state), 0.0)
        partial_ref[i] = dot(weights, values) + outside
        weight_ref[i] = jnp.where(doc_col == start_doc, jnp.exp(cum_col + at_prefix) * SCALE, 0.0)
        mark_ref[i] = jnp.where(marked & (doc_col == number), 1.0, 0.0).astype(BF16)
        state, carry, prefix = advance(*middle, odd)
    state_ref[0:DH, :] = state
    row = lax.broadcasted_iota(jnp.int32, (8, TOK), 0)
    state_ref[DH : DH + 8, :] = jnp.where(row == 0, prefix, jnp.where(row == 1, carry, start_doc))


def enter_kernel(
    info_ref, own_ref, partial_ref, weight_ref, state_ref, near_ref, far_ref, linear_ref, square_ref, need_ref
):
    x = info_ref[0]
    near_decay, near_doc = near_ref[DH : DH + 1, :], near_ref[DH + 1 : DH + 2, :]
    far_doc, start_doc = far_ref[DH + 1 : DH + 2, :], state_ref[DH + 2 : DH + 3, :]
    keep = jnp.where((far_doc == near_doc) & (x >= 2), jnp.exp(near_decay), 0.0)
    state = near_ref[0:DH, :] + keep * far_ref[0:DH, :]
    state = jnp.where((start_doc == near_doc) & (x >= 1), state, 0.0)
    high = state.astype(BF16)
    low = (state - high.astype(F32)).astype(BF16)
    queries = jnp.concatenate([own_ref[i, KV_ROWS:ROWS, :] for i in range(HEADS)], axis=0)
    product = dot(queries, jnp.concatenate([high, low], axis=1))
    product = product[:, :DH] + product[:, DH:]
    eye = lax.broadcasted_iota(jnp.int32, (TOK, DH), 0) == lax.broadcasted_iota(jnp.int32, (TOK, DH), 1)
    for i in range(HEADS):
        linear = partial_ref[i] + weight_ref[i] * product[i * TOK : (i + 1) * TOK]
        linear_ref[i] = linear.astype(BF16)
        square = jnp.sum(linear * linear, axis=1, keepdims=True)
        square_ref[i : i + 1, :] = jnp.sum(jnp.where(eye, square, 0.0), axis=0, keepdims=True)
    for tile in range(TILES):
        tile_doc = jnp.broadcast_to(meta_rows(own_ref, 2 * tile)[3:4, :1], (1, TOK))
        need_ref[2 * tile] = jnp.where(x >= 1, jnp.max(jnp.where(tile_doc == near_doc, 1, 0)), 0)
        need_ref[2 * tile + 1] = jnp.where(x >= 2, jnp.max(jnp.where(tile_doc == far_doc, 1, 0)), 0)


def marked_queries(own_ref, mark_ref, tile):
    i = 2 * tile
    queries = jnp.concatenate([own_ref[i, KV_ROWS:ROWS, :], own_ref[i + 1, KV_ROWS:ROWS, :]], axis=0)
    marks = jnp.concatenate([mark_ref[i], mark_ref[i + 1]], axis=0)[:, :META]
    return jnp.concatenate([queries, marks], axis=1)


def absorb(queries, pieces, old):
    scores = []
    top = None
    for ref, m, mask in pieces:
        keys = jnp.concatenate([ref[2 * m, 0:VALUE_AT, :], ref[2 * m + 1, 0:VALUE_AT, :]], axis=1)
        score = dot(queries, keys)
        if mask is not None:
            score = jnp.where(mask, score, LOW)
        scores.append(score)
        most = jnp.maximum(score[:, :TOK], score[:, TOK:])
        top = most if top is None else jnp.maximum(top, most)
    top = jnp.max(top, axis=1, keepdims=True)
    if old is not None:
        top = jnp.maximum(top, old[0])
    base = top * EXP2_SCALE
    sums, output = None, None
    for (ref, m, _), score in zip(pieces, scores):
        weights = jnp.exp2(score * EXP2_SCALE - base)
        part = weights[:, :TOK] + weights[:, TOK:]
        sums = part if sums is None else sums + part
        values = jnp.concatenate([ref[2 * m, VALUE_AT:KV_ROWS, :], ref[2 * m + 1, VALUE_AT:KV_ROWS, :]], axis=0)
        product = dot(weights.astype(BF16), values)
        output = product if output is None else output + product
    total = jnp.sum(sums, axis=1, keepdims=True)
    if old is not None:
        shrink = jnp.exp2(old[0] * EXP2_SCALE - base)
        total = total + old[1] * shrink
        output = output + old[2] * shrink
    return top, total, output


def tile_places(core, own):
    rows = lax.broadcasted_iota(jnp.int32, (CHUNK, CHUNK), 0)
    lanes = lax.broadcasted_iota(jnp.int32, (CHUNK, CHUNK), 1)
    key_core = core if own else 1 - core
    at = jnp.where(rows < TOK, rows, rows + TOK) + core * TOK
    key = jnp.where(lanes < TOK, lanes, lanes + TOK) + key_core * TOK
    return at, key


def span_of(tile):
    return pl.ds(tile * CHUNK, CHUNK)


def load_part(refs, tile):
    top_ref, total_ref, output_ref = refs
    span = span_of(tile)
    return top_ref[span, :1], total_ref[span, :1], output_ref[span, :]


def store_part(refs, tile, part):
    span = span_of(tile)
    for ref, value in zip(refs, part):
        ref[span, :] = jnp.broadcast_to(value, (CHUNK, TOK))


def own_window_kernel(info_ref, own_ref, low_ref, high_ref, mark_ref, *refs):
    core = info_ref[2]
    masks = []
    for own in (True, False):
        at, key = tile_places(core, own)
        masks.append(key <= at)
    for tile in range(TILES):
        queries = marked_queries(own_ref, mark_ref, tile)
        pieces = [(own_ref, m, masks[0] if m == tile else None) for m in range(tile + 1)]
        pieces += [
            ((low_ref, high_ref)[m // 2], m % 2, masks[1] if m == tile else None) for m in range(tile + 1)
        ]
        store_part(refs, tile, absorb(queries, pieces, None))


def near_kernel(need_ref, own_ref, mark_ref, near_ref, other_ref, more_ref, a_ref, b_ref, c_ref, *refs):
    olds = (a_ref, b_ref, c_ref)
    for tile in range(TILES):
        needed = need_ref[2 * tile] == 1

        @pl.when(needed)
        def _(tile=tile):
            queries = marked_queries(own_ref, mark_ref, tile)
            pieces = [(near_ref, m, None) for m in range(TILES)]
            pieces += [(ref, m, None) for ref in (other_ref, more_ref) for m in range(TILES // 2)]
            store_part(refs, tile, absorb(queries, pieces, load_part(olds, tile)))

        @pl.when(jnp.logical_not(needed))
        def _(tile=tile):
            store_part(refs, tile, load_part(olds, tile))


def far_blocks(core, own, own_ref, mark_ref, need_ref, far_ref, olds, refs):
    at, key = tile_places(core, own)
    mask = key > at
    for tile in range(TILES):
        needed = need_ref[2 * tile + 1] == 1

        @pl.when(needed)
        def _(tile=tile):
            queries = marked_queries(own_ref, mark_ref, tile)
            pieces = [(far_ref, m, mask if m == tile else None) for m in range(tile, TILES)]
            store_part(refs, tile, absorb(queries, pieces, load_part(olds, tile)))

        @pl.when(jnp.logical_not(needed))
        def _(tile=tile):
            store_part(refs, tile, load_part(olds, tile))


def far_own_kernel(info_ref, need_ref, own_ref, mark_ref, far_ref, a_ref, b_ref, c_ref, *refs):
    far_blocks(info_ref[2], True, own_ref, mark_ref, need_ref, far_ref, (a_ref, b_ref, c_ref), refs)


def far_other_kernel(
    info_ref, need_ref, own_ref, mark_ref, far_ref, a_ref, b_ref, c_ref, linear_ref, square_ref, out_ref, *refs
):
    row = lax.broadcasted_iota(jnp.int32, (META, TOK), 0)
    for i in range(HEADS):
        out_ref[i, TOK : 2 * TOK, :] = linear_ref[i]
        meta = jnp.zeros((META, TOK), F32)
        for n, part in enumerate(split3(square_ref[i : i + 1, :])):
            meta = jnp.where(row == n, jnp.broadcast_to(part.astype(F32), (META, TOK)), meta)
        out_ref[i, 2 * TOK :, :] = meta.astype(BF16)
    far_blocks(info_ref[2], False, own_ref, mark_ref, need_ref, far_ref, (a_ref, b_ref, c_ref), refs)
    _, total_ref, output_ref = refs
    for i in range(HEADS):
        span = pl.ds(i * TOK, TOK)
        out_ref[i, 0:TOK, :] = (output_ref[span, :] / total_ref[span, :]).astype(BF16)


def finish_kernel(got_ref, gain_ref, out_ref):
    total = jnp.zeros((1, TOK), F32)
    for h in range(HEADS):
        total = total + joined(got_ref[h, 2 * TOK :, :], 0)
    inverse = column(lax.rsqrt(total / (HEAD_TOTAL * DH) + 1e-06))
    for h in range(HEADS):
        cols = pl.ds(h * DH, DH)
        linear = got_ref[h, TOK : 2 * TOK, :].astype(F32)
        window = got_ref[h, 0:TOK, :].astype(F32)
        out_ref[:, cols] = (gain_ref[:, cols] * linear * inverse + window).astype(BF16)


VMEM = pl.BlockSpec(memory_space=pltpu.VMEM)
SMEM = pl.BlockSpec(memory_space=pltpu.SMEM)
HBM = pl.BlockSpec(memory_space=pltpu.HBM)


LIMIT = {"prepare": 58}


def call(kernel, name, specs, shapes, scratch=(), outs=None):
    many = isinstance(shapes, (list, tuple))
    return pl.pallas_call(
        kernel,
        name=name,
        out_shape=shapes,
        in_specs=specs,
        out_specs=outs or ([VMEM] * len(shapes) if many else VMEM),
        scratch_shapes=list(scratch),
        compiler_params=pltpu.CompilerParams(vmem_limit_bytes=LIMIT.get(name, 16) * 2**20),
        cost_estimate=pl.CostEstimate(flops=0, bytes_accessed=0, transcendentals=0),
    )


def body(queries, keys, values, init_state, lin_gain, rate_table, rate_index, speed, drop, doc_id):
    x, z, core = (lax.axis_index(a).astype(jnp.int32) for a in ("x", "z", "core"))
    info = jnp.stack([x, z, core])
    shape = jax.ShapeDtypeStruct
    packed = call(
        prepare_kernel,
        "prepare",
        [SMEM, SMEM, HBM, HBM, HBM, VMEM, VMEM, VMEM],
        shape((HEADS, ROWS, TOK), BF16),
        scratch=[pltpu.VMEM((TOK, HEADS * DH), BF16)] * 3 + [pltpu.SemaphoreType.DMA((3,))],
    )(rate_table, rate_index, queries, keys, values, speed.T, drop.T, doc_id[None, :])
    own = lax.all_to_all(packed, "z", 0, 0, tiled=True)
    sent = own[:, :KV_ROWS]
    pair = [(0, 1), (1, 0)]
    near = lax.ppermute(sent, "x", [(0, 1), (1, 2), (2, 3)])
    other = [lax.ppermute(sent[at : at + TILES], "core", pair) for at in (0, TILES)]

    tokens = HEADS * TOK
    part_shapes = [shape((tokens, TOK), F32), shape((tokens, TOK), F32), shape((tokens, DH), F32)]
    init = lax.dynamic_slice_in_dim(init_state, z, 1, 0)
    partial, weight, state, mark = call(
        linear_kernel,
        "linear",
        [SMEM] + [VMEM] * 4,
        [
            shape((HEADS, TOK, DH), F32),
            shape((HEADS, TOK, DH), F32),
            shape((DH + 8, DH), F32),
            shape((HEADS, TOK, TOK), BF16),
        ],
    )(info, own, *other, init)
    near_state = lax.ppermute(state, "x", [(0, 1), (1, 2), (2, 3)])
    far_state = lax.ppermute(state, "x", [(0, 2), (1, 3)])
    own_part = call(
        own_window_kernel, "own_window", [SMEM] + [VMEM] * 4, part_shapes
    )(info, own, *other, mark)
    sent, own_part = lax.optimization_barrier((sent, own_part))
    far = lax.ppermute(sent, "x", [(0, 2), (1, 3)])
    near_state, far_state, own_part = lax.optimization_barrier((near_state, far_state, own_part))
    linear, square, need = call(
        enter_kernel,
        "enter",
        [SMEM] + [VMEM] * 6,
        [shape((HEADS, TOK, DH), BF16), shape((HEADS, TOK), F32), shape((2 * TILES,), jnp.int32)],
        outs=[VMEM, VMEM, SMEM],
    )(info, own, partial, weight, state, near_state, far_state)
    near, own_part = lax.optimization_barrier((near, own_part))
    near_other = [lax.ppermute(near[at : at + TILES], "core", pair) for at in (0, TILES)]
    squares = [lax.ppermute(square, "head", [(i, i ^ step) for i in range(4)]) for step in (1, 2, 3)]
    part = call(near_kernel, "near_window", [SMEM] + [VMEM] * 8, part_shapes)(
        need, own, mark, near, *near_other, *own_part
    )
    far, part, squares = lax.optimization_barrier((far, part, squares))
    square = square + squares[0] + (squares[1] + squares[2])
    far_other = lax.ppermute(far, "core", pair)
    part = call(far_own_kernel, "far_own", [SMEM] * 2 + [VMEM] * 6, part_shapes)(info, need, own, mark, far, *part)
    mixed = call(
        far_other_kernel,
        "far_other",
        [SMEM] * 2 + [VMEM] * 8,
        shape((HEADS, 2 * TOK + META, DH), BF16),
        scratch=[pltpu.VMEM((tokens, TOK), F32)] * 3,
    )(info, need, own, mark, far_other, *part, linear, square)
    back = lax.all_to_all(mixed, "z", 0, 0, tiled=True)
    return call(finish_kernel, "finish", [VMEM] * 2, shape((TOK, HEADS * DH), BF16))(
        back, lin_gain[None, :]
    )


def solution(mesh):
    split = Mesh(mesh.devices.reshape(4, 8, 2, 4), ("x", "z", "core", "head"))
    ctx = ("x", "z", "core")
    placed = (
        P(ctx, "head"),
        P(ctx, "head"),
        P(ctx, "head"),
        P("head", None, None),
        P("head"),
        P(),
        P("head"),
        P(ctx, "head"),
        P(ctx, "head"),
        P(ctx),
    )
    return jax.shard_map(body, mesh=split, in_specs=placed, out_specs=P(ctx, "head"), check_vma=False)
```

```python
import math

import jax
import jax.numpy as jnp
from jax import lax
from jax.experimental import pallas as pl
from jax.experimental.pallas import tpu as pltpu
from jax.sharding import Mesh
from jax.sharding import PartitionSpec as P

HEAD_TOTAL = 32
DH = 128
TOK = 128
WINDOW = 4096
HEADS = 8
META = 16
KV_ROWS = 2 * DH + META
ROWS = KV_ROWS + TOK
PLANE = 2 * HEADS * TOK
SCALE = 1.0 / math.sqrt(DH)
EXP2_SCALE = SCALE / math.log(2.0)
LOW = -1e30
F32 = jnp.float32
BF16 = jnp.bfloat16
CHUNK = 2 * TOK
TILES = HEADS // 2
META_AT = DH
VALUE_AT = DH + META


def dot(a, b):
    return jnp.dot(a, b, preferred_element_type=F32)


def split3(x):
    high = x.astype(BF16)
    rest = x - high.astype(F32)
    mid = rest.astype(BF16)
    low = (rest - mid.astype(F32)).astype(BF16)
    return high, mid, low


def joined(rows, at):
    part = rows.astype(F32)
    return part[at : at + 1] + part[at + 1 : at + 2] + part[at + 2 : at + 3]


def column(row):
    return jnp.transpose(jnp.broadcast_to(row, (TOK, TOK)))


def split_dot(a, state):
    high = state.astype(BF16)
    low = (state - high.astype(F32)).astype(BF16)
    return dot(a, high) + dot(a, low)


def prepare_kernel(
    table_ref, index_ref, q_hbm, k_hbm, v_hbm, speed_ref, drop_ref, doc_ref, out_ref, q_ref, k_ref, v_ref, sems
):
    copies = [
        pltpu.make_async_copy(src, dst, sems.at[n])
        for n, (src, dst) in enumerate(((k_hbm, k_ref), (v_hbm, v_ref), (q_hbm, q_ref)))
    ]
    for copy in copies:
        copy.start()
    head = lax.broadcasted_iota(jnp.int32, (HEADS, TOK), 0)
    rate = jnp.zeros((HEADS, TOK), F32)
    for h in range(HEADS):
        rate = jnp.where(head == h, table_ref[index_ref[h]], rate)
    log_decay = -rate * speed_ref[...] - drop_ref[...]
    upto = (
        lax.broadcasted_iota(jnp.int32, (TOK, TOK), 0)
        <= lax.broadcasted_iota(jnp.int32, (TOK, TOK), 1)
    ).astype(F32)
    cum = jnp.dot(log_decay, upto, precision=lax.Precision.HIGHEST, preferred_element_type=F32)
    parts = [part.astype(F32) for part in split3(cum)]
    row = lax.broadcasted_iota(jnp.int32, (META, TOK), 0)
    doc = jnp.broadcast_to(doc_ref[...].astype(F32), (META, TOK))
    bias = jnp.where(doc == (row - 4).astype(F32), 0.0, LOW)
    shared = jnp.where(row == 3, doc, jnp.where((row >= 4) & (row < 8), bias, 0.0))
    for h in range(HEADS):
        meta = shared
        for n, part in enumerate(parts):
            meta = jnp.where(row == n, jnp.broadcast_to(part[h : h + 1], (META, TOK)), meta)
        out_ref[h, META_AT:VALUE_AT, :] = meta.astype(BF16)
    copies[0].wait()
    for h in range(HEADS):
        out_ref[h, 0:DH, :] = jnp.transpose(k_ref[:, pl.ds(h * DH, DH)])
    copies[1].wait()
    copies[2].wait()
    for h in range(HEADS):
        cols = pl.ds(h * DH, DH)
        out_ref[h, VALUE_AT:KV_ROWS, :] = v_ref[:, cols]
        out_ref[h, KV_ROWS:ROWS, :] = q_ref[:, cols]


def meta_rows(ref, i):
    return ref[i, META_AT:VALUE_AT, :].astype(F32)


def linear_kernel(info_ref, own_ref, low_ref, high_ref, init_ref, partial_ref, weight_ref, state_ref, mark_ref):
    x, core = info_ref[0], info_ref[2]
    first = core == 0
    state = jnp.where(x == 0, init_ref[0], 0.0)
    carry = jnp.where(x == 0, jnp.zeros((1, TOK), F32), jnp.full((1, TOK), -1.0, F32))
    prefix = jnp.zeros((1, TOK), F32)
    places = lax.broadcasted_iota(jnp.int32, (TOK, TOK), 0)
    lanes = lax.broadcasted_iota(jnp.int32, (TOK, TOK), 1)
    causal = places >= lanes
    marked = (lanes >= 4) & (lanes < 8)
    number = (lanes - 4).astype(F32)
    start_doc = None

    def read(swap, i):
        mine, theirs = own_ref[i, 0:KV_ROWS, :], (low_ref, high_ref)[i // TILES][i % TILES]
        got = jnp.where(swap, theirs, mine)
        rows = got[META_AT:VALUE_AT].astype(F32)
        cum, doc = rows[0:1] + rows[1:2] + rows[2:3], rows[3:4]
        overall = jnp.broadcast_to(cum[:, TOK - 1 :], (1, TOK))
        last = jnp.broadcast_to(doc[:, TOK - 1 :], (1, TOK))
        return got[:DH], got[VALUE_AT:], cum, doc, overall, last

    def advance(state, carry, prefix, block):
        keys, values, cum, doc, overall, last = block
        factor = jnp.where(doc == last, jnp.exp(overall - cum), 0.0)
        scaled = (keys.astype(F32) * factor).astype(BF16)
        keep = jnp.where(last == carry, jnp.exp(overall), 0.0)
        return dot(scaled, values) + keep * state, last, prefix + overall

    for i in range(HEADS):
        even = read(jnp.logical_not(first), i)
        odd = read(first, i)
        if start_doc is None:
            start_doc = jnp.broadcast_to(even[3][:, :1], (1, TOK))
        middle = advance(state, carry, prefix, even)
        at_state = jnp.where(first, state, middle[0])
        at_carry = jnp.where(first, carry, middle[1])
        at_prefix = jnp.where(first, prefix, middle[2])
        keys, values, cum, doc, _, _ = [jnp.where(first, a, b) for a, b in zip(even, odd)]
        queries = own_ref[i, KV_ROWS:ROWS, :]
        cum_col, doc_col = column(cum), column(doc)
        inside = causal & (doc_col == doc)
        fading = jnp.exp(jnp.where(inside, cum_col - cum, 0.0))
        weights = jnp.where(inside, fading * dot(queries, keys) * SCALE, 0.0).astype(BF16)
        grown = jnp.exp(cum_col) * SCALE
        outside = jnp.where(doc_col == at_carry, grown * split_dot(queries, at_state), 0.0)
        partial_ref[i] = dot(weights, values) + outside
        weight_ref[i] = jnp.where(doc_col == start_doc, jnp.exp(cum_col + at_prefix) * SCALE, 0.0)
        mark_ref[i] = jnp.where(marked & (doc_col == number), 1.0, 0.0).astype(BF16)
        state, carry, prefix = advance(*middle, odd)
    state_ref[0:DH, :] = state
    row = lax.broadcasted_iota(jnp.int32, (8, TOK), 0)
    state_ref[DH : DH + 8, :] = jnp.where(row == 0, prefix, jnp.where(row == 1, carry, start_doc))


def enter_kernel(
    info_ref, own_ref, partial_ref, weight_ref, state_ref, near_ref, far_ref, linear_ref, square_ref, need_ref
):
    x = info_ref[0]
    near_decay, near_doc = near_ref[DH : DH + 1, :], near_ref[DH + 1 : DH + 2, :]
    far_doc, start_doc = far_ref[DH + 1 : DH + 2, :], state_ref[DH + 2 : DH + 3, :]
    keep = jnp.where((far_doc == near_doc) & (x >= 2), jnp.exp(near_decay), 0.0)
    state = near_ref[0:DH, :] + keep * far_ref[0:DH, :]
    state = jnp.where((start_doc == near_doc) & (x >= 1), state, 0.0)
    high = state.astype(BF16)
    low = (state - high.astype(F32)).astype(BF16)
    queries = jnp.concatenate([own_ref[i, KV_ROWS:ROWS, :] for i in range(HEADS)], axis=0)
    product = dot(queries, jnp.concatenate([high, low], axis=1))
    product = product[:, :DH] + product[:, DH:]
    eye = lax.broadcasted_iota(jnp.int32, (TOK, DH), 0) == lax.broadcasted_iota(jnp.int32, (TOK, DH), 1)
    for i in range(HEADS):
        linear = partial_ref[i] + weight_ref[i] * product[i * TOK : (i + 1) * TOK]
        linear_ref[i] = linear.astype(BF16)
        square = jnp.sum(linear * linear, axis=1, keepdims=True)
        square_ref[i : i + 1, :] = jnp.sum(jnp.where(eye, square, 0.0), axis=0, keepdims=True)
    for tile in range(TILES):
        tile_doc = jnp.broadcast_to(meta_rows(own_ref, 2 * tile)[3:4, :1], (1, TOK))
        need_ref[2 * tile] = jnp.where(x >= 1, jnp.max(jnp.where(tile_doc == near_doc, 1, 0)), 0)
        need_ref[2 * tile + 1] = jnp.where(x >= 2, jnp.max(jnp.where(tile_doc == far_doc, 1, 0)), 0)


def marked_queries(own_ref, mark_ref, tile):
    i = 2 * tile
    queries = jnp.concatenate([own_ref[i, KV_ROWS:ROWS, :], own_ref[i + 1, KV_ROWS:ROWS, :]], axis=0)
    marks = jnp.concatenate([mark_ref[i], mark_ref[i + 1]], axis=0)[:, :META]
    return jnp.concatenate([queries, marks], axis=1)


def absorb(queries, pieces, old):
    scores = []
    top = None
    for ref, m, mask in pieces:
        keys = jnp.concatenate([ref[2 * m, 0:VALUE_AT, :], ref[2 * m + 1, 0:VALUE_AT, :]], axis=1)
        score = dot(queries, keys)
        if mask is not None:
            score = jnp.where(mask, score, LOW)
        scores.append(score)
        most = jnp.maximum(score[:, :TOK], score[:, TOK:])
        top = most if top is None else jnp.maximum(top, most)
    top = jnp.max(top, axis=1, keepdims=True)
    if old is not None:
        top = jnp.maximum(top, old[0])
    base = top * EXP2_SCALE
    sums, output = None, None
    for (ref, m, _), score in zip(pieces, scores):
        weights = jnp.exp2(score * EXP2_SCALE - base)
        part = weights[:, :TOK] + weights[:, TOK:]
        sums = part if sums is None else sums + part
        values = jnp.concatenate([ref[2 * m, VALUE_AT:KV_ROWS, :], ref[2 * m + 1, VALUE_AT:KV_ROWS, :]], axis=0)
        product = dot(weights.astype(BF16), values)
        output = product if output is None else output + product
    total = jnp.sum(sums, axis=1, keepdims=True)
    if old is not None:
        shrink = jnp.exp2(old[0] * EXP2_SCALE - base)
        total = total + old[1] * shrink
        output = output + old[2] * shrink
    return top, total, output


def tile_places(core, own):
    rows = lax.broadcasted_iota(jnp.int32, (CHUNK, CHUNK), 0)
    lanes = lax.broadcasted_iota(jnp.int32, (CHUNK, CHUNK), 1)
    key_core = core if own else 1 - core
    at = jnp.where(rows < TOK, rows, rows + TOK) + core * TOK
    key = jnp.where(lanes < TOK, lanes, lanes + TOK) + key_core * TOK
    return at, key


def span_of(tile):
    return pl.ds(tile * CHUNK, CHUNK)


def load_part(refs, tile):
    top_ref, total_ref, output_ref = refs
    span = span_of(tile)
    return top_ref[span, :1], total_ref[span, :1], output_ref[span, :]


def store_part(refs, tile, part):
    span = span_of(tile)
    for ref, value in zip(refs, part):
        ref[span, :] = jnp.broadcast_to(value, (CHUNK, TOK))


def own_window_kernel(info_ref, own_ref, low_ref, high_ref, mark_ref, *refs):
    core = info_ref[2]
    masks = []
    for own in (True, False):
        at, key = tile_places(core, own)
        masks.append(key <= at)
    for tile in range(TILES):
        queries = marked_queries(own_ref, mark_ref, tile)
        pieces = [(own_ref, m, masks[0] if m == tile else None) for m in range(tile + 1)]
        pieces += [
            ((low_ref, high_ref)[m // 2], m % 2, masks[1] if m == tile else None) for m in range(tile + 1)
        ]
        store_part(refs, tile, absorb(queries, pieces, None))


def near_kernel(need_ref, own_ref, mark_ref, near_ref, other_ref, more_ref, a_ref, b_ref, c_ref, *refs):
    olds = (a_ref, b_ref, c_ref)
    for tile in range(TILES):
        needed = need_ref[2 * tile] == 1

        @pl.when(needed)
        def _(tile=tile):
            queries = marked_queries(own_ref, mark_ref, tile)
            pieces = [(near_ref, m, None) for m in range(TILES)]
            pieces += [(ref, m, None) for ref in (other_ref, more_ref) for m in range(TILES // 2)]
            store_part(refs, tile, absorb(queries, pieces, load_part(olds, tile)))

        @pl.when(jnp.logical_not(needed))
        def _(tile=tile):
            store_part(refs, tile, load_part(olds, tile))


def far_blocks(core, own, own_ref, mark_ref, need_ref, far_ref, olds, refs):
    at, key = tile_places(core, own)
    mask = key > at
    for tile in range(TILES):
        needed = need_ref[2 * tile + 1] == 1

        @pl.when(needed)
        def _(tile=tile):
            queries = marked_queries(own_ref, mark_ref, tile)
            pieces = [(far_ref, m, mask if m == tile else None) for m in range(tile, TILES)]
            store_part(refs, tile, absorb(queries, pieces, load_part(olds, tile)))

        @pl.when(jnp.logical_not(needed))
        def _(tile=tile):
            store_part(refs, tile, load_part(olds, tile))


def far_own_kernel(info_ref, need_ref, own_ref, mark_ref, far_ref, a_ref, b_ref, c_ref, *refs):
    far_blocks(info_ref[2], True, own_ref, mark_ref, need_ref, far_ref, (a_ref, b_ref, c_ref), refs)


def far_other_kernel(
    info_ref, need_ref, own_ref, mark_ref, far_ref, a_ref, b_ref, c_ref, linear_ref, square_ref, out_ref, *refs
):
    row = lax.broadcasted_iota(jnp.int32, (META, TOK), 0)
    for i in range(HEADS):
        out_ref[i, TOK : 2 * TOK, :] = linear_ref[i]
        meta = jnp.zeros((META, TOK), F32)
        for n, part in enumerate(split3(square_ref[i : i + 1, :])):
            meta = jnp.where(row == n, jnp.broadcast_to(part.astype(F32), (META, TOK)), meta)
        out_ref[i, 2 * TOK :, :] = meta.astype(BF16)
    far_blocks(info_ref[2], False, own_ref, mark_ref, need_ref, far_ref, (a_ref, b_ref, c_ref), refs)
    _, total_ref, output_ref = refs
    for i in range(HEADS):
        span = pl.ds(i * TOK, TOK)
        out_ref[i, 0:TOK, :] = (output_ref[span, :] / total_ref[span, :]).astype(BF16)


def finish_kernel(got_ref, gain_ref, out_ref):
    total = jnp.zeros((1, TOK), F32)
    for h in range(HEADS):
        total = total + joined(got_ref[h, 2 * TOK :, :], 0)
    inverse = column(lax.rsqrt(total / (HEAD_TOTAL * DH) + 1e-06))
    for h in range(HEADS):
        cols = pl.ds(h * DH, DH)
        linear = got_ref[h, TOK : 2 * TOK, :].astype(F32)
        window = got_ref[h, 0:TOK, :].astype(F32)
        out_ref[:, cols] = (gain_ref[:, cols] * linear * inverse + window).astype(BF16)


VMEM = pl.BlockSpec(memory_space=pltpu.VMEM)
SMEM = pl.BlockSpec(memory_space=pltpu.SMEM)
HBM = pl.BlockSpec(memory_space=pltpu.HBM)


LIMIT = {"prepare": 58}


def call(kernel, name, specs, shapes, scratch=(), outs=None):
    many = isinstance(shapes, (list, tuple))
    return pl.pallas_call(
        kernel,
        name=name,
        out_shape=shapes,
        in_specs=specs,
        out_specs=outs or ([VMEM] * len(shapes) if many else VMEM),
        scratch_shapes=list(scratch),
        compiler_params=pltpu.CompilerParams(vmem_limit_bytes=LIMIT.get(name, 16) * 2**20),
        cost_estimate=pl.CostEstimate(flops=0, bytes_accessed=0, transcendentals=0),
    )


def body(queries, keys, values, init_state, lin_gain, rate_table, rate_index, speed, drop, doc_id):
    x, z, core = (lax.axis_index(a).astype(jnp.int32) for a in ("x", "z", "core"))
    info = jnp.stack([x, z, core])
    shape = jax.ShapeDtypeStruct
    packed = call(
        prepare_kernel,
        "prepare",
        [SMEM, SMEM, HBM, HBM, HBM, VMEM, VMEM, VMEM],
        shape((HEADS, ROWS, TOK), BF16),
        scratch=[pltpu.VMEM((TOK, HEADS * DH), BF16)] * 3 + [pltpu.SemaphoreType.DMA((3,))],
    )(rate_table, rate_index, queries, keys, values, speed.T, drop.T, doc_id[None, :])
    own = lax.all_to_all(packed, "z", 0, 0, tiled=True)
    sent = own[:, :KV_ROWS]
    pair = [(0, 1), (1, 0)]
    near = lax.ppermute(sent, "x", [(0, 1), (1, 2), (2, 3)])
    other = [lax.ppermute(sent[at : at + TILES], "core", pair) for at in (0, TILES)]

    tokens = HEADS * TOK
    part_shapes = [shape((tokens, TOK), F32), shape((tokens, TOK), F32), shape((tokens, DH), F32)]
    init = lax.dynamic_slice_in_dim(init_state, z, 1, 0)
    partial, weight, state, mark = call(
        linear_kernel,
        "linear",
        [SMEM] + [VMEM] * 4,
        [
            shape((HEADS, TOK, DH), F32),
            shape((HEADS, TOK, DH), F32),
            shape((DH + 8, DH), F32),
            shape((HEADS, TOK, TOK), BF16),
        ],
    )(info, own, *other, init)
    near_state = lax.ppermute(state, "x", [(0, 1), (1, 2), (2, 3)])
    far_state = lax.ppermute(state, "x", [(0, 2), (1, 3)])
    own_part = call(
        own_window_kernel, "own_window", [SMEM] + [VMEM] * 4, part_shapes
    )(info, own, *other, mark)
    sent, partial = lax.optimization_barrier((sent, partial))
    far = lax.ppermute(sent, "x", [(0, 2), (1, 3)])
    near_state, far_state, own_part = lax.optimization_barrier((near_state, far_state, own_part))
    linear, square, need = call(
        enter_kernel,
        "enter",
        [SMEM] + [VMEM] * 6,
        [shape((HEADS, TOK, DH), BF16), shape((HEADS, TOK), F32), shape((2 * TILES,), jnp.int32)],
        outs=[VMEM, VMEM, SMEM],
    )(info, own, partial, weight, state, near_state, far_state)
    near, own_part = lax.optimization_barrier((near, own_part))
    near_other = [lax.ppermute(near[at : at + TILES], "core", pair) for at in (0, TILES)]
    squares = [lax.ppermute(square, "head", [(i, i ^ step) for i in range(4)]) for step in (1, 2, 3)]
    part = call(near_kernel, "near_window", [SMEM] + [VMEM] * 8, part_shapes)(
        need, own, mark, near, *near_other, *own_part
    )
    far, part, squares = lax.optimization_barrier((far, part, squares))
    square = square + squares[0] + (squares[1] + squares[2])
    far_other = lax.ppermute(far, "core", pair)
    part = call(far_own_kernel, "far_own", [SMEM] * 2 + [VMEM] * 6, part_shapes)(info, need, own, mark, far, *part)
    mixed = call(
        far_other_kernel,
        "far_other",
        [SMEM] * 2 + [VMEM] * 8,
        shape((HEADS, 2 * TOK + META, DH), BF16),
        scratch=[pltpu.VMEM((tokens, TOK), F32)] * 3,
    )(info, need, own, mark, far_other, *part, linear, square)
    back = lax.all_to_all(mixed, "z", 0, 0, tiled=True)
    return call(finish_kernel, "finish", [VMEM] * 2, shape((TOK, HEADS * DH), BF16))(
        back, lin_gain[None, :]
    )


def solution(mesh):
    split = Mesh(mesh.devices.reshape(4, 8, 2, 4), ("x", "z", "core", "head"))
    ctx = ("x", "z", "core")
    placed = (
        P(ctx, "head"),
        P(ctx, "head"),
        P(ctx, "head"),
        P("head", None, None),
        P("head"),
        P(),
        P("head"),
        P(ctx, "head"),
        P(ctx, "head"),
        P(ctx),
    )
    return jax.shard_map(body, mesh=split, in_specs=placed, out_specs=P(ctx, "head"), check_vma=False)
```

```python
import math

import jax
import jax.numpy as jnp
from jax import lax
from jax.experimental import pallas as pl
from jax.experimental.pallas import tpu as pltpu
from jax.sharding import Mesh
from jax.sharding import PartitionSpec as P

HEAD_TOTAL = 32
DH = 128
TOK = 128
WINDOW = 4096
HEADS = 8
META = 16
KV_ROWS = 2 * DH + META
ROWS = KV_ROWS + TOK
PLANE = 2 * HEADS * TOK
SCALE = 1.0 / math.sqrt(DH)
EXP2_SCALE = SCALE / math.log(2.0)
LOW = -1e30
F32 = jnp.float32
BF16 = jnp.bfloat16
CHUNK = 2 * TOK
TILES = HEADS // 2
META_AT = DH
VALUE_AT = DH + META


def dot(a, b):
    return jnp.dot(a, b, preferred_element_type=F32)


def split3(x):
    high = x.astype(BF16)
    rest = x - high.astype(F32)
    mid = rest.astype(BF16)
    low = (rest - mid.astype(F32)).astype(BF16)
    return high, mid, low


def joined(rows, at):
    part = rows.astype(F32)
    return part[at : at + 1] + part[at + 1 : at + 2] + part[at + 2 : at + 3]


def column(row):
    return jnp.transpose(jnp.broadcast_to(row, (TOK, TOK)))


def split_dot(a, state):
    high = state.astype(BF16)
    low = (state - high.astype(F32)).astype(BF16)
    return dot(a, high) + dot(a, low)


def prepare_kernel(
    table_ref, index_ref, q_hbm, k_hbm, v_hbm, speed_ref, drop_ref, doc_ref, out_ref, q_ref, k_ref, v_ref, sems
):
    copies = [
        pltpu.make_async_copy(src, dst, sems.at[n])
        for n, (src, dst) in enumerate(((k_hbm, k_ref), (v_hbm, v_ref), (q_hbm, q_ref)))
    ]
    for copy in copies:
        copy.start()
    head = lax.broadcasted_iota(jnp.int32, (HEADS, TOK), 0)
    rate = jnp.zeros((HEADS, TOK), F32)
    for h in range(HEADS):
        rate = jnp.where(head == h, table_ref[index_ref[h]], rate)
    log_decay = -rate * speed_ref[...] - drop_ref[...]
    upto = (
        lax.broadcasted_iota(jnp.int32, (TOK, TOK), 0)
        <= lax.broadcasted_iota(jnp.int32, (TOK, TOK), 1)
    ).astype(F32)
    cum = jnp.dot(log_decay, upto, precision=lax.Precision.HIGHEST, preferred_element_type=F32)
    parts = [part.astype(F32) for part in split3(cum)]
    row = lax.broadcasted_iota(jnp.int32, (META, TOK), 0)
    doc = jnp.broadcast_to(doc_ref[...].astype(F32), (META, TOK))
    bias = jnp.where(doc == (row - 4).astype(F32), 0.0, LOW)
    shared = jnp.where(row == 3, doc, jnp.where((row >= 4) & (row < 8), bias, 0.0))
    for h in range(HEADS):
        meta = shared
        for n, part in enumerate(parts):
            meta = jnp.where(row == n, jnp.broadcast_to(part[h : h + 1], (META, TOK)), meta)
        out_ref[h, META_AT:VALUE_AT, :] = meta.astype(BF16)
    copies[0].wait()
    for h in range(HEADS):
        out_ref[h, 0:DH, :] = jnp.transpose(k_ref[:, pl.ds(h * DH, DH)])
    copies[1].wait()
    copies[2].wait()
    for h in range(HEADS):
        cols = pl.ds(h * DH, DH)
        out_ref[h, VALUE_AT:KV_ROWS, :] = v_ref[:, cols]
        out_ref[h, KV_ROWS:ROWS, :] = q_ref[:, cols]


def meta_rows(ref, i):
    return ref[i, META_AT:VALUE_AT, :].astype(F32)


def linear_kernel(info_ref, own_ref, low_ref, high_ref, init_ref, partial_ref, weight_ref, state_ref, mark_ref):
    x, core = info_ref[0], info_ref[2]
    first = core == 0
    state = jnp.where(x == 0, init_ref[0], 0.0)
    carry = jnp.where(x == 0, jnp.zeros((1, TOK), F32), jnp.full((1, TOK), -1.0, F32))
    prefix = jnp.zeros((1, TOK), F32)
    places = lax.broadcasted_iota(jnp.int32, (TOK, TOK), 0)
    lanes = lax.broadcasted_iota(jnp.int32, (TOK, TOK), 1)
    causal = places >= lanes
    marked = (lanes >= 4) & (lanes < 8)
    number = (lanes - 4).astype(F32)
    start_doc = None

    def read(swap, i):
        mine, theirs = own_ref[i, 0:KV_ROWS, :], (low_ref, high_ref)[i // TILES][i % TILES]
        got = jnp.where(swap, theirs, mine)
        rows = got[META_AT:VALUE_AT].astype(F32)
        cum, doc = rows[0:1] + rows[1:2] + rows[2:3], rows[3:4]
        overall = jnp.broadcast_to(cum[:, TOK - 1 :], (1, TOK))
        last = jnp.broadcast_to(doc[:, TOK - 1 :], (1, TOK))
        return got[:DH], got[VALUE_AT:], cum, doc, overall, last

    def advance(state, carry, prefix, block):
        keys, values, cum, doc, overall, last = block
        factor = jnp.where(doc == last, jnp.exp(overall - cum), 0.0)
        scaled = (keys.astype(F32) * factor).astype(BF16)
        keep = jnp.where(last == carry, jnp.exp(overall), 0.0)
        return dot(scaled, values) + keep * state, last, prefix + overall

    for i in range(HEADS):
        even = read(jnp.logical_not(first), i)
        odd = read(first, i)
        if start_doc is None:
            start_doc = jnp.broadcast_to(even[3][:, :1], (1, TOK))
        middle = advance(state, carry, prefix, even)
        at_state = jnp.where(first, state, middle[0])
        at_carry = jnp.where(first, carry, middle[1])
        at_prefix = jnp.where(first, prefix, middle[2])
        keys, values, cum, doc, _, _ = [jnp.where(first, a, b) for a, b in zip(even, odd)]
        queries = own_ref[i, KV_ROWS:ROWS, :]
        cum_col, doc_col = column(cum), column(doc)
        inside = causal & (doc_col == doc)
        fading = jnp.exp(jnp.where(inside, cum_col - cum, 0.0))
        weights = jnp.where(inside, fading * dot(queries, keys) * SCALE, 0.0).astype(BF16)
        grown = jnp.exp(cum_col) * SCALE
        outside = jnp.where(doc_col == at_carry, grown * split_dot(queries, at_state), 0.0)
        partial_ref[i] = dot(weights, values) + outside
        weight_ref[i] = jnp.where(doc_col == start_doc, jnp.exp(cum_col + at_prefix) * SCALE, 0.0)
        mark_ref[i] = jnp.where(marked & (doc_col == number), 1.0, 0.0).astype(BF16)
        state, carry, prefix = advance(*middle, odd)
    state_ref[0:DH, :] = state
    row = lax.broadcasted_iota(jnp.int32, (8, TOK), 0)
    state_ref[DH : DH + 8, :] = jnp.where(row == 0, prefix, jnp.where(row == 1, carry, start_doc))


def enter_kernel(
    info_ref, own_ref, partial_ref, weight_ref, state_ref, near_ref, far_ref, linear_ref, square_ref, need_ref
):
    x = info_ref[0]
    near_decay, near_doc = near_ref[DH : DH + 1, :], near_ref[DH + 1 : DH + 2, :]
    far_doc, start_doc = far_ref[DH + 1 : DH + 2, :], state_ref[DH + 2 : DH + 3, :]
    keep = jnp.where((far_doc == near_doc) & (x >= 2), jnp.exp(near_decay), 0.0)
    state = near_ref[0:DH, :] + keep * far_ref[0:DH, :]
    state = jnp.where((start_doc == near_doc) & (x >= 1), state, 0.0)
    high = state.astype(BF16)
    low = (state - high.astype(F32)).astype(BF16)
    queries = jnp.concatenate([own_ref[i, KV_ROWS:ROWS, :] for i in range(HEADS)], axis=0)
    product = dot(queries, jnp.concatenate([high, low], axis=1))
    product = product[:, :DH] + product[:, DH:]
    eye = lax.broadcasted_iota(jnp.int32, (TOK, DH), 0) == lax.broadcasted_iota(jnp.int32, (TOK, DH), 1)
    for i in range(HEADS):
        linear = partial_ref[i] + weight_ref[i] * product[i * TOK : (i + 1) * TOK]
        linear_ref[i] = linear.astype(BF16)
        square = jnp.sum(linear * linear, axis=1, keepdims=True)
        square_ref[i : i + 1, :] = jnp.sum(jnp.where(eye, square, 0.0), axis=0, keepdims=True)
    for tile in range(TILES):
        tile_doc = jnp.broadcast_to(meta_rows(own_ref, 2 * tile)[3:4, :1], (1, TOK))
        need_ref[2 * tile] = jnp.where(x >= 1, jnp.max(jnp.where(tile_doc == near_doc, 1, 0)), 0)
        need_ref[2 * tile + 1] = jnp.where(x >= 2, jnp.max(jnp.where(tile_doc == far_doc, 1, 0)), 0)


def marked_queries(own_ref, mark_ref, tile):
    i = 2 * tile
    queries = jnp.concatenate([own_ref[i, KV_ROWS:ROWS, :], own_ref[i + 1, KV_ROWS:ROWS, :]], axis=0)
    marks = jnp.concatenate([mark_ref[i], mark_ref[i + 1]], axis=0)[:, :META]
    return jnp.concatenate([queries, marks], axis=1)


def absorb(queries, pieces, old):
    scores = []
    top = None
    for ref, m, mask in pieces:
        keys = jnp.concatenate([ref[2 * m, 0:VALUE_AT, :], ref[2 * m + 1, 0:VALUE_AT, :]], axis=1)
        score = dot(queries, keys)
        if mask is not None:
            score = jnp.where(mask, score, LOW)
        scores.append(score)
        most = jnp.maximum(score[:, :TOK], score[:, TOK:])
        top = most if top is None else jnp.maximum(top, most)
    top = jnp.max(top, axis=1, keepdims=True)
    if old is not None:
        top = jnp.maximum(top, old[0])
    base = top * EXP2_SCALE
    sums, output = None, None
    for (ref, m, _), score in zip(pieces, scores):
        weights = jnp.exp2(score * EXP2_SCALE - base)
        part = weights[:, :TOK] + weights[:, TOK:]
        sums = part if sums is None else sums + part
        values = jnp.concatenate([ref[2 * m, VALUE_AT:KV_ROWS, :], ref[2 * m + 1, VALUE_AT:KV_ROWS, :]], axis=0)
        product = dot(weights.astype(BF16), values)
        output = product if output is None else output + product
    total = jnp.sum(sums, axis=1, keepdims=True)
    if old is not None:
        shrink = jnp.exp2(old[0] * EXP2_SCALE - base)
        total = total + old[1] * shrink
        output = output + old[2] * shrink
    return top, total, output


def tile_places(core, own):
    rows = lax.broadcasted_iota(jnp.int32, (CHUNK, CHUNK), 0)
    lanes = lax.broadcasted_iota(jnp.int32, (CHUNK, CHUNK), 1)
    key_core = core if own else 1 - core
    at = jnp.where(rows < TOK, rows, rows + TOK) + core * TOK
    key = jnp.where(lanes < TOK, lanes, lanes + TOK) + key_core * TOK
    return at, key


def span_of(tile):
    return pl.ds(tile * CHUNK, CHUNK)


def load_part(refs, tile):
    top_ref, total_ref, output_ref = refs
    span = span_of(tile)
    return top_ref[span, :1], total_ref[span, :1], output_ref[span, :]


def store_part(refs, tile, part):
    span = span_of(tile)
    for ref, value in zip(refs, part):
        ref[span, :] = jnp.broadcast_to(value, (CHUNK, TOK))


def own_window_kernel(info_ref, own_ref, low_ref, high_ref, mark_ref, *refs):
    core = info_ref[2]
    masks = []
    for own in (True, False):
        at, key = tile_places(core, own)
        masks.append(key <= at)
    for tile in range(TILES):
        queries = marked_queries(own_ref, mark_ref, tile)
        pieces = [(own_ref, m, masks[0] if m == tile else None) for m in range(tile + 1)]
        pieces += [
            ((low_ref, high_ref)[m // 2], m % 2, masks[1] if m == tile else None) for m in range(tile + 1)
        ]
        store_part(refs, tile, absorb(queries, pieces, None))


def near_kernel(need_ref, own_ref, mark_ref, near_ref, other_ref, more_ref, a_ref, b_ref, c_ref, *refs):
    olds = (a_ref, b_ref, c_ref)
    for tile in range(TILES):
        needed = need_ref[2 * tile] == 1

        @pl.when(needed)
        def _(tile=tile):
            queries = marked_queries(own_ref, mark_ref, tile)
            pieces = [(near_ref, m, None) for m in range(TILES)]
            pieces += [(ref, m, None) for ref in (other_ref, more_ref) for m in range(TILES // 2)]
            store_part(refs, tile, absorb(queries, pieces, load_part(olds, tile)))

        @pl.when(jnp.logical_not(needed))
        def _(tile=tile):
            store_part(refs, tile, load_part(olds, tile))


def far_blocks(core, own, own_ref, mark_ref, need_ref, far_ref, olds, refs):
    at, key = tile_places(core, own)
    mask = key > at
    for tile in range(TILES):
        needed = need_ref[2 * tile + 1] == 1

        @pl.when(needed)
        def _(tile=tile):
            queries = marked_queries(own_ref, mark_ref, tile)
            pieces = [(far_ref, m, mask if m == tile else None) for m in range(tile, TILES)]
            store_part(refs, tile, absorb(queries, pieces, load_part(olds, tile)))

        @pl.when(jnp.logical_not(needed))
        def _(tile=tile):
            store_part(refs, tile, load_part(olds, tile))


def far_own_kernel(info_ref, need_ref, own_ref, mark_ref, far_ref, a_ref, b_ref, c_ref, *refs):
    far_blocks(info_ref[2], True, own_ref, mark_ref, need_ref, far_ref, (a_ref, b_ref, c_ref), refs)


def far_other_kernel(
    info_ref, need_ref, own_ref, mark_ref, far_ref, a_ref, b_ref, c_ref, linear_ref, square_ref, out_ref, *refs
):
    row = lax.broadcasted_iota(jnp.int32, (META, TOK), 0)
    for i in range(HEADS):
        out_ref[i, TOK : 2 * TOK, :] = linear_ref[i]
        meta = jnp.zeros((META, TOK), F32)
        for n, part in enumerate(split3(square_ref[i : i + 1, :])):
            meta = jnp.where(row == n, jnp.broadcast_to(part.astype(F32), (META, TOK)), meta)
        out_ref[i, 2 * TOK :, :] = meta.astype(BF16)
    far_blocks(info_ref[2], False, own_ref, mark_ref, need_ref, far_ref, (a_ref, b_ref, c_ref), refs)
    _, total_ref, output_ref = refs
    for i in range(HEADS):
        span = pl.ds(i * TOK, TOK)
        out_ref[i, 0:TOK, :] = (output_ref[span, :] / total_ref[span, :]).astype(BF16)


def finish_kernel(got_ref, gain_ref, out_ref):
    total = jnp.zeros((1, TOK), F32)
    for h in range(HEADS):
        total = total + joined(got_ref[h, 2 * TOK :, :], 0)
    inverse = column(lax.rsqrt(total / (HEAD_TOTAL * DH) + 1e-06))
    for h in range(HEADS):
        cols = pl.ds(h * DH, DH)
        linear = got_ref[h, TOK : 2 * TOK, :].astype(F32)
        window = got_ref[h, 0:TOK, :].astype(F32)
        out_ref[:, cols] = (gain_ref[:, cols] * linear * inverse + window).astype(BF16)


VMEM = pl.BlockSpec(memory_space=pltpu.VMEM)
SMEM = pl.BlockSpec(memory_space=pltpu.SMEM)
HBM = pl.BlockSpec(memory_space=pltpu.HBM)


LIMIT = {"prepare": 58}


def call(kernel, name, specs, shapes, scratch=(), outs=None):
    many = isinstance(shapes, (list, tuple))
    return pl.pallas_call(
        kernel,
        name=name,
        out_shape=shapes,
        in_specs=specs,
        out_specs=outs or ([VMEM] * len(shapes) if many else VMEM),
        scratch_shapes=list(scratch),
        compiler_params=pltpu.CompilerParams(vmem_limit_bytes=LIMIT.get(name, 16) * 2**20),
        cost_estimate=pl.CostEstimate(flops=0, bytes_accessed=0, transcendentals=0),
    )


def body(queries, keys, values, init_state, lin_gain, rate_table, rate_index, speed, drop, doc_id):
    x, z, core = (lax.axis_index(a).astype(jnp.int32) for a in ("x", "z", "core"))
    info = jnp.stack([x, z, core])
    shape = jax.ShapeDtypeStruct
    packed = call(
        prepare_kernel,
        "prepare",
        [SMEM, SMEM, HBM, HBM, HBM, VMEM, VMEM, VMEM],
        shape((HEADS, ROWS, TOK), BF16),
        scratch=[pltpu.VMEM((TOK, HEADS * DH), BF16)] * 3 + [pltpu.SemaphoreType.DMA((3,))],
    )(rate_table, rate_index, queries, keys, values, speed.T, drop.T, doc_id[None, :])
    own = lax.all_to_all(packed, "z", 0, 0, tiled=True)
    sent = own[:, :KV_ROWS]
    pair = [(0, 1), (1, 0)]
    near = lax.ppermute(sent, "x", [(0, 1), (1, 2), (2, 3)])
    other = [
        lax.ppermute(own[:TILES, :KV_ROWS], "core", pair),
        lax.ppermute(lax.optimization_barrier(own)[TILES:, :KV_ROWS], "core", pair),
    ]

    tokens = HEADS * TOK
    part_shapes = [shape((tokens, TOK), F32), shape((tokens, TOK), F32), shape((tokens, DH), F32)]
    init = lax.dynamic_slice_in_dim(init_state, z, 1, 0)
    partial, weight, state, mark = call(
        linear_kernel,
        "linear",
        [SMEM] + [VMEM] * 4,
        [
            shape((HEADS, TOK, DH), F32),
            shape((HEADS, TOK, DH), F32),
            shape((DH + 8, DH), F32),
            shape((HEADS, TOK, TOK), BF16),
        ],
    )(info, own, *other, init)
    near_state = lax.ppermute(state, "x", [(0, 1), (1, 2), (2, 3)])
    far_state = lax.ppermute(state, "x", [(0, 2), (1, 3)])
    own_part = call(
        own_window_kernel, "own_window", [SMEM] + [VMEM] * 4, part_shapes
    )(info, own, *other, mark)
    sent, partial = lax.optimization_barrier((sent, partial))
    far = lax.ppermute(sent, "x", [(0, 2), (1, 3)])
    near_state, far_state, own_part = lax.optimization_barrier((near_state, far_state, own_part))
    linear, square, need = call(
        enter_kernel,
        "enter",
        [SMEM] + [VMEM] * 6,
        [shape((HEADS, TOK, DH), BF16), shape((HEADS, TOK), F32), shape((2 * TILES,), jnp.int32)],
        outs=[VMEM, VMEM, SMEM],
    )(info, own, partial, weight, state, near_state, far_state)
    near, own_part = lax.optimization_barrier((near, own_part))
    near_other = [lax.ppermute(near[at : at + TILES], "core", pair) for at in (0, TILES)]
    squares = [lax.ppermute(square, "head", [(i, i ^ step) for i in range(4)]) for step in (1, 2, 3)]
    part = call(near_kernel, "near_window", [SMEM] + [VMEM] * 8, part_shapes)(
        need, own, mark, near, *near_other, *own_part
    )
    far, part, squares = lax.optimization_barrier((far, part, squares))
    square = square + squares[0] + (squares[1] + squares[2])
    far_other = lax.ppermute(far, "core", pair)
    part = call(far_own_kernel, "far_own", [SMEM] * 2 + [VMEM] * 6, part_shapes)(info, need, own, mark, far, *part)
    mixed = call(
        far_other_kernel,
        "far_other",
        [SMEM] * 2 + [VMEM] * 8,
        shape((HEADS, 2 * TOK + META, DH), BF16),
        scratch=[pltpu.VMEM((tokens, TOK), F32)] * 3,
    )(info, need, own, mark, far_other, *part, linear, square)
    back = lax.all_to_all(mixed, "z", 0, 0, tiled=True)
    return call(finish_kernel, "finish", [VMEM] * 2, shape((TOK, HEADS * DH), BF16))(
        back, lin_gain[None, :]
    )


def solution(mesh):
    split = Mesh(mesh.devices.reshape(4, 8, 2, 4), ("x", "z", "core", "head"))
    ctx = ("x", "z", "core")
    placed = (
        P(ctx, "head"),
        P(ctx, "head"),
        P(ctx, "head"),
        P("head", None, None),
        P("head"),
        P(),
        P("head"),
        P(ctx, "head"),
        P(ctx, "head"),
        P(ctx),
    )
    return jax.shard_map(body, mesh=split, in_specs=placed, out_specs=P(ctx, "head"), check_vma=False)
```
